512 devices in a mesh: row: 16 (over y_lo, x, core), col: 32 (over y_hi, z).
Axes of the slice: x: 4, y: 8 (y_hi: 4, y_lo: 2; y = y_hi * 2 + y_lo), z: 8, core: 2. Of those that a mesh axis runs over, the one named last changes fastest.
Arguments:
- obj: float32 [2, 2048, 4096], P(None, 'row', 'col'), may hold values from -5 to 5
- probe: float32 [2, 2, 128, 128], replicated, may hold values from -5 to 5
- measured: float32 [16, 32, 2, 8, 128, 128], P('row', 'col'), may hold values from 0.05 to 4
- offsets: int32 [16, 32, 2, 8, 2], P('row', 'col'), may hold values from -64 to 64, as said below
Outputs:
- new_obj: float32 [2, 2048, 4096], P(None, 'row', 'col')
- new_probe: float32 [2, 2, 128, 128], replicated
- probe_gradient: float32 [2, 2, 128, 128], replicated
The draws below stay inside these ranges and needn't reach their ends.
Inputs may be any that keep to these rules, and one draw needn't show every extreme that they name: `offsets`: window starts are relative to the device's own tile of 128 pixels, so a window may reach up to 64 pixels into neighbouring tiles; both extremes occur in every draw.
All inputs are finite; a program needn't handle non-finite values.
Results may differ from the reference program's by a relative error of at most 0.0003.
Values sent between devices are 32-bit elements; how exact they have to be, the bound alone decides.
No kernel may reach another device: no remote copies, remote signals or barrier semaphores. Data moves between devices by JAX's collectives and lax.ppermute only.
A program may use at most 64 MiB of HBM per device.

```python
import math
import jax
import jax.numpy as jnp
from jax import lax

PROBE_EXTENT = 128
MODES = 2
TILE = 128
SCAN_PER_DEVICE = 8
BATCHES = 2
HALF = 64
OBJ_ROWS = 2048
OBJ_COLS = 4096
N_ROW = 16
N_COL = 32


def draw_offsets(key, part):
    key = jax.random.fold_in(key, 11)
    lowest = -(PROBE_EXTENT // 2)
    highest = TILE - PROBE_EXTENT // 2
    values = jax.random.randint(key, (N_ROW, N_COL, BATCHES, SCAN_PER_DEVICE, 2), lowest, highest + 1, dtype=jnp.int32)
    values = values.at[0, 0, 0, 0].set(lowest)
    values = values.at[0, 0, 0, 1].set(highest)
    return values


def level_of(rng, extent, split, smallest, high):
    gain = 1.0
    for position, shards_of in split:
        heights = jax.random.uniform(jax.random.fold_in(jax.random.fold_in(rng, 6), position), (shards_of,), jnp.float32, smallest / len(split), high / len(split))
        gain = gain * jnp.repeat(jnp.exp(heights), extent[position] // shards_of).reshape((-1,) + (1,) * (len(extent) - 1 - position))
    return gain


def gaussian(own_key, shape, scale, limit, shards=(), kind=jnp.bfloat16):
    values = scale * jax.random.normal(own_key, shape, jnp.float32)
    if shards:
        values = values * level_of(own_key, shape, shards, -0.22, 0.18)
    return jnp.clip(values, -limit, limit).astype(kind)


def setup_inputs(seed: int = 0) -> dict:
    seeds = jax.random.split(jax.random.key(seed), 5)
    obj = gaussian(seeds[0], (2, OBJ_ROWS, OBJ_COLS), 0.7, 5.0, ((1, 16), (2, 32)), jnp.float32)
    probe = gaussian(seeds[1], (2, MODES, PROBE_EXTENT, PROBE_EXTENT), 0.7, 5.0, (), jnp.float32)
    measured = jnp.clip(jnp.exp(math.log(4.0) - 4.3820266 * jax.random.uniform(seeds[2], (N_ROW, N_COL, BATCHES, SCAN_PER_DEVICE, PROBE_EXTENT, PROBE_EXTENT), jnp.float32) ** level_of(seeds[2], (N_ROW, N_COL, BATCHES, SCAN_PER_DEVICE, PROBE_EXTENT, PROBE_EXTENT), ((0, 16), (1, 32)), -0.2, 0.2)), 0.05, 4.0)
    offsets = draw_offsets(jax.random.fold_in(seeds[4], 71), 0)
    return dict(obj=obj, probe=probe, measured=measured, offsets=offsets)


def exit_residual(probe_complex, object_window, recorded_pattern):
    psi = probe_complex[None] * object_window[:, None]
    wave = jnp.fft.fft2(psi, norm='ortho')
    model_intensity = lax.optimization_barrier(jnp.sum(wave.real * wave.real + wave.imag * wave.imag, axis=1))
    amplitude_ratio = jnp.sqrt(recorded_pattern) / jnp.maximum(jnp.sqrt(model_intensity), 0.5) - 1.0
    return jnp.fft.ifft2(wave * amplitude_ratio[:, None], norm='ortho')

def take_windows(field, row_indices, column_indices):
    return jax.vmap(lambda a, b: lax.dynamic_slice(field, (a, b), (PROBE_EXTENT, PROBE_EXTENT)))(row_indices, column_indices)

def reference(obj, probe, measured, offsets):
    obj_c = obj[0] + 1j * obj[1]
    probe_complex = probe[0] + 1j * probe[1]
    tile_r = jnp.arange(N_ROW, dtype=jnp.int32) * TILE
    tile_c = jnp.arange(N_COL, dtype=jnp.int32) * TILE
    gradient = None
    for scan_batch in range(BATCHES):
        row_indices = (tile_r[:, None, None] + offsets[:, :, scan_batch, :, 0] + HALF).reshape(-1, SCAN_PER_DEVICE).astype(jnp.int32)
        column_indices = (tile_c[None, :, None] + offsets[:, :, scan_batch, :, 1] + HALF).reshape(-1, SCAN_PER_DEVICE).astype(jnp.int32)
        recorded_pattern = measured[:, :, scan_batch].reshape(-1, SCAN_PER_DEVICE, PROBE_EXTENT, PROBE_EXTENT)
        padded = jnp.pad(obj_c, HALF)
        light = lax.optimization_barrier(jnp.sum(probe_complex.real ** 2 + probe_complex.imag ** 2, axis=0))

        def leading_batch(carry, item):
            running_accumulator, probe_numer_sum, probe_denominator = carry
            r, c, m = item
            object_window = take_windows(padded, r, c)
            chi = exit_residual(probe_complex, object_window, m)
            contrib = lax.optimization_barrier(jnp.sum(jnp.conj(probe_complex)[None] * chi, axis=1))

            def place(k, total):
                block = jnp.stack([contrib[k].real, contrib[k].imag, light])
                zero = jnp.zeros((), jnp.int32)
                cur = lax.dynamic_slice(total, (zero, r[k], c[k]), (3, PROBE_EXTENT, PROBE_EXTENT))
                return lax.dynamic_update_slice(total, cur + block, (zero, r[k], c[k]))
            running_accumulator = lax.fori_loop(0, SCAN_PER_DEVICE, place, running_accumulator)
            probe_numer_sum = probe_numer_sum + lax.optimization_barrier(jnp.sum(jnp.conj(object_window)[:, None] * chi, axis=0))
            probe_denominator = probe_denominator + lax.optimization_barrier(jnp.sum(object_window.real ** 2 + object_window.imag ** 2, axis=0))
            return ((running_accumulator, probe_numer_sum, probe_denominator), None)
        initial_accumulator = jnp.zeros((3, OBJ_ROWS + 2 * HALF, OBJ_COLS + 2 * HALF), jnp.float32)
        initial_probe_numer_sum = jnp.zeros((MODES, PROBE_EXTENT, PROBE_EXTENT), probe_complex.dtype)
        initial_probe_denominator = jnp.zeros((PROBE_EXTENT, PROBE_EXTENT), jnp.float32)
        (running_accumulator, probe_numer_sum, probe_denominator), unused_slot = lax.scan(leading_batch, (initial_accumulator, initial_probe_numer_sum, initial_probe_denominator), (row_indices, column_indices, recorded_pattern))
        inner = running_accumulator[:, HALF:HALF + OBJ_ROWS, HALF:HALF + OBJ_COLS]
        d_obj = (inner[0] + 1j * inner[1]) / (inner[2] + 1.0)
        d_probe = probe_numer_sum / (probe_denominator + 1.0)
        gradient = probe_numer_sum / jnp.sqrt(probe_denominator + 1.0)
        dpad = jnp.pad(d_obj, HALF)

        def trailing_batch(carry, item):
            r, c, m = item
            object_window = take_windows(padded, r, c)
            dpatch = take_windows(dpad, r, c)
            chi = exit_residual(probe_complex, object_window, m)
            u1 = probe_complex[None] * dpatch[:, None]
            u2 = d_probe[None] * object_window[:, None]
            terms = jnp.stack([jnp.sum(u1.real ** 2 + u1.imag ** 2), jnp.sum(u2.real ** 2 + u2.imag ** 2), jnp.sum(u1.real * u2.real + u1.imag * u2.imag), jnp.sum(u1.real * chi.real + u1.imag * chi.imag), jnp.sum(u2.real * chi.real + u2.imag * chi.imag)])
            return (carry + terms, None)
        batch_sums, unused_slot = lax.scan(trailing_batch, jnp.zeros((5,), jnp.float32), (row_indices, column_indices, recorded_pattern))
        a11 = 1.1 * batch_sums[0]
        a22 = 1.1 * batch_sums[1]
        a12 = batch_sums[2]
        det = a11 * a22 - a12 * a12
        step_obj = (batch_sums[3] * a22 - a12 * batch_sums[4]) / det
        step_probe = (a11 * batch_sums[4] - a12 * batch_sums[3]) / det
        obj_c = obj_c + step_obj * d_obj
        probe_complex = probe_complex + step_probe * d_probe
    new_obj = jnp.stack([obj_c.real, obj_c.imag]).astype(jnp.float32)
    new_probe = jnp.stack([probe_complex.real, probe_complex.imag]).astype(jnp.float32)
    probe_gradient = jnp.stack([gradient.real, gradient.imag]).astype(jnp.float32)
    return (new_obj, new_probe, probe_gradient)
```

```python
import math

import jax
import jax.numpy as jnp
import numpy as np
from jax import lax
from jax.experimental import pallas as pl
from jax.experimental.pallas import tpu as pltpu
from jax.sharding import Mesh, PartitionSpec as P

SIZE = 128
HALF = 64
MODES = 2
COUNT = 8
GROUP = 2
ROW = ("yl", "x", "c")
COL = ("yh", "z")
ALL = ROW + COL
TILES = 8
VMEM_LIMIT = 48 * 1024 * 1024
F32 = jnp.float32
BF16 = jnp.bfloat16


def dft_tables():
    index = np.arange(SIZE)
    angle = 2.0 * math.pi / SIZE * (np.outer(index, index) % SIZE)
    real = np.cos(angle) / math.sqrt(SIZE)
    imag = -np.sin(angle) / math.sqrt(SIZE)
    right = np.block([[real, imag], [-imag, real]]).astype(np.float32)
    high = right.astype(jnp.bfloat16)
    low = (right - high.astype(np.float32)).astype(jnp.bfloat16)
    right3 = np.concatenate([high, high, low], axis=0)
    left3 = np.ascontiguousarray(right3.T)
    return right3, left3


def halves(x):
    high = x.astype(BF16)
    return high, (x - high.astype(F32)).astype(BF16)


def right_transform(fields, table):
    rows = []
    for real, imag in fields:
        rh, rl = halves(real)
        ih, il = halves(imag)
        rows.append(jnp.concatenate([rh, ih, rl, il, rh, ih], axis=1))
    out = jnp.dot(jnp.concatenate(rows, axis=0), table, preferred_element_type=F32)
    return [
        (out[SIZE * n : SIZE * (n + 1), :SIZE], out[SIZE * n : SIZE * (n + 1), SIZE:])
        for n in range(len(fields))
    ]


def left_transform(fields, table):
    cols = []
    for real, imag in fields:
        rh, rl = halves(real)
        ih, il = halves(imag)
        cols.append(jnp.concatenate([rh, ih, rl, il, rh, ih], axis=0))
    out = jnp.dot(table, jnp.concatenate(cols, axis=1), preferred_element_type=F32)
    return [
        (out[:SIZE, SIZE * n : SIZE * (n + 1)], out[SIZE:, SIZE * n : SIZE * (n + 1)])
        for n in range(len(fields))
    ]


def lanes():
    return lax.broadcasted_iota(jnp.int32, (SIZE, SIZE), 1)


def window(ref, lead, row, col):
    shift = lax.rem(SIZE - col, SIZE)
    first = pltpu.roll(ref[lead + (0, pl.ds(row, SIZE))], shift, 1)
    second = pltpu.roll(ref[lead + (1, pl.ds(row, SIZE))], shift, 1)
    return jnp.where(lanes() < SIZE - col, first, second)


def place(ref, plane, row, col, block):
    moved = pltpu.roll(block, lax.rem(col, SIZE), 1)
    first = lanes() >= col
    rows = pl.ds(row, SIZE)
    ref[plane, 0, rows] += jnp.where(first, moved, 0.0)
    ref[plane, 1, rows] += jnp.where(first, 0.0, moved)


def join(low, first, second):
    return jnp.where(low, pltpu.roll(first, HALF, 1), pltpu.roll(second, HALF, 1))


def pack_low(low, upper, lower):
    return jnp.where(low, upper, pltpu.roll(lower, HALF, 1))


def pack_high(low, upper, lower):
    return jnp.where(low, pltpu.roll(upper, HALF, 1), lower)


def low_lanes(rows):
    return lax.broadcasted_iota(jnp.int32, (rows, SIZE), 1) < HALF


def pad_field(above, own, below, from_left, from_right, store):
    low = low_lanes(HALF)
    for c in range(2):
        strips = (above[c], own[c, :HALF], own[c, HALF:], below[c])
        for k in range(4):
            half = slice(HALF * (k % 2), HALF * (k % 2 + 1))
            left, right = from_left[c, half], from_right[c, half]
            if k < 2:
                right = pltpu.roll(right, HALF, 1)
            else:
                left = pltpu.roll(left, HALF, 1)
            mine = pltpu.roll(strips[k], HALF, 1)
            rows = slice(HALF * k, HALF * (k + 1))
            store(c, 0, rows, jnp.where(low, left, mine))
            store(c, 1, rows, jnp.where(low, mine, right))


def pack_kernel(above, own, below, left, right):
    low = low_lanes(HALF)
    for c in range(2):
        strips = (above[c], own[c, :HALF], own[c, HALF:], below[c])
        for k in range(2):
            rows = slice(HALF * k, HALF * (k + 1))
            left[c, rows] = pack_low(low, strips[k], strips[k + 2])
            right[c, rows] = pack_high(low, strips[k], strips[k + 2])


def sweep(batch, starts, padded, probe, measured, right3, left3, top, middle, bottom, sums, accum):
    accum[...] = jnp.zeros_like(accum)
    sums[...] = jnp.zeros_like(sums)
    light = sum(probe[c, m] * probe[c, m] for c in range(2) for m in range(MODES))
    tr = right3[...]
    tl = left3[...]

    def body(step, carry):
        wins = []
        fields = []
        for g in range(GROUP):
            j = step * GROUP + g
            row, col = starts[j, 0], starts[j, 1]
            wr = window(padded, (0,), row, col)
            wi = window(padded, (1,), row, col)
            wins.append((row, col, wr, wi))
            for m in range(MODES):
                pr, pi = probe[0, m], probe[1, m]
                fields.append((pr * wr - pi * wi, pr * wi + pi * wr))
        waves = left_transform(right_transform(fields, tr), tl)
        back = []
        for g in range(GROUP):
            own = waves[g * MODES : (g + 1) * MODES]
            intensity = sum(r * r + i * i for r, i in own)
            recorded = measured[0, 0, batch, step * GROUP + g]
            ratio = jnp.sqrt(recorded) / jnp.maximum(jnp.sqrt(intensity), 0.5) - 1.0
            back += [(r * ratio, -(i * ratio)) for r, i in own]
        chis = right_transform(left_transform(back, tl), tr)
        for g in range(GROUP):
            row, col, wr, wi = wins[g]
            cr = jnp.zeros((SIZE, SIZE), F32)
            ci = jnp.zeros((SIZE, SIZE), F32)
            for m in range(MODES):
                xr, xn = chis[g * MODES + m]
                pr, pi = probe[0, m], probe[1, m]
                cr += pr * xr - pi * xn
                ci -= pr * xn + pi * xr
                sums[m] += wr * xr - wi * xn
                sums[MODES + m] -= wr * xn + wi * xr
            sums[2 * MODES] += wr * wr + wi * wi
            place(accum, 0, row, col, cr)
            place(accum, 1, row, col, ci)
            place(accum, 2, row, col, light)
        return carry

    lax.fori_loop(0, COUNT // GROUP, body, 0)
    top[...] = accum[:, :, :HALF]
    middle[...] = accum[:, :, HALF : HALF + SIZE]
    bottom[...] = accum[:, :, HALF + SIZE :]


def first_kernel(starts, above, own, below, from_left, from_right, probe, measured, right3, left3,
                 top, middle, bottom, sums, padded, accum):
    def store(c, h, rows, value):
        padded[c, h, rows] = value

    pad_field(above, own, below, from_left, from_right, store)
    sweep(0, starts, padded, probe, measured, right3, left3, top, middle, bottom, sums, accum)


def fold_kernel(middle, from_above, from_below, tile, left, right):
    low = low_lanes(HALF)
    for k in range(3):
        upper = [middle[k, h, :HALF] + from_above[k, h] for h in range(2)]
        lower = [middle[k, h, HALF:] + from_below[k, h] for h in range(2)]
        tile[k, :HALF] = join(low, *upper)
        tile[k, HALF:] = join(low, *lower)
        left[k] = pack_low(low, upper[0], lower[0])
        right[k] = pack_high(low, upper[1], lower[1])


def merge_kernel(shifts, tile, from_left, from_right, padded, sums,
                 packed, numbers, direction, product, overlap):
    low = low_lanes(HALF)
    lane = lanes()
    a11 = jnp.zeros((1, SIZE), F32)
    b1 = jnp.zeros((1, SIZE), F32)
    product[...] = jnp.zeros_like(product)
    for v in range(2):
        rows = slice(HALF * v, HALF * (v + 1))
        full = []
        for k in range(3):
            left, right = from_left[k], from_right[k]
            if v == 0:
                right = pltpu.roll(right, HALF, 1)
            else:
                left = pltpu.roll(left, HALF, 1)
            full.append(tile[k, rows] + jnp.where(low, left, right))
        gr, gi, cover = full
        inverse = 1.0 / (cover + 1.0)
        dr = gr * inverse
        di = gi * inverse
        direction[0, rows] = dr
        direction[1, rows] = di
        span = slice(HALF * (v + 1), HALF * (v + 2))
        pr = join(low, padded[0, 0, span], padded[0, 1, span])
        pi = join(low, padded[1, 0, span], padded[1, 1, span])
        inner = slice(SIZE + HALF * v, SIZE + HALF * (v + 1))
        product[0, inner] = dr * pr + di * pi
        product[1, inner] = dr * pi - di * pr
        power = dr * dr + di * di
        a11 += jnp.sum(power * cover, axis=0, keepdims=True)
        b1 += jnp.sum(power * (cover + 1.0), axis=0, keepdims=True)
    line = lax.broadcasted_iota(jnp.int32, (TILES, SIZE), 0)
    numbers[...] = jnp.where(line == 0, a11, jnp.where(line == 1, b1, 0.0))

    overlap[...] = jnp.zeros_like(overlap)

    def body(k, carry):
        down, across = shifts[k, 0], shifts[k, 1]

        @pl.when((jnp.abs(down) < SIZE) & (jnp.abs(across) < SIZE))
        def _():
            turn = lax.rem(SIZE - across, SIZE)
            source = lane + across
            inside = (source >= 0) & (source < SIZE)
            for c in range(2):
                moved = pltpu.roll(product[c, pl.ds(SIZE + down, SIZE)], turn, 1)
                overlap[c] += jnp.where(inside, moved, 0.0)

        return carry

    lax.fori_loop(0, shifts.shape[0], body, 0)

    strips = (SIZE // TILES, TILES, SIZE)
    for k in range(5):
        packed[:, k] = sums[k].reshape(strips)
    for c in range(2):
        packed[:, 5 + c] = overlap[c].reshape(strips)


def add_all(parts):
    total = parts[0]
    for k in range(1, parts.shape[0]):
        total = total + parts[k]
    return total


def scatter_kernel(parts, numbers, out):
    total = add_all(parts)
    for k in range(out.shape[0]):
        out[k, :7] = total
        out[k, 7] = numbers[...]


def reduce_kernel(parts, out):
    total = add_all(parts)
    for k in range(out.shape[0]):
        out[k] = total


def strip_kernel(place_ref, parts, probe, out):
    total = add_all(parts)
    rows = pl.ds(pl.multiple_of(place_ref[0] * TILES, TILES), TILES)
    cover = total[2 * MODES]
    inverse = 1.0 / (cover + 1.0)
    cross = jnp.zeros((TILES, SIZE), F32)
    power = jnp.zeros((TILES, SIZE), F32)
    for m in range(MODES):
        dr, di = total[m] * inverse, total[MODES + m] * inverse
        pr, pi = probe[0, m, rows], probe[1, m, rows]
        cross += (pr * dr + pi * di) * total[5] - (pr * di - pi * dr) * total[6]
        power += dr * dr + di * di
    line = lax.broadcasted_iota(jnp.int32, (TILES, SIZE), 0)
    numbers = total[7]
    for k, term in ((2, power * cover), (3, power * (cover + 1.0)), (4, cross)):
        numbers = jnp.where(line == k, jnp.sum(term, axis=0, keepdims=True), numbers)
    for k in range(out.shape[0]):
        out[k, :5] = total[:5]
        out[k, 5] = numbers


def step_sizes(totals, probe, new_probe, gradient=None):
    numbers = jnp.sum(add_all(totals.at[:, 5]), axis=1, keepdims=True)
    a11, b1, a22, b2, a12 = (numbers[k : k + 1] for k in range(5))
    a11 = 1.1 * a11
    a22 = 1.1 * a22
    det = a11 * a22 - a12 * a12
    step_obj = (b1 * a22 - a12 * b2) / det
    step_probe = (a11 * b2 - a12 * b1) / det
    cover = totals[:, 4].reshape(SIZE, SIZE) + 1.0
    scale = step_probe / cover
    for m in range(MODES):
        for c in range(2):
            numer = totals[:, MODES * c + m].reshape(SIZE, SIZE)
            new_probe[c, m] = probe[c, m] + scale * numer
            if gradient is not None:
                gradient[c, m] = numer * lax.rsqrt(cover)
    return step_obj


def next_kernel(starts, totals, padded, above, direction, below, from_left, from_right, probe,
                measured, right3, left3,
                top, middle, bottom, sums, new_padded, new_probe, accum):
    step = step_sizes(totals, probe, new_probe)

    def store(c, h, rows, value):
        new_padded[c, h, rows] = padded[c, h, rows] + step * value

    pad_field(above, direction, below, from_left, from_right, store)
    sweep(1, starts, new_padded, new_probe, measured, right3, left3, top, middle, bottom, sums, accum)


def last_kernel(totals, padded, direction, probe, new_obj, new_probe, gradient):
    step = step_sizes(totals, probe, new_probe, gradient)
    low = lanes() < HALF
    rows = slice(HALF, HALF + SIZE)
    for c in range(2):
        old = join(low, padded[c, 0, rows], padded[c, 1, rows])
        new_obj[c] = old + step * direction[c]


def shape(*dims):
    return jax.ShapeDtypeStruct(dims, F32)


def call(kernel, ins, outs, scratch=()):
    vmem = pl.BlockSpec(memory_space=pltpu.VMEM)
    smem = pl.BlockSpec(memory_space=pltpu.SMEM)
    specs = [smem if x.dtype == jnp.int32 else vmem for x in ins]
    return pl.pallas_call(
        kernel,
        in_specs=specs,
        out_specs=[vmem] * len(outs),
        out_shape=list(outs),
        scratch_shapes=list(scratch),
        compiler_params=pltpu.CompilerParams(vmem_limit_bytes=VMEM_LIMIT),
        name=kernel.__name__,
    )(*ins)


def shift(block, rows, cols):
    n_row = math.prod(lax.axis_size(a) for a in ROW)
    n_col = math.prod(lax.axis_size(a) for a in COL)
    route = [
        (r * n_col + c, (r + rows) * n_col + c + cols)
        for r in range(n_row)
        for c in range(n_col)
        if 0 <= r + rows < n_row and 0 <= c + cols < n_col
    ]
    return lax.ppermute(block, ALL, route)


def exchange(block, axes):
    return lax.all_to_all(block, axes, 0, 0, tiled=True)


def size_of(axes):
    return math.prod(lax.axis_size(a) for a in axes)


def reduce_all(packed, numbers, probe, place_in_row, direction=None):
    halo = None
    if direction is not None:
        above = shift(direction[:, HALF:], 1, 0)
        below = shift(direction[:, :HALF], -1, 0)
    part = exchange(packed, ROW)
    if direction is not None:
        part, above, below = lax.optimization_barrier((part, above, below))
        left, right = call(pack_kernel, [above, direction, below], [shape(2, SIZE, SIZE)] * 2)
        from_left = shift(right, 0, 1)
        from_right = shift(left, 0, -1)
    (part,) = call(scatter_kernel, [part, numbers], [shape(size_of(("z",)), 8, TILES, SIZE)])
    part = exchange(part, ("z",))
    if direction is not None:
        part, from_left, from_right = lax.optimization_barrier((part, from_left, from_right))
        halo = above, direction, below, from_left, from_right
    (part,) = call(reduce_kernel, [part], [shape(size_of(("yh",)), 8, TILES, SIZE)])
    part = exchange(part, ("yh",))
    (part,) = call(strip_kernel, [place_in_row, part, probe], [shape(packed.shape[0], 6, TILES, SIZE)])
    return exchange(part, ROW), halo


MARK = 1024.0


def per_device(obj, probe, measured, offsets):
    right3, left3 = (jnp.asarray(t) for t in dft_tables())
    offsets = offsets[0, 0]
    starts = offsets + HALF
    batches = offsets.shape[0]
    place_in_row = lax.axis_index(ROW).astype(jnp.int32).reshape(1)

    code = jnp.zeros((TILES * SIZE,), F32).at[: offsets.size].set(
        offsets.reshape(-1).astype(F32) + MARK)
    code = code.reshape(1, TILES, SIZE)

    def with_code(strip, more):
        return jnp.concatenate([strip, jnp.pad(more, ((0, 1), (0, 0), (0, 0)))], axis=1)

    above = shift(with_code(obj[:, HALF:], code), 1, 0)
    below = shift(with_code(obj[:, :HALF], code), -1, 0)
    codes = jnp.concatenate([above[:1, HALF:], code, below[:1, HALF:]], axis=1)
    above, below = above[:, :HALF], below[:, :HALF]
    packed_field = shape(2, SIZE, SIZE)
    left, right = call(pack_kernel, [above, obj, below], [packed_field] * 2)
    from_left = shift(with_code(right, codes), 0, 1)
    from_right = shift(with_code(left, codes), 0, -1)
    codes = jnp.stack([from_left[0, SIZE:], codes[0], from_right[0, SIZE:]])
    codes = codes.reshape(3, 3, -1)[:, :, : offsets.size].reshape((3, 3) + offsets.shape)
    away = jnp.arange(-1, 2, dtype=jnp.int32) * SIZE
    steps = jnp.stack([
        jnp.broadcast_to(away[None, :, None, None], codes.shape[:-1]),
        jnp.broadcast_to(away[:, None, None, None], codes.shape[:-1]),
    ], axis=-1)
    shifts = (codes - MARK).astype(jnp.int32) + steps
    shifts = jnp.moveaxis(shifts, 2, 0).reshape(batches, -1, 2)

    whole = 2 * SIZE
    field = shape(2, 2, whole, SIZE)
    edge = shape(3, 2, HALF, SIZE)
    middle = shape(3, 2, SIZE, SIZE)
    planes = shape(2, MODES, SIZE, SIZE)
    accum = pltpu.VMEM((3, 2, whole, SIZE), F32)

    top, middle_in, bottom, sums, padded = call(
        first_kernel,
        [starts[0], above, obj, below, from_left[:, :SIZE], from_right[:, :SIZE], probe,
         measured, right3, left3],
        [edge, middle, edge, shape(5, SIZE, SIZE), field],
        [accum],
    )

    def merge(top, middle_in, bottom, sums, padded, batch):
        from_above = shift(bottom, 1, 0)
        from_below = shift(top, -1, 0)
        side = shape(3, HALF, SIZE)
        tile, left, right = call(
            fold_kernel, [middle_in, from_above, from_below], [shape(3, SIZE, SIZE), side, side])
        left_in = shift(right, 0, 1)
        right_in = shift(left, 0, -1)
        return call(
            merge_kernel,
            [shifts[batch], tile, left_in, right_in, padded, sums],
            [shape(SIZE // TILES, 7, TILES, SIZE), shape(TILES, SIZE), shape(2, SIZE, SIZE)],
            [pltpu.VMEM((2, 3 * SIZE, SIZE), F32), pltpu.VMEM((2, SIZE, SIZE), F32)],
        )

    packed, numbers, direction = merge(top, middle_in, bottom, sums, padded, 0)
    totals, halo = reduce_all(packed, numbers, probe, place_in_row, direction)
    top, middle_in, bottom, sums, padded, probe = call(
        next_kernel,
        [starts[1], totals, padded, *halo, probe, measured, right3, left3],
        [edge, middle, edge, shape(5, SIZE, SIZE), field, planes],
        [accum],
    )
    packed, numbers, direction = merge(top, middle_in, bottom, sums, padded, 1)
    totals, _ = reduce_all(packed, numbers, probe, place_in_row)
    return tuple(call(
        last_kernel, [totals, padded, direction, probe], [shape(2, SIZE, SIZE), planes, planes]
    ))


def solution(mesh):
    parts = Mesh(mesh.devices.reshape(2, 4, 2, 4, 8), ALL)
    in_specs = (P(None, ROW, COL), P(), P(ROW, COL), P(ROW, COL))
    out_specs = (P(None, ROW, COL), P(), P())
    return jax.shard_map(
        per_device, mesh=parts, in_specs=in_specs, out_specs=out_specs, check_vma=False
    )
```

```python
import math
from functools import partial

import jax
import jax.numpy as jnp
import numpy as np
from jax import lax
from jax.experimental import pallas as pl
from jax.experimental.pallas import tpu as pltpu
from jax.sharding import Mesh, PartitionSpec as P

SIZE = 128
HALF = 64
MODES = 2
COUNT = 8
GROUP = 2
ROW = ("yl", "x", "c")
COL = ("yh", "z")
ALL = ROW + COL
TILES = 8
VMEM_LIMIT = 48 * 1024 * 1024
F32 = jnp.float32
BF16 = jnp.bfloat16


def dft_tables():
    index = np.arange(SIZE)
    angle = 2.0 * math.pi / SIZE * (np.outer(index, index) % SIZE)
    real = np.cos(angle) / math.sqrt(SIZE)
    imag = -np.sin(angle) / math.sqrt(SIZE)
    right = np.block([[real, imag], [-imag, real]]).astype(np.float32)
    high = right.astype(jnp.bfloat16)
    low = (right - high.astype(np.float32)).astype(jnp.bfloat16)
    right3 = np.concatenate([high, high, low], axis=0)
    left3 = np.ascontiguousarray(right3.T)
    return right3, left3


def halves(x):
    high = x.astype(BF16)
    return high, (x - high.astype(F32)).astype(BF16)


def right_transform(fields, table):
    rows = []
    for real, imag in fields:
        rh, rl = halves(real)
        ih, il = halves(imag)
        rows.append(jnp.concatenate([rh, ih, rl, il, rh, ih], axis=1))
    out = jnp.dot(jnp.concatenate(rows, axis=0), table, preferred_element_type=F32)
    return [
        (out[SIZE * n : SIZE * (n + 1), :SIZE], out[SIZE * n : SIZE * (n + 1), SIZE:])
        for n in range(len(fields))
    ]


def left_transform(fields, table):
    cols = []
    for real, imag in fields:
        rh, rl = halves(real)
        ih, il = halves(imag)
        cols.append(jnp.concatenate([rh, ih, rl, il, rh, ih], axis=0))
    out = jnp.dot(table, jnp.concatenate(cols, axis=1), preferred_element_type=F32)
    return [
        (out[:SIZE, SIZE * n : SIZE * (n + 1)], out[SIZE:, SIZE * n : SIZE * (n + 1)])
        for n in range(len(fields))
    ]


def lanes():
    return lax.broadcasted_iota(jnp.int32, (SIZE, SIZE), 1)


def window(ref, lead, row, col):
    shift = lax.rem(SIZE - col, SIZE)
    first = pltpu.roll(ref[lead + (0, pl.ds(row, SIZE))], shift, 1)
    second = pltpu.roll(ref[lead + (1, pl.ds(row, SIZE))], shift, 1)
    return jnp.where(lanes() < SIZE - col, first, second)


def place(ref, plane, row, col, block):
    moved = pltpu.roll(block, lax.rem(col, SIZE), 1)
    first = lanes() >= col
    rows = pl.ds(row, SIZE)
    ref[plane, 0, rows] += jnp.where(first, moved, 0.0)
    ref[plane, 1, rows] += jnp.where(first, 0.0, moved)


def join(low, first, second):
    return jnp.where(low, pltpu.roll(first, HALF, 1), pltpu.roll(second, HALF, 1))


def pack_low(low, upper, lower):
    return jnp.where(low, upper, pltpu.roll(lower, HALF, 1))


def pack_high(low, upper, lower):
    return jnp.where(low, pltpu.roll(upper, HALF, 1), lower)


def low_lanes(rows):
    return lax.broadcasted_iota(jnp.int32, (rows, SIZE), 1) < HALF


def bounds(edges):
    return tuple(edges[k] for k in range(4))


def inside(limits, down, across, rows=SIZE):
    row_low, row_high, col_low, col_high = limits
    line = lax.broadcasted_iota(jnp.int32, (rows, SIZE), 0) + down
    lane = lax.broadcasted_iota(jnp.int32, (rows, SIZE), 1) + across
    return (line >= row_low) & (line < row_high) & (lane >= col_low) & (lane < col_high)


def send_kernel(offsets, own, bottom, top):
    line = lax.broadcasted_iota(jnp.int32, (TILES, SIZE), 0)
    lane = lax.broadcasted_iota(jnp.int32, (TILES, SIZE), 1)
    code = jnp.zeros((TILES, SIZE), jnp.int32)
    batches, count, _ = offsets.shape
    for b in range(batches):
        for k in range(count):
            for d in range(2):
                code = jnp.where(lane == (b * count + k) * 2 + d, offsets[b, k, d], code)
    code = jnp.where(line == 0, code, 0).astype(F32)
    for c in range(2):
        bottom[c, :HALF] = own[c, HALF:]
        bottom[c, HALF:] = code
        top[c] = own[c, :HALF]


def pack_kernel(above, own, below, bottom, to_left, to_right):
    low = low_lanes(HALF)
    for c in range(2):
        strips = (above[c, :HALF], own[c, :HALF], own[c, HALF:], below[c])
        for k in range(2):
            rows = slice(HALF * k, HALF * (k + 1))
            to_left[c, rows] = pack_low(low, strips[k], strips[k + 2])
            to_right[c, rows] = pack_high(low, strips[k], strips[k + 2])
        to_right[c, SIZE : SIZE + TILES] = bottom[c, HALF:]
        to_right[c, SIZE + TILES :] = above[c, HALF:]


def sweep(batch, offsets, limits, padded, probe, measured, right3, left3,
          own, right, below, corner, sums, accum):
    accum[...] = jnp.zeros_like(accum)
    sums[...] = jnp.zeros_like(sums)
    tr = right3[...]
    tl = left3[...]

    def body(step, carry):
        wins = []
        fields = []
        for g in range(GROUP):
            j = step * GROUP + g
            row, col = offsets[batch, j, 0] + HALF, offsets[batch, j, 1] + HALF
            wr = window(padded, (0,), row, col)
            wi = window(padded, (1,), row, col)
            wins.append((row, col, wr, wi))
            for m in range(MODES):
                pr, pi = probe[0, m], probe[1, m]
                fields.append((pr * wr - pi * wi, pr * wi + pi * wr))
        waves = left_transform(right_transform(fields, tr), tl)
        back = []
        for g in range(GROUP):
            mine = waves[g * MODES : (g + 1) * MODES]
            intensity = sum(r * r + i * i for r, i in mine)
            recorded = measured[0, 0, batch, step * GROUP + g]
            ratio = jnp.sqrt(recorded) / jnp.maximum(jnp.sqrt(intensity), 0.5) - 1.0
            back += [(r * ratio, -(i * ratio)) for r, i in mine]
        chis = right_transform(left_transform(back, tl), tr)
        for g in range(GROUP):
            row, col, wr, wi = wins[g]
            cr = jnp.zeros((SIZE, SIZE), F32)
            ci = jnp.zeros((SIZE, SIZE), F32)
            for m in range(MODES):
                xr, xn = chis[g * MODES + m]
                pr, pi = probe[0, m], probe[1, m]
                cr += pr * xr - pi * xn
                ci -= pr * xn + pi * xr
                sums[m] += wr * xr - wi * xn
                sums[MODES + m] -= wr * xn + wi * xr
            sums[2 * MODES] += wr * wr + wi * wi
            place(accum, 0, row, col, cr)
            place(accum, 1, row, col, ci)
        return carry

    lax.fori_loop(0, COUNT // GROUP, body, 0)
    for v, h, out in ((0, 0, own), (0, 1, right), (1, 0, below), (1, 1, corner)):
        valid = inside(limits, v * SIZE, h * SIZE)
        for c in range(2):
            out[c] = jnp.where(valid, accum[c, h, v * SIZE : (v + 1) * SIZE], 0.0)


def first_kernel(offsets, edges, above, tile, below, from_left, from_right, probe, measured, right3, left3,
                 own_g, right_g, below_g, corner_g, sums, padded, core, accum):
    limits = bounds(edges)
    low = low_lanes(HALF)
    for c in range(2):
        strips = (above[c, :HALF], tile[c, :HALF], tile[c, HALF:], below[c])
        for k in range(4):
            half = slice(HALF * (k % 2), HALF * (k % 2 + 1))
            left, right = from_left[c, half], from_right[c, half]
            if k < 2:
                right = pltpu.roll(right, HALF, 1)
            else:
                left = pltpu.roll(left, HALF, 1)
            mine = pltpu.roll(strips[k], HALF, 1)
            rows = slice(HALF * k, HALF * (k + 1))
            first = jnp.where(low, left, mine)
            second = jnp.where(low, mine, right)
            if k < 2:
                core[c, rows] = first
            padded[c, 0, rows] = jnp.where(inside(limits, HALF * k, 0, HALF), first, 0.0)
            padded[c, 1, rows] = jnp.where(inside(limits, HALF * k, SIZE, HALF), second, 0.0)
    sweep(0, offsets, limits, padded, probe, measured, right3, left3,
          own_g, right_g, below_g, corner_g, sums, accum)


def window_classes(offsets, others, batch, limits):
    row_low, _, col_low, _ = limits
    line = lax.broadcasted_iota(jnp.int32, (SIZE, SIZE), 0)
    lane = lanes()
    count = offsets.shape[1]
    for v in range(2):
        for h in range(2):
            rows = line < SIZE - row_low if v else line >= row_low
            cols = lane < SIZE - col_low if h else lane >= col_low
            shifts = []
            for j in range(count):
                if v or h:
                    at = (batch * count + j) * 2
                    which = 2 * v + h - 1
                    row, col = others[which, at], others[which, at + 1]
                else:
                    row, col = offsets[batch, j, 0], offsets[batch, j, 1]
                shifts.append((row + HALF - v * SIZE, col + HALF - h * SIZE))
            yield rows & cols, shifts


def moved_sum(ref, lead, shifts, sign):
    lane = lanes()
    total = jnp.zeros((SIZE, SIZE), F32)
    for row, col in shifts:
        row, col = sign * row, sign * col
        moved = pltpu.roll(ref[lead + (pl.ds(SIZE + row, SIZE),)], lax.rem(2 * SIZE - col, SIZE), 1)
        source = lane + col
        total += jnp.where((source >= 0) & (source < SIZE), moved, 0.0)
    return total


def cover_kernel(batch, offsets, others, edges, probe, cover, light):
    limits = bounds(edges)
    light[...] = jnp.zeros_like(light)
    light[SIZE : 2 * SIZE] = sum(probe[c, m] * probe[c, m] for c in range(2) for m in range(MODES))
    total = jnp.zeros((SIZE, SIZE), F32)
    for mask, shifts in window_classes(offsets, others, batch, limits):
        total += jnp.where(mask, moved_sum(light, (), shifts, -1), 0.0)
    cover[...] = total


def merge_kernel(batch, offsets, others, edges, own, from_left, from_above, from_corner, cover, core, sums,
                 packed, numbers, direction, product):
    limits = bounds(edges)
    light = cover[...]
    inverse = 1.0 / (light + 1.0)
    dr, di = ((own[c] + from_left[c] + from_above[c] + from_corner[c]) * inverse for c in range(2))
    direction[0] = dr
    direction[1] = di
    power = dr * dr + di * di
    a11 = jnp.sum(power * light, axis=0, keepdims=True)
    b1 = jnp.sum(power * (light + 1.0), axis=0, keepdims=True)
    line = lax.broadcasted_iota(jnp.int32, (TILES, SIZE), 0)
    numbers[...] = jnp.where(line == 0, a11, jnp.where(line == 1, b1, 0.0))

    er = dr * core[0] + di * core[1]
    ei = dr * core[1] - di * core[0]
    for c in range(2):
        product[c, :SIZE] = jnp.zeros((SIZE, SIZE), F32)
        product[c, 2 * SIZE :] = jnp.zeros((SIZE, SIZE), F32)
    overlap = [jnp.zeros((SIZE, SIZE), F32)] * 2
    for mask, shifts in window_classes(offsets, others, batch, limits):
        product[0, SIZE : 2 * SIZE] = jnp.where(mask, er, 0.0)
        product[1, SIZE : 2 * SIZE] = jnp.where(mask, ei, 0.0)
        overlap = [overlap[c] + moved_sum(product, (c,), shifts, 1) for c in range(2)]

    strips = (SIZE // TILES, TILES, SIZE)
    for k in range(5):
        packed[:, k] = sums[k].reshape(strips)
    for c in range(2):
        packed[:, 5 + c] = overlap[c].reshape(strips)


def add_all(parts):
    total = parts[0]
    for k in range(1, parts.shape[0]):
        total = total + parts[k]
    return total


def scatter_kernel(parts, numbers, out):
    total = add_all(parts)
    for k in range(out.shape[0]):
        out[k, :7] = total
        out[k, 7] = numbers[...]


def reduce_kernel(parts, out):
    total = add_all(parts)
    for k in range(out.shape[0]):
        out[k] = total


def strip_kernel(place_ref, parts, probe, out):
    total = add_all(parts)
    rows = pl.ds(pl.multiple_of(place_ref[0] * TILES, TILES), TILES)
    cover = total[2 * MODES]
    inverse = 1.0 / (cover + 1.0)
    cross = jnp.zeros((TILES, SIZE), F32)
    power = jnp.zeros((TILES, SIZE), F32)
    for m in range(MODES):
        dr, di = total[m] * inverse, total[MODES + m] * inverse
        pr, pi = probe[0, m, rows], probe[1, m, rows]
        cross += (pr * dr + pi * di) * total[5] - (pr * di - pi * dr) * total[6]
        power += dr * dr + di * di
    line = lax.broadcasted_iota(jnp.int32, (TILES, SIZE), 0)
    numbers = total[7]
    for k, term in ((2, power * cover), (3, power * (cover + 1.0)), (4, cross)):
        numbers = jnp.where(line == k, jnp.sum(term, axis=0, keepdims=True), numbers)
    for k in range(out.shape[0]):
        out[k, :5] = total[:5]
        out[k, 5] = numbers


def step_sizes(totals, probe, new_probe, gradient=None):
    numbers = jnp.sum(add_all(totals.at[:, 5]), axis=1, keepdims=True)
    a11, b1, a22, b2, a12 = (numbers[k : k + 1] for k in range(5))
    a11 = 1.1 * a11
    a22 = 1.1 * a22
    det = a11 * a22 - a12 * a12
    step_obj = (b1 * a22 - a12 * b2) / det
    step_probe = (a11 * b2 - a12 * b1) / det
    cover = totals[:, 4].reshape(SIZE, SIZE) + 1.0
    scale = step_probe / cover
    for m in range(MODES):
        for c in range(2):
            numer = totals[:, MODES * c + m].reshape(SIZE, SIZE)
            new_probe[c, m] = probe[c, m] + scale * numer
            if gradient is not None:
                gradient[c, m] = numer * lax.rsqrt(cover)
    return step_obj


def next_kernel(offsets, edges, totals, padded, core, direction, from_below, from_right, from_corner, probe,
                measured, right3, left3,
                own_g, right_g, below_g, corner_g, sums, new_padded, new_core, new_probe, accum):
    limits = bounds(edges)
    step = step_sizes(totals, probe, new_probe)
    for v, h, part in ((0, 0, direction), (0, 1, from_right), (1, 0, from_below), (1, 1, from_corner)):
        valid = inside(limits, v * SIZE, h * SIZE)
        rows = slice(v * SIZE, (v + 1) * SIZE)
        for c in range(2):
            move = step * part[c]
            if (v, h) == (0, 0):
                new_core[c] = core[c] + move
            new_padded[c, h, rows] = padded[c, h, rows] + jnp.where(valid, move, 0.0)
    sweep(1, offsets, limits, new_padded, new_probe, measured, right3, left3,
          own_g, right_g, below_g, corner_g, sums, accum)


def last_kernel(totals, padded, direction, from_below, from_right, from_corner, probe,
                new_obj, new_probe, gradient):
    step = step_sizes(totals, probe, new_probe, gradient)
    low = low_lanes(HALF)
    for c in range(2):
        moves = (join(low, direction[c, HALF:], from_right[c]), join(low, from_below[c], from_corner[c]))
        for k in range(2):
            span = slice(HALF * (k + 1), HALF * (k + 2))
            old = join(low, padded[c, 0, span], padded[c, 1, span])
            new_obj[c, HALF * k : HALF * (k + 1)] = old + step * moves[k]


def shape(*dims):
    return jax.ShapeDtypeStruct(dims, F32)


def call(kernel, ins, outs, scratch=()):
    vmem = pl.BlockSpec(memory_space=pltpu.VMEM)
    smem = pl.BlockSpec(memory_space=pltpu.SMEM)
    specs = [smem if x.dtype == jnp.int32 else vmem for x in ins]
    return pl.pallas_call(
        kernel,
        in_specs=specs,
        out_specs=[vmem] * len(outs),
        out_shape=list(outs),
        scratch_shapes=list(scratch),
        compiler_params=pltpu.CompilerParams(vmem_limit_bytes=VMEM_LIMIT),
        name=getattr(kernel, "func", kernel).__name__,
    )(*ins)


def size_of(axes):
    return math.prod(lax.axis_size(a) for a in axes)


def shift(block, rows, cols):
    n_row, n_col = size_of(ROW), size_of(COL)
    route = [
        (r * n_col + c, (r + rows) % n_row * n_col + (c + cols) % n_col)
        for r in range(n_row)
        for c in range(n_col)
    ]
    return lax.ppermute(block, ALL, route)


def exchange(block, axes):
    return lax.all_to_all(block, axes, 0, 0, tiled=True)


def reduce_all(packed, numbers, probe, place_in_row, halo):
    part = exchange(packed, ROW)
    part, *halo = lax.optimization_barrier((part, *halo))
    (part,) = call(scatter_kernel, [part, numbers], [shape(size_of(("z",)), 8, TILES, SIZE)])
    part = exchange(part, ("z",))
    (part,) = call(reduce_kernel, [part], [shape(size_of(("yh",)), 8, TILES, SIZE)])
    part = exchange(part, ("yh",))
    (part,) = call(strip_kernel, [place_in_row, part, probe], [shape(packed.shape[0], 6, TILES, SIZE)])
    return exchange(part, ROW), halo


def per_device(obj, probe, measured, offsets):
    right3, left3 = (jnp.asarray(t) for t in dft_tables())
    offsets = offsets[0, 0]
    r, c = (lax.axis_index(axes).astype(jnp.int32) for axes in (ROW, COL))
    place_in_row = r.reshape(1)
    whole = 2 * SIZE
    edges = jnp.stack([
        jnp.where(r == 0, HALF, 0),
        jnp.where(r == size_of(ROW) - 1, whole - HALF, whole),
        jnp.where(c == 0, HALF, 0),
        jnp.where(c == size_of(COL) - 1, whole - HALF, whole),
    ]).astype(jnp.int32)
    quad = shape(2, SIZE, SIZE)
    field = shape(2, 2, whole, SIZE)
    planes = shape(2, MODES, SIZE, SIZE)
    accum = pltpu.VMEM((2, 2, whole, SIZE), F32)

    bottom, top = call(send_kernel, [offsets, obj], [shape(2, HALF + TILES, SIZE), shape(2, HALF, SIZE)])
    above = shift(bottom, 1, 0)
    below = shift(top, -1, 0)
    to_left, to_right = call(
        pack_kernel, [above, obj, below, bottom], [quad, shape(2, SIZE + 2 * TILES, SIZE)])
    from_left = shift(to_right, 0, 1)
    from_right = shift(to_left, 0, -1)
    others = jnp.concatenate(
        [from_left[0, SIZE : SIZE + 1], above[0, HALF : HALF + 1],
         from_left[0, SIZE + TILES : SIZE + TILES + 1]], axis=0)
    others = others[:, : offsets.size].astype(jnp.int32)

    *parts, sums, padded, core = call(
        first_kernel,
        [offsets, edges, above, obj, below, from_left, from_right, probe, measured, right3, left3],
        [quad] * 4 + [shape(5, SIZE, SIZE), field, quad],
        [accum],
    )

    def merge(batch, parts, sums, core, probe):
        own, right, below, corner = parts
        from_left = shift(right, 0, 1)
        from_above = shift(below, 1, 0)
        from_corner = shift(corner, 1, 1)
        (cover,) = call(
            partial(cover_kernel, batch), [offsets, others, edges, probe], [shape(SIZE, SIZE)],
            [pltpu.VMEM((3 * SIZE, SIZE), F32)])
        return call(
            partial(merge_kernel, batch),
            [offsets, others, edges, own, from_left, from_above, from_corner, cover, core, sums],
            [shape(SIZE // TILES, 7, TILES, SIZE), shape(TILES, SIZE), quad],
            [pltpu.VMEM((2, 3 * SIZE, SIZE), F32)],
        )

    packed, numbers, direction = merge(0, parts, sums, core, probe)
    halo = shift(direction, -1, 0), shift(direction, 0, -1), shift(direction, -1, -1)
    totals, halo = reduce_all(packed, numbers, probe, place_in_row, halo)
    *parts, sums, padded, core, probe = call(
        next_kernel,
        [offsets, edges, totals, padded, core, direction, *halo, probe, measured, right3, left3],
        [quad] * 4 + [shape(5, SIZE, SIZE), field, quad, planes],
        [accum],
    )
    packed, numbers, direction = merge(1, parts, sums, core, probe)
    upper, lower = direction[:, :HALF], direction[:, HALF:]
    halo = shift(upper, -1, 0), shift(lower, 0, -1), shift(upper, -1, -1)
    totals, halo = reduce_all(packed, numbers, probe, place_in_row, halo)
    return tuple(call(
        last_kernel, [totals, padded, direction, *halo, probe], [quad, planes, planes]))


def solution(mesh):
    parts = Mesh(mesh.devices.reshape(2, 4, 2, 4, 8), ALL)
    in_specs = (P(None, ROW, COL), P(), P(ROW, COL), P(ROW, COL))
    out_specs = (P(None, ROW, COL), P(), P())
    return jax.shard_map(
        per_device, mesh=parts, in_specs=in_specs, out_specs=out_specs, check_vma=False
    )
```

```python
import math
from functools import partial

import jax
import jax.numpy as jnp
import numpy as np
from jax import lax
from jax.experimental import pallas as pl
from jax.experimental.pallas import tpu as pltpu
from jax.sharding import Mesh, PartitionSpec as P

SIZE = 128
HALF = 64
MODES = 2
COUNT = 8
GROUP = 2
ROW = ("yl", "x", "c")
COL = ("yh", "zh", "zl")
ALL = ROW + COL
SCATTER = ROW + ("zl",)
REST = ("yh", "zh")
TILES = 8
VMEM_LIMIT = 48 * 1024 * 1024
F32 = jnp.float32
BF16 = jnp.bfloat16


def dft_tables():
    index = np.arange(SIZE)
    angle = 2.0 * math.pi / SIZE * (np.outer(index, index) % SIZE)
    real = np.cos(angle) / math.sqrt(SIZE)
    imag = -np.sin(angle) / math.sqrt(SIZE)
    right = np.block([[real, imag], [-imag, real]]).astype(np.float32)
    high = right.astype(jnp.bfloat16)
    low = (right - high.astype(np.float32)).astype(jnp.bfloat16)
    right3 = np.concatenate([high, high, low], axis=0)
    left3 = np.ascontiguousarray(right3.T)
    return right3, left3


def halves(x):
    high = x.astype(BF16)
    return high, (x - high.astype(F32)).astype(BF16)


def right_transform(fields, table):
    rows = []
    for real, imag in fields:
        rh, rl = halves(real)
        ih, il = halves(imag)
        rows.append(jnp.concatenate([rh, ih, rl, il, rh, ih], axis=1))
    out = jnp.dot(jnp.concatenate(rows, axis=0), table, preferred_element_type=F32)
    return [
        (out[SIZE * n : SIZE * (n + 1), :SIZE], out[SIZE * n : SIZE * (n + 1), SIZE:])
        for n in range(len(fields))
    ]


def left_transform(fields, table):
    cols = []
    for real, imag in fields:
        rh, rl = halves(real)
        ih, il = halves(imag)
        cols.append(jnp.concatenate([rh, ih, rl, il, rh, ih], axis=0))
    out = jnp.dot(table, jnp.concatenate(cols, axis=1), preferred_element_type=F32)
    return [
        (out[:SIZE, SIZE * n : SIZE * (n + 1)], out[SIZE:, SIZE * n : SIZE * (n + 1)])
        for n in range(len(fields))
    ]


def lanes():
    return lax.broadcasted_iota(jnp.int32, (SIZE, SIZE), 1)


def window(ref, lead, row, col):
    shift = lax.rem(SIZE - col, SIZE)
    first = pltpu.roll(ref[lead + (0, pl.ds(row, SIZE))], shift, 1)
    second = pltpu.roll(ref[lead + (1, pl.ds(row, SIZE))], shift, 1)
    return jnp.where(lanes() < SIZE - col, first, second)


def place(ref, plane, row, col, block):
    moved = pltpu.roll(block, lax.rem(col, SIZE), 1)
    first = lanes() >= col
    rows = pl.ds(row, SIZE)
    ref[plane, 0, rows] += jnp.where(first, moved, 0.0)
    ref[plane, 1, rows] += jnp.where(first, 0.0, moved)


def join(low, first, second):
    return jnp.where(low, pltpu.roll(first, HALF, 1), pltpu.roll(second, HALF, 1))


def pack_low(low, upper, lower):
    return jnp.where(low, upper, pltpu.roll(lower, HALF, 1))


def pack_high(low, upper, lower):
    return jnp.where(low, pltpu.roll(upper, HALF, 1), lower)


def low_lanes(rows):
    return lax.broadcasted_iota(jnp.int32, (rows, SIZE), 1) < HALF


def bounds(edges):
    return tuple(edges[k] for k in range(4))


def inside(limits, down, across, rows=SIZE):
    row_low, row_high, col_low, col_high = limits
    line = lax.broadcasted_iota(jnp.int32, (rows, SIZE), 0) + down
    lane = lax.broadcasted_iota(jnp.int32, (rows, SIZE), 1) + across
    return (line >= row_low) & (line < row_high) & (lane >= col_low) & (lane < col_high)


def pad_field(above, own, below, from_left, from_right, store):
    low = low_lanes(HALF)
    for c in range(2):
        strips = (above[c], own[c, :HALF], own[c, HALF:], below[c])
        for k in range(4):
            half = slice(HALF * (k % 2), HALF * (k % 2 + 1))
            left, right = from_left[c, half], from_right[c, half]
            if k < 2:
                right = pltpu.roll(right, HALF, 1)
            else:
                left = pltpu.roll(left, HALF, 1)
            mine = pltpu.roll(strips[k], HALF, 1)
            rows = slice(HALF * k, HALF * (k + 1))
            store(c, 0, rows, jnp.where(low, left, mine))
            store(c, 1, rows, jnp.where(low, mine, right))


def pack_kernel(above, own, below, left, right):
    low = low_lanes(HALF)
    for c in range(2):
        strips = (above[c], own[c, :HALF], own[c, HALF:], below[c])
        for k in range(2):
            rows = slice(HALF * k, HALF * (k + 1))
            left[c, rows] = pack_low(low, strips[k], strips[k + 2])
            right[c, rows] = pack_high(low, strips[k], strips[k + 2])


def power_of(probe):
    return sum(probe[c, m] * probe[c, m] for c in range(2) for m in range(MODES))


def sweep(batch, offsets, padded, probe, measured, right3, left3, sums, accum):
    accum[...] = jnp.zeros_like(accum)
    sums[...] = jnp.zeros_like(sums)
    light = power_of(probe) if accum.shape[0] == 3 else None
    tr = right3[...]
    tl = left3[...]

    def body(step, carry):
        wins = []
        fields = []
        for g in range(GROUP):
            j = step * GROUP + g
            row, col = offsets[batch, j, 0] + HALF, offsets[batch, j, 1] + HALF
            wr = window(padded, (0,), row, col)
            wi = window(padded, (1,), row, col)
            wins.append((row, col, wr, wi))
            for m in range(MODES):
                pr, pi = probe[0, m], probe[1, m]
                fields.append((pr * wr - pi * wi, pr * wi + pi * wr))
        waves = left_transform(right_transform(fields, tr), tl)
        back = []
        for g in range(GROUP):
            own = waves[g * MODES : (g + 1) * MODES]
            intensity = sum(r * r + i * i for r, i in own)
            recorded = measured[0, 0, batch, step * GROUP + g]
            ratio = jnp.sqrt(recorded) / jnp.maximum(jnp.sqrt(intensity), 0.5) - 1.0
            back += [(r * ratio, -(i * ratio)) for r, i in own]
        chis = right_transform(left_transform(back, tl), tr)
        for g in range(GROUP):
            row, col, wr, wi = wins[g]
            cr = jnp.zeros((SIZE, SIZE), F32)
            ci = jnp.zeros((SIZE, SIZE), F32)
            for m in range(MODES):
                xr, xn = chis[g * MODES + m]
                pr, pi = probe[0, m], probe[1, m]
                cr += pr * xr - pi * xn
                ci -= pr * xn + pi * xr
                sums[m] += wr * xr - wi * xn
                sums[MODES + m] -= wr * xn + wi * xr
            sums[2 * MODES] += wr * wr + wi * wi
            place(accum, 0, row, col, cr)
            place(accum, 1, row, col, ci)
            if light is not None:
                place(accum, 2, row, col, light)
        return carry

    lax.fori_loop(0, COUNT // GROUP, body, 0)


def first_kernel(offsets, above, own, below, from_left, from_right, probe, measured, right3, left3,
                 top, bottom, sums, padded, accum):
    def store(c, h, rows, value):
        padded[c, h, rows] = value

    pad_field(above, own, below, from_left, from_right, store)
    sweep(0, offsets, padded, probe, measured, right3, left3, sums, accum)
    top[...] = accum[:, :, :SIZE]
    bottom[...] = accum[:, :, SIZE:]


def cover_kernel(shifts, probe, cover, total):
    total[...] = jnp.zeros_like(total)
    light = power_of(probe)
    lane = lanes()

    def body(k, carry):
        row, col = shifts[k, 0] + SIZE + HALF, shifts[k, 1] + SIZE + HALF

        @pl.when((row >= 0) & (row <= 3 * SIZE) & (col >= 0) & (col <= 3 * SIZE))
        def _():
            block = lax.div(col, SIZE)
            turn = lax.rem(col, SIZE)
            moved = pltpu.roll(light, turn, 1)
            first = lane >= turn
            rows = pl.ds(row, SIZE)
            total[block, rows] += jnp.where(first, moved, 0.0)
            total[block + 1, rows] += jnp.where(first, 0.0, moved)

        return carry

    lax.fori_loop(0, shifts.shape[0], body, 0)
    cover[...] = total[1:3, SIZE : 3 * SIZE]


def wide_fold_kernel(top, bottom, from_above, from_below, left, right):
    for v, own, other in ((0, top, from_above), (1, bottom, from_below)):
        left[v] = own[:, 0] + other[:, 0]
        right[v] = own[:, 1] + other[:, 1]


def pack_planes(packed, planes):
    strips = (SIZE // TILES, TILES, SIZE)
    upper = lax.rem(lax.broadcasted_iota(jnp.int32, (SIZE, SIZE), 0), TILES) < TILES // 2
    for q in range(len(planes) // 2):
        one, two = planes[2 * q], planes[2 * q + 1]
        packed[:, 0, q] = jnp.where(upper, one, pltpu.roll(two, TILES // 2, 0)).reshape(strips)
        packed[:, 1, q] = jnp.where(upper, pltpu.roll(one, SIZE - TILES // 2, 0), two).reshape(strips)


def unpack_planes(packed, q):
    upper = lax.rem(lax.broadcasted_iota(jnp.int32, (SIZE, SIZE), 0), TILES) < TILES // 2
    one, two = (packed[:, h, q].reshape(SIZE, SIZE) for h in range(2))
    return (jnp.where(upper, one, pltpu.roll(two, TILES // 2, 0)),
            jnp.where(upper, pltpu.roll(one, SIZE - TILES // 2, 0), two))


def pack_sums(packed, sums, overlap, a11, b1):
    turn = lax.rem(lax.broadcasted_iota(jnp.int32, (SIZE, SIZE), 0), TILES // 2)
    numbers = jnp.where(turn == 0, a11, jnp.where(turn == 1, b1, 0.0))
    pack_planes(packed, [sums[k] for k in range(5)] + [numbers] + list(overlap))


def wide_merge_kernel(edges, offsets, left, right, from_left, from_right, cover, padded, sums,
                      packed, direction, product):
    limits = bounds(edges)
    a11 = jnp.zeros((1, SIZE), F32)
    b1 = jnp.zeros((1, SIZE), F32)
    for v in range(2):
        rows = slice(v * SIZE, (v + 1) * SIZE)
        mine_rows = lax.broadcasted_iota(jnp.int32, (SIZE, SIZE), 0) + v * SIZE
        for h in range(2):
            own, other = ((left, from_left), (right, from_right))[h]
            light = cover[h, rows]
            inverse = jnp.where(inside(limits, v * SIZE, h * SIZE), 1.0 / (light + 1.0), 0.0)
            dr, di = ((own[v, c] + other[v, c]) * inverse for c in range(2))
            direction[0, h, rows] = dr
            direction[1, h, rows] = di
            pr, pi = padded[0, h, rows], padded[1, h, rows]
            product[0, h, rows] = dr * pr + di * pi
            product[1, h, rows] = dr * pi - di * pr
            across = lanes() + h * SIZE
            mine = (mine_rows >= HALF) & (mine_rows < HALF + SIZE) & (across >= HALF) & (across < HALF + SIZE)
            power = jnp.where(mine, dr * dr + di * di, 0.0)
            a11 += jnp.sum(power * light, axis=0, keepdims=True)
            b1 += jnp.sum(power * (light + 1.0), axis=0, keepdims=True)
    overlap = [jnp.zeros((SIZE, SIZE), F32)] * 2
    for j in range(COUNT):
        row, col = offsets[0, j, 0] + HALF, offsets[0, j, 1] + HALF
        overlap = [overlap[c] + window(product, (c,), row, col) for c in range(2)]
    pack_sums(packed, sums, overlap, a11, b1)


def fold_kernel(middle, from_above, from_below, tile, left, right):
    low = low_lanes(HALF)
    for k in range(3):
        upper = [middle[k, h, :HALF] + from_above[k, h] for h in range(2)]
        lower = [middle[k, h, HALF:] + from_below[k, h] for h in range(2)]
        tile[k, :HALF] = join(low, *upper)
        tile[k, HALF:] = join(low, *lower)
        left[k] = pack_low(low, upper[0], lower[0])
        right[k] = pack_high(low, upper[1], lower[1])


def merge_kernel(shifts, tile, from_left, from_right, padded, sums,
                 packed, direction, product, overlap):
    low = low_lanes(HALF)
    lane = lanes()
    a11 = jnp.zeros((1, SIZE), F32)
    b1 = jnp.zeros((1, SIZE), F32)
    product[...] = jnp.zeros_like(product)
    for v in range(2):
        rows = slice(HALF * v, HALF * (v + 1))
        full = []
        for k in range(3):
            left, right = from_left[k], from_right[k]
            if v == 0:
                right = pltpu.roll(right, HALF, 1)
            else:
                left = pltpu.roll(left, HALF, 1)
            full.append(tile[k, rows] + jnp.where(low, left, right))
        gr, gi, cover = full
        inverse = 1.0 / (cover + 1.0)
        dr = gr * inverse
        di = gi * inverse
        direction[0, rows] = dr
        direction[1, rows] = di
        span = slice(HALF * (v + 1), HALF * (v + 2))
        pr = join(low, padded[0, 0, span], padded[0, 1, span])
        pi = join(low, padded[1, 0, span], padded[1, 1, span])
        inner = slice(SIZE + HALF * v, SIZE + HALF * (v + 1))
        product[0, inner] = dr * pr + di * pi
        product[1, inner] = dr * pi - di * pr
        power = dr * dr + di * di
        a11 += jnp.sum(power * cover, axis=0, keepdims=True)
        b1 += jnp.sum(power * (cover + 1.0), axis=0, keepdims=True)
    overlap[...] = jnp.zeros_like(overlap)

    def body(k, carry):
        down, across = shifts[k, 0], shifts[k, 1]

        @pl.when((jnp.abs(down) < SIZE) & (jnp.abs(across) < SIZE))
        def _():
            turn = lax.rem(SIZE - across, SIZE)
            source = lane + across
            inside = (source >= 0) & (source < SIZE)
            for c in range(2):
                moved = pltpu.roll(product[c, pl.ds(SIZE + down, SIZE)], turn, 1)
                overlap[c] += jnp.where(inside, moved, 0.0)

        return carry

    lax.fori_loop(0, shifts.shape[0], body, 0)

    pack_sums(packed, sums, (overlap[0], overlap[1]), a11, b1)


def add_all(parts):
    total = parts[0]
    for k in range(1, parts.shape[0]):
        total = total + parts[k]
    return total


def reduce_kernel(parts, out):
    total = add_all(parts)
    for k in range(out.shape[0]):
        out[k] = total


def strip_kernel(place_ref, parts, probe, out):
    total = add_all(parts)
    line = lax.broadcasted_iota(jnp.int32, (TILES, SIZE), 0)
    half = TILES // 2
    upper = line < half
    first = place_ref[1] == 0
    rows = pl.ds(pl.multiple_of(place_ref[0] * TILES, TILES), TILES)

    def turned(x):
        return pltpu.roll(x, half, 0)

    def both(x, of_upper):
        return jnp.where(upper == of_upper, x, turned(x))

    def modes(c):
        one, two = probe[c, 0, rows], probe[c, 1, rows]
        return jnp.where(upper, jnp.where(first, one, turned(one)), jnp.where(first, turned(two), two))

    pr, pi = modes(0), modes(1)
    cover = both(total[2], True)
    inverse = 1.0 / (cover + 1.0)
    dr, di = total[0] * inverse, total[1] * inverse
    cross = (pr * dr + pi * di) * both(total[3], True) - (pr * di - pi * dr) * both(total[3], False)
    power = dr * dr + di * di
    a22, b2, a12 = (
        jnp.sum(x, axis=0, keepdims=True) for x in (power * cover, power * (cover + 1.0), cross))
    a11, b1 = total[2, half : half + 1], total[2, half + 1 : half + 2]
    low = low_lanes(1)
    known = jnp.where(low, a11 + pltpu.roll(a11, HALF, 1), b1 + pltpu.roll(b1, HALF, 1))
    numbers = total[2]
    for k, term in enumerate((known, a22, b2, a12)):
        numbers = jnp.where(line == half + k, term, numbers)
    for k in range(out.shape[0]):
        out[k, 0] = total[0]
        out[k, 1] = total[1]
        out[k, 2] = numbers


def step_sizes(totals, probe, new_probe, gradient=None):
    numbers = jnp.zeros((TILES, SIZE), F32)
    for k in range(totals.shape[0]):
        numbers += totals[k, 0, 2] + totals[k, 1, 2]
    half = TILES // 2
    low = low_lanes(1)
    known, *rest = (numbers[half + k : half + k + 1] for k in range(4))
    a22, b2, a12 = (jnp.sum(x, axis=1, keepdims=True) for x in rest)
    share = 1.0 / (2 * totals.shape[0])
    a11 = jnp.sum(jnp.where(low, known, 0.0), axis=1, keepdims=True) * share
    b1 = jnp.sum(jnp.where(low, 0.0, known), axis=1, keepdims=True) * share
    a11 = 1.1 * a11
    a22 = 1.1 * a22
    det = a11 * a22 - a12 * a12
    step_obj = (b1 * a22 - a12 * b2) / det
    step_probe = (a11 * b2 - a12 * b1) / det
    cover, _ = unpack_planes(totals, 2)
    cover = cover + 1.0
    scale = step_probe / cover
    for c in range(2):
        for m, numer in enumerate(unpack_planes(totals, c)):
            new_probe[c, m] = probe[c, m] + scale * numer
            if gradient is not None:
                gradient[c, m] = numer * lax.rsqrt(cover)
    return step_obj


def next_kernel(offsets, totals, padded, direction, probe, measured, right3, left3,
                top, middle, bottom, sums, new_padded, new_probe, accum):
    step = step_sizes(totals, probe, new_probe)
    new_padded[...] = padded[...] + step * direction[...]
    sweep(1, offsets, new_padded, new_probe, measured, right3, left3, sums, accum)
    top[...] = accum[:, :, :HALF]
    middle[...] = accum[:, :, HALF : HALF + SIZE]
    bottom[...] = accum[:, :, HALF + SIZE :]


def last_kernel(totals, padded, direction, probe, new_obj, new_probe, gradient):
    step = step_sizes(totals, probe, new_probe, gradient)
    low = lanes() < HALF
    rows = slice(HALF, HALF + SIZE)
    for c in range(2):
        old = join(low, padded[c, 0, rows], padded[c, 1, rows])
        new_obj[c] = old + step * direction[c]


def shape(*dims):
    return jax.ShapeDtypeStruct(dims, F32)


def call(kernel, ins, outs, scratch=()):
    vmem = pl.BlockSpec(memory_space=pltpu.VMEM)
    smem = pl.BlockSpec(memory_space=pltpu.SMEM)
    specs = [smem if x.dtype == jnp.int32 else vmem for x in ins]
    return pl.pallas_call(
        kernel,
        in_specs=specs,
        out_specs=[vmem] * len(outs),
        out_shape=list(outs),
        scratch_shapes=list(scratch),
        compiler_params=pltpu.CompilerParams(vmem_limit_bytes=VMEM_LIMIT),
        name=getattr(kernel, "func", kernel).__name__,
    )(*ins)


def shift(block, rows, cols):
    n_row = math.prod(lax.axis_size(a) for a in ROW)
    n_col = math.prod(lax.axis_size(a) for a in COL)
    route = [
        (r * n_col + c, (r + rows) * n_col + c + cols)
        for r in range(n_row)
        for c in range(n_col)
        if 0 <= r + rows < n_row and 0 <= c + cols < n_col
    ]
    return lax.ppermute(block, ALL, route)


def exchange(block, axes):
    return lax.all_to_all(block, axes, 0, 0, tiled=True)


def size_of(axes):
    return math.prod(lax.axis_size(a) for a in axes)


def reduce_all(packed, probe, place_in_group):
    group, rest = size_of(SCATTER), size_of(REST)
    part = exchange(packed.reshape(group, 4, TILES, SIZE), SCATTER)
    (part,) = call(reduce_kernel, [part], [shape(rest, 4, TILES, SIZE)])
    part = exchange(part, REST)
    (part,) = call(strip_kernel, [place_in_group, part, probe], [shape(group, 3, TILES, SIZE)])
    return exchange(part, SCATTER).reshape(SIZE // TILES, 2, 3, TILES, SIZE)


MARK = 1024.0


def per_device(obj, probe, measured, offsets):
    right3, left3 = (jnp.asarray(t) for t in dft_tables())
    offsets = offsets[0, 0]
    batches = offsets.shape[0]
    r, c, half = (lax.axis_index(axes).astype(jnp.int32) for axes in (ROW, COL, ("zl",)))
    whole = 2 * SIZE
    place_in_group = jnp.stack([r, half])
    edges = jnp.stack([
        jnp.where(r == 0, HALF, 0),
        jnp.where(r == size_of(ROW) - 1, whole - HALF, whole),
        jnp.where(c == 0, HALF, 0),
        jnp.where(c == size_of(COL) - 1, whole - HALF, whole),
    ]).astype(jnp.int32)

    code = jnp.zeros((TILES * SIZE,), F32).at[: offsets.size].set(
        offsets.reshape(-1).astype(F32) + MARK)
    code = code.reshape(1, TILES, SIZE)

    def with_code(strip, more):
        return jnp.concatenate([strip, jnp.pad(more, ((0, 1), (0, 0), (0, 0)))], axis=1)

    above = shift(with_code(obj[:, HALF:], code), 1, 0)
    below = shift(with_code(obj[:, :HALF], code), -1, 0)
    codes = jnp.concatenate([above[:1, HALF:], code, below[:1, HALF:]], axis=1)
    above, below = above[:, :HALF], below[:, :HALF]
    packed_field = shape(2, SIZE, SIZE)
    left, right = call(pack_kernel, [above, obj, below], [packed_field] * 2)
    from_left = shift(with_code(right, codes), 0, 1)
    from_right = shift(with_code(left, codes), 0, -1)
    codes = jnp.stack([from_left[0, SIZE:], codes[0], from_right[0, SIZE:]])
    codes = codes.reshape(3, 3, -1)[:, :, : offsets.size].reshape((3, 3) + offsets.shape)
    away = jnp.arange(-1, 2, dtype=jnp.int32) * SIZE
    steps = jnp.stack([
        jnp.broadcast_to(away[None, :, None, None], codes.shape[:-1]),
        jnp.broadcast_to(away[:, None, None, None], codes.shape[:-1]),
    ], axis=-1)
    shifts = (codes - MARK).astype(jnp.int32) + steps
    shifts = jnp.moveaxis(shifts, 2, 0).reshape(batches, -1, 2)

    field = shape(2, 2, whole, SIZE)
    edge = shape(3, 2, HALF, SIZE)
    quads = shape(2, 2, SIZE, SIZE)
    planes = shape(2, MODES, SIZE, SIZE)
    sums_shape = shape(5, SIZE, SIZE)
    packed_shape = shape(SIZE // TILES, 2, 4, TILES, SIZE)

    top, bottom, sums, padded = call(
        first_kernel,
        [offsets, above, obj, below, from_left[:, :SIZE], from_right[:, :SIZE], probe, measured, right3, left3],
        [quads, quads, sums_shape, field],
        [pltpu.VMEM((2, 2, whole, SIZE), F32)],
    )
    from_above = shift(bottom, 1, 0)
    from_below = shift(top, -1, 0)
    (cover,) = call(
        cover_kernel, [shifts[0], probe], [shape(2, whole, SIZE)], [pltpu.VMEM((5, 4 * SIZE, SIZE), F32)])
    left, right = call(wide_fold_kernel, [top, bottom, from_above, from_below], [quads, quads])
    from_left = shift(right, 0, 1)
    from_right = shift(left, 0, -1)
    packed, direction = call(
        wide_merge_kernel,
        [edges, offsets, left, right, from_left, from_right, cover, padded, sums],
        [packed_shape, field],
        [pltpu.VMEM((2, 2, whole, SIZE), F32)],
    )
    totals = reduce_all(packed, probe, place_in_group)

    top, middle, bottom, sums, padded, probe = call(
        next_kernel,
        [offsets, totals, padded, direction, probe, measured, right3, left3],
        [edge, shape(3, 2, SIZE, SIZE), edge, sums_shape, field, planes],
        [pltpu.VMEM((3, 2, whole, SIZE), F32)],
    )
    from_above = shift(bottom, 1, 0)
    from_below = shift(top, -1, 0)
    side = shape(3, HALF, SIZE)
    tile, left, right = call(
        fold_kernel, [middle, from_above, from_below], [shape(3, SIZE, SIZE), side, side])
    from_left = shift(right, 0, 1)
    from_right = shift(left, 0, -1)
    packed, direction = call(
        merge_kernel,
        [shifts[1], tile, from_left, from_right, padded, sums],
        [packed_shape, shape(2, SIZE, SIZE)],
        [pltpu.VMEM((2, 3 * SIZE, SIZE), F32), pltpu.VMEM((2, SIZE, SIZE), F32)],
    )
    totals = reduce_all(packed, probe, place_in_group)
    return tuple(call(
        last_kernel, [totals, padded, direction, probe], [shape(2, SIZE, SIZE), planes, planes]
    ))


def solution(mesh):
    parts = Mesh(mesh.devices.reshape(2, 4, 2, 4, 4, 2), ALL)
    in_specs = (P(None, ROW, COL), P(), P(ROW, COL), P(ROW, COL))
    out_specs = (P(None, ROW, COL), P(), P())
    return jax.shard_map(
        per_device, mesh=parts, in_specs=in_specs, out_specs=out_specs, check_vma=False
    )
```

```python
import math
from functools import partial

import jax
import jax.numpy as jnp
import numpy as np
from jax import lax
from jax.experimental import pallas as pl
from jax.experimental.pallas import tpu as pltpu
from jax.sharding import Mesh, PartitionSpec as P

SIZE = 128
HALF = 64
MODES = 2
COUNT = 8
GROUP = 8
ROW = ("yl", "x", "c")
COL = ("yh", "zh", "zl")
ALL = ROW + COL
SCATTER = ROW + ("zl",)
REST = ("yh", "zh")
MARK = 1024
LIST_STEP = 4
LIST_SIZE = 9 * COUNT + 8
TILES = 8
VMEM_LIMIT = 16 * 1024 * 1024
F32 = jnp.float32
BF16 = jnp.bfloat16


def dft_tables():
    index = np.arange(SIZE)
    angle = 2.0 * math.pi / SIZE * (np.outer(index, index) % SIZE)
    real = np.cos(angle) / math.sqrt(SIZE)
    imag = -np.sin(angle) / math.sqrt(SIZE)
    right = np.block([[real, imag], [-imag, real]]).astype(np.float32)
    high = right.astype(jnp.bfloat16)
    low = (right - high.astype(np.float32)).astype(jnp.bfloat16)
    right3 = np.concatenate([high, high, low], axis=0)
    left3 = np.ascontiguousarray(right3.T)
    return right3, left3


def halves(x):
    high = x.astype(BF16)
    return high, (x - high.astype(F32)).astype(BF16)


def right_transform(fields, table):
    rows = []
    for real, imag in fields:
        rh, rl = halves(real)
        ih, il = halves(imag)
        rows.append(jnp.concatenate([rh, ih, rl, il, rh, ih], axis=1))
    out = jnp.dot(jnp.concatenate(rows, axis=0), table, preferred_element_type=F32)
    return [
        (out[SIZE * n : SIZE * (n + 1), :SIZE], out[SIZE * n : SIZE * (n + 1), SIZE:])
        for n in range(len(fields))
    ]


def left_transform(fields, table):
    cols = []
    for real, imag in fields:
        rh, rl = halves(real)
        ih, il = halves(imag)
        cols.append(jnp.concatenate([rh, ih, rl, il, rh, ih], axis=0))
    out = jnp.dot(table, jnp.concatenate(cols, axis=1), preferred_element_type=F32)
    return [
        (out[:SIZE, SIZE * n : SIZE * (n + 1)], out[SIZE:, SIZE * n : SIZE * (n + 1)])
        for n in range(len(fields))
    ]


def lanes():
    return lax.broadcasted_iota(jnp.int32, (SIZE, SIZE), 1)


def window(ref, lead, row, col):
    shift = lax.rem(SIZE - col, SIZE)
    rows = pl.ds(row, SIZE)
    mixed = jnp.where(lanes() >= col, ref[lead + (0, rows)], ref[lead + (1, rows)])
    return pltpu.roll(mixed, shift, 1)


def place(ref, plane, row, col, block):
    moved = pltpu.roll(block, lax.rem(col, SIZE), 1)
    first = lanes() >= col
    rows = pl.ds(row, SIZE)
    ref[plane, 0, rows] += jnp.where(first, moved, 0.0)
    ref[plane, 1, rows] += jnp.where(first, 0.0, moved)


def join(low, first, second):
    return jnp.where(low, pltpu.roll(first, HALF, 1), pltpu.roll(second, HALF, 1))


def pack_low(low, upper, lower):
    return jnp.where(low, upper, pltpu.roll(lower, HALF, 1))


def pack_high(low, upper, lower):
    return jnp.where(low, pltpu.roll(upper, HALF, 1), lower)


def low_lanes(rows):
    return lax.broadcasted_iota(jnp.int32, (rows, SIZE), 1) < HALF


def bounds(edges):
    return tuple(edges[k] for k in range(4))


def inside(limits, down, across, rows=SIZE):
    row_low, row_high, col_low, col_high = limits
    line = lax.broadcasted_iota(jnp.int32, (rows, SIZE), 0) + down
    lane = lax.broadcasted_iota(jnp.int32, (rows, SIZE), 1) + across
    return (line >= row_low) & (line < row_high) & (lane >= col_low) & (lane < col_high)


def pad_field(above, own, below, from_left, from_right, store):
    low = low_lanes(HALF)
    for c in range(2):
        strips = (above[c, :HALF], own[c, :HALF], own[c, HALF:], below[c, :HALF])
        for k in range(4):
            half = slice(HALF * (k % 2), HALF * (k % 2 + 1))
            left, right = from_left[c, half], from_right[c, half]
            if k < 2:
                right = pltpu.roll(right, HALF, 1)
            else:
                left = pltpu.roll(left, HALF, 1)
            mine = pltpu.roll(strips[k], HALF, 1)
            rows = slice(HALF * k, HALF * (k + 1))
            store(c, 0, rows, jnp.where(low, left, mine))
            store(c, 1, rows, jnp.where(low, mine, right))


def send_kernel(offsets, own, to_below, to_above):
    line = lax.broadcasted_iota(jnp.int32, (TILES, SIZE), 0)
    lane = lax.broadcasted_iota(jnp.int32, (TILES, SIZE), 1)
    code = jnp.zeros((TILES, SIZE), jnp.int32)
    batches, count, _ = offsets.shape
    for b in range(batches):
        for k in range(count):
            for d in range(2):
                code = jnp.where(lane == (b * count + k) * 2 + d, offsets[b, k, d] + MARK, code)
    code = jnp.where(line == 0, code, 0).astype(F32)
    for c in range(2):
        to_below[c, :HALF] = own[c, HALF:]
        to_above[c, :HALF] = own[c, :HALF]
        to_below[c, HALF:] = code
        to_above[c, HALF:] = code


def pack_kernel(above, own, below, mine, to_left, to_right, codes):
    low = low_lanes(HALF)
    for c in range(2):
        strips = (above[c, :HALF], own[c, :HALF], own[c, HALF:], below[c, :HALF])
        for k in range(2):
            rows = slice(HALF * k, HALF * (k + 1))
            to_left[c, rows] = pack_low(low, strips[k], strips[k + 2])
            to_right[c, rows] = pack_high(low, strips[k], strips[k + 2])
    code = mine[0, HALF:] + pltpu.roll(above[0, HALF:], 1, 0) + pltpu.roll(below[0, HALF:], 2, 0)
    for c in range(2):
        to_left[c, SIZE:] = code
        to_right[c, SIZE:] = code
    codes[...] = code


def power_of(probe):
    return sum(probe[c, m] * probe[c, m] for c in range(2) for m in range(MODES))


def sweep(batch, offsets, padded, probe, measured, right3, left3, sums, accum):
    accum[...] = jnp.zeros_like(accum)
    sums[...] = jnp.zeros_like(sums)
    light = power_of(probe) if accum.shape[0] == 3 else None
    tr = right3[...]
    tl = left3[...]

    def body(step, carry):
        wins = []
        fields = []
        for g in range(GROUP):
            j = step * GROUP + g
            row, col = offsets[batch, j, 0] + HALF, offsets[batch, j, 1] + HALF
            wr = window(padded, (0,), row, col)
            wi = window(padded, (1,), row, col)
            wins.append((row, col, wr, wi))
            for m in range(MODES):
                pr, pi = probe[0, m], probe[1, m]
                fields.append((pr * wr - pi * wi, pr * wi + pi * wr))
        waves = left_transform(right_transform(fields, tr), tl)
        back = []
        for g in range(GROUP):
            own = waves[g * MODES : (g + 1) * MODES]
            intensity = sum(r * r + i * i for r, i in own)
            recorded = measured[0, 0, batch, step * GROUP + g]
            ratio = jnp.sqrt(recorded) / jnp.maximum(jnp.sqrt(intensity), 0.5) - 1.0
            back += [(r * ratio, -(i * ratio)) for r, i in own]
        chis = right_transform(left_transform(back, tl), tr)
        for g in range(GROUP):
            row, col, wr, wi = wins[g]
            cr = jnp.zeros((SIZE, SIZE), F32)
            ci = jnp.zeros((SIZE, SIZE), F32)
            for m in range(MODES):
                xr, xn = chis[g * MODES + m]
                pr, pi = probe[0, m], probe[1, m]
                cr += pr * xr - pi * xn
                ci -= pr * xn + pi * xr
                sums[m] += wr * xr - wi * xn
                sums[MODES + m] -= wr * xn + wi * xr
            sums[2 * MODES] += wr * wr + wi * wi
            place(accum, 0, row, col, cr)
            place(accum, 1, row, col, ci)
            if light is not None:
                place(accum, 2, row, col, light)
        return carry

    lax.fori_loop(0, COUNT // GROUP, body, 0)


def first_kernel(offsets, above, own, below, from_left, from_right, probe, measured, right3, left3,
                 top, bottom, sums, padded, accum):
    def store(c, h, rows, value):
        padded[c, h, rows] = value

    pad_field(above, own, below, from_left, from_right, store)
    sweep(0, offsets, padded, probe, measured, right3, left3, sums, accum)
    top[...] = accum[:, :, :SIZE]
    bottom[...] = accum[:, :, SIZE:]


def offset_of(others, batch, across, down, j, d):
    return others[TILES * across + (1, 0, 2)[down], (batch * COUNT + j) * 2 + d] - MARK


def cover_kernel(others, probe, cover, near, light):
    none = jnp.zeros((SIZE, SIZE), F32)
    light[:SIZE] = none
    light[SIZE : 2 * SIZE] = power_of(probe)
    light[2 * SIZE :] = none
    lane = lanes()
    for v in range(2):
        total = [none, none]
        for down in (v, v + 1):
            for across in range(3):
                for j in range(COUNT):
                    row, col = (offset_of(others, 0, across, down, j, d) + HALF for d in range(2))
                    row = jnp.clip(row + SIZE * (down - 1 - v), -SIZE, SIZE)
                    col = jnp.clip(col, 0, SIZE)
                    moved = pltpu.roll(light[pl.ds(SIZE - row, SIZE)], lax.rem(col, SIZE), 1)
                    first = lane >= col
                    if across >= 1:
                        total[across - 1] = total[across - 1] + jnp.where(first, moved, 0.0)
                    if across <= 1:
                        total[across] = total[across] + jnp.where(first, 0.0, moved)
        for h in range(2):
            cover[h, v * SIZE : (v + 1) * SIZE] = total[h]

    count = jnp.int32(0)
    for down in range(3):
        for across in range(3):
            for j in range(COUNT):
                row = offset_of(others, 1, across, down, j, 0) + SIZE * (down - 1)
                col = offset_of(others, 1, across, down, j, 1) + SIZE * (across - 1)
                near[count, 0] = row
                near[count, 1] = col
                reaches = (jnp.abs(row) < SIZE) & (jnp.abs(col) < SIZE)
                count += reaches.astype(jnp.int32)
    for k in range(LIST_STEP):
        near[count + k, 0] = SIZE
        near[count + k, 1] = 0
    near[LIST_SIZE - 1, 0] = count


def wide_fold_kernel(top, bottom, from_above, from_below, left, right):
    for v, own, other in ((0, top, from_above), (1, bottom, from_below)):
        left[v] = own[:, 0] + other[:, 0]
        right[v] = own[:, 1] + other[:, 1]


def pack_planes(packed, planes):
    strips = (SIZE // TILES, TILES, SIZE)
    upper = lax.rem(lax.broadcasted_iota(jnp.int32, (SIZE, SIZE), 0), TILES) < TILES // 2
    for q in range(len(planes) // 2):
        one, two = planes[2 * q], planes[2 * q + 1]
        packed[:, 0, q] = jnp.where(upper, one, pltpu.roll(two, TILES // 2, 0)).reshape(strips)
        packed[:, 1, q] = jnp.where(upper, pltpu.roll(one, SIZE - TILES // 2, 0), two).reshape(strips)


def unpack_planes(packed, q):
    upper = lax.rem(lax.broadcasted_iota(jnp.int32, (SIZE, SIZE), 0), TILES) < TILES // 2
    one, two = (packed[:, h, q].reshape(SIZE, SIZE) for h in range(2))
    return (jnp.where(upper, one, pltpu.roll(two, TILES // 2, 0)),
            jnp.where(upper, pltpu.roll(one, SIZE - TILES // 2, 0), two))


def pack_sums(packed, sums, overlap, a11, b1):
    turn = lax.rem(lax.broadcasted_iota(jnp.int32, (SIZE, SIZE), 0), TILES // 2)
    numbers = jnp.where(turn == 0, a11, jnp.where(turn == 1, b1, 0.0))
    pack_planes(packed, [sums[k] for k in range(5)] + [numbers] + list(overlap))


def wide_merge_kernel(edges, offsets, left, right, from_left, from_right, cover, padded, sums,
                      packed, direction, product):
    limits = bounds(edges)
    a11 = jnp.zeros((1, SIZE), F32)
    b1 = jnp.zeros((1, SIZE), F32)
    for v in range(2):
        rows = slice(v * SIZE, (v + 1) * SIZE)
        mine_rows = lax.broadcasted_iota(jnp.int32, (SIZE, SIZE), 0) + v * SIZE
        for h in range(2):
            own, other = ((left, from_left), (right, from_right))[h]
            light = cover[h, rows]
            inverse = jnp.where(inside(limits, v * SIZE, h * SIZE), 1.0 / (light + 1.0), 0.0)
            dr, di = ((own[v, c] + other[v, c]) * inverse for c in range(2))
            direction[0, h, rows] = dr
            direction[1, h, rows] = di
            pr, pi = padded[0, h, rows], padded[1, h, rows]
            product[0, h, rows] = dr * pr + di * pi
            product[1, h, rows] = dr * pi - di * pr
            across = lanes() + h * SIZE
            mine = (mine_rows >= HALF) & (mine_rows < HALF + SIZE) & (across >= HALF) & (across < HALF + SIZE)
            power = jnp.where(mine, dr * dr + di * di, 0.0)
            a11 += jnp.sum(power * light, axis=0, keepdims=True)
            b1 += jnp.sum(power * (light + 1.0), axis=0, keepdims=True)
    overlap = [jnp.zeros((SIZE, SIZE), F32)] * 2
    for j in range(COUNT):
        row, col = offsets[0, j, 0] + HALF, offsets[0, j, 1] + HALF
        overlap = [overlap[c] + window(product, (c,), row, col) for c in range(2)]
    pack_sums(packed, sums, overlap, a11, b1)


def fold_kernel(middle, from_above, from_below, tile, left, right):
    low = low_lanes(HALF)
    for k in range(3):
        upper = [middle[k, h, :HALF] + from_above[k, h] for h in range(2)]
        lower = [middle[k, h, HALF:] + from_below[k, h] for h in range(2)]
        tile[k, :HALF] = join(low, *upper)
        tile[k, HALF:] = join(low, *lower)
        left[k] = pack_low(low, upper[0], lower[0])
        right[k] = pack_high(low, upper[1], lower[1])


def merge_kernel(near, tile, from_left, from_right, padded, sums,
                 packed, direction, product, overlap):
    low = low_lanes(HALF)
    lane = lanes()
    a11 = jnp.zeros((1, SIZE), F32)
    b1 = jnp.zeros((1, SIZE), F32)
    product[...] = jnp.zeros_like(product)
    for v in range(2):
        rows = slice(HALF * v, HALF * (v + 1))
        full = []
        for k in range(3):
            left, right = from_left[k], from_right[k]
            if v == 0:
                right = pltpu.roll(right, HALF, 1)
            else:
                left = pltpu.roll(left, HALF, 1)
            full.append(tile[k, rows] + jnp.where(low, left, right))
        gr, gi, cover = full
        inverse = 1.0 / (cover + 1.0)
        dr = gr * inverse
        di = gi * inverse
        direction[0, rows] = dr
        direction[1, rows] = di
        span = slice(HALF * (v + 1), HALF * (v + 2))
        pr = join(low, padded[0, 0, span], padded[0, 1, span])
        pi = join(low, padded[1, 0, span], padded[1, 1, span])
        inner = slice(SIZE + HALF * v, SIZE + HALF * (v + 1))
        product[0, inner] = dr * pr + di * pi
        product[1, inner] = dr * pi - di * pr
        power = dr * dr + di * di
        a11 += jnp.sum(power * cover, axis=0, keepdims=True)
        b1 += jnp.sum(power * (cover + 1.0), axis=0, keepdims=True)
    overlap[...] = jnp.zeros_like(overlap)

    def body(step, carry):
        total = [0.0, 0.0]
        for g in range(LIST_STEP):
            down, across = near[step * LIST_STEP + g, 0], near[step * LIST_STEP + g, 1]
            turn = lax.rem(2 * SIZE - across, SIZE)
            source = lane + across
            valid = (source >= 0) & (source < SIZE)
            for c in range(2):
                moved = pltpu.roll(product[c, pl.ds(SIZE + down, SIZE)], turn, 1)
                total[c] = total[c] + jnp.where(valid, moved, 0.0)
        for c in range(2):
            overlap[c] += total[c]
        return carry

    lax.fori_loop(0, lax.div(near[LIST_SIZE - 1, 0] + LIST_STEP - 1, LIST_STEP), body, 0)

    pack_sums(packed, sums, (overlap[0], overlap[1]), a11, b1)


def add_all(parts):
    total = parts[0]
    for k in range(1, parts.shape[0]):
        total = total + parts[k]
    return total


def reduce_kernel(parts, out):
    total = add_all(parts)
    for k in range(out.shape[0]):
        out[k] = total


def strip_kernel(place_ref, parts, probe, out):
    total = add_all(parts)
    line = lax.broadcasted_iota(jnp.int32, (TILES, SIZE), 0)
    half = TILES // 2
    upper = line < half
    first = place_ref[1] == 0
    rows = pl.ds(pl.multiple_of(place_ref[0] * TILES, TILES), TILES)

    def turned(x):
        return pltpu.roll(x, half, 0)

    def both(x, of_upper):
        return jnp.where(upper == of_upper, x, turned(x))

    def modes(c):
        one, two = probe[c, 0, rows], probe[c, 1, rows]
        return jnp.where(upper, jnp.where(first, one, turned(one)), jnp.where(first, turned(two), two))

    pr, pi = modes(0), modes(1)
    cover = both(total[2], True)
    inverse = 1.0 / (cover + 1.0)
    dr, di = total[0] * inverse, total[1] * inverse
    cross = (pr * dr + pi * di) * both(total[3], True) - (pr * di - pi * dr) * both(total[3], False)
    power = dr * dr + di * di
    a22, b2, a12 = (
        jnp.sum(x, axis=0, keepdims=True) for x in (power * cover, power * (cover + 1.0), cross))
    a11, b1 = total[2, half : half + 1], total[2, half + 1 : half + 2]
    low = low_lanes(1)
    known = jnp.where(low, a11 + pltpu.roll(a11, HALF, 1), b1 + pltpu.roll(b1, HALF, 1))
    numbers = total[2]
    for k, term in enumerate((known, a22, b2, a12)):
        numbers = jnp.where(line == half + k, term, numbers)
    for k in range(out.shape[0]):
        out[k, 0] = total[0]
        out[k, 1] = total[1]
        out[k, 2] = numbers


def step_sizes(totals, probe, new_probe, gradient=None):
    numbers = jnp.zeros((TILES, SIZE), F32)
    for k in range(totals.shape[0]):
        numbers += totals[k, 0, 2] + totals[k, 1, 2]
    half = TILES // 2
    low = low_lanes(1)
    known, *rest = (numbers[half + k : half + k + 1] for k in range(4))
    a22, b2, a12 = (jnp.sum(x, axis=1, keepdims=True) for x in rest)
    share = 1.0 / (2 * totals.shape[0])
    a11 = jnp.sum(jnp.where(low, known, 0.0), axis=1, keepdims=True) * share
    b1 = jnp.sum(jnp.where(low, 0.0, known), axis=1, keepdims=True) * share
    a11 = 1.1 * a11
    a22 = 1.1 * a22
    det = a11 * a22 - a12 * a12
    step_obj = (b1 * a22 - a12 * b2) / det
    step_probe = (a11 * b2 - a12 * b1) / det
    cover, _ = unpack_planes(totals, 2)
    cover = cover + 1.0
    scale = step_probe / cover
    for c in range(2):
        for m, numer in enumerate(unpack_planes(totals, c)):
            new_probe[c, m] = probe[c, m] + scale * numer
            if gradient is not None:
                gradient[c, m] = numer * lax.rsqrt(cover)
    return step_obj


def next_kernel(offsets, totals, padded, direction, probe, measured, right3, left3,
                top, middle, bottom, sums, new_padded, new_probe, accum):
    step = step_sizes(totals, probe, new_probe)
    new_padded[...] = padded[...] + step * direction[...]
    sweep(1, offsets, new_padded, new_probe, measured, right3, left3, sums, accum)
    top[...] = accum[:, :, :HALF]
    middle[...] = accum[:, :, HALF : HALF + SIZE]
    bottom[...] = accum[:, :, HALF + SIZE :]


def last_kernel(totals, padded, direction, probe, new_obj, new_probe, gradient):
    step = step_sizes(totals, probe, new_probe, gradient)
    low = lanes() < HALF
    rows = slice(HALF, HALF + SIZE)
    for c in range(2):
        old = join(low, padded[c, 0, rows], padded[c, 1, rows])
        new_obj[c] = old + step * direction[c]


def shape(*dims):
    return jax.ShapeDtypeStruct(dims, F32)


def call(kernel, ins, outs, scratch=()):
    vmem = pl.BlockSpec(memory_space=pltpu.VMEM)
    smem = pl.BlockSpec(memory_space=pltpu.SMEM)
    specs = [smem if x.dtype == jnp.int32 else vmem for x in ins]
    return pl.pallas_call(
        kernel,
        in_specs=specs,
        out_specs=[smem if x.dtype == jnp.int32 else vmem for x in outs],
        out_shape=list(outs),
        scratch_shapes=list(scratch),
        compiler_params=pltpu.CompilerParams(vmem_limit_bytes=VMEM_LIMIT),
        name=getattr(kernel, "func", kernel).__name__,
    )(*ins)


def shift(block, rows, cols):
    n_row = math.prod(lax.axis_size(a) for a in ROW)
    n_col = math.prod(lax.axis_size(a) for a in COL)
    route = [
        (r * n_col + c, (r + rows) * n_col + c + cols)
        for r in range(n_row)
        for c in range(n_col)
        if 0 <= r + rows < n_row and 0 <= c + cols < n_col
    ]
    return lax.ppermute(block, ALL, route)


def exchange(block, axes):
    return lax.all_to_all(block, axes, 0, 0, tiled=True)


def size_of(axes):
    return math.prod(lax.axis_size(a) for a in axes)


def reduce_all(packed, probe, place_in_group):
    group, rest = size_of(SCATTER), size_of(REST)
    part = exchange(packed.reshape(group, 4, TILES, SIZE), SCATTER)
    (part,) = call(reduce_kernel, [part], [shape(rest, 4, TILES, SIZE)])
    part = exchange(part, REST)
    (part,) = call(strip_kernel, [place_in_group, part, probe], [shape(group, 3, TILES, SIZE)])
    return exchange(part, SCATTER).reshape(SIZE // TILES, 2, 3, TILES, SIZE)


def per_device(obj, probe, measured, offsets):
    right3, left3 = (jnp.asarray(t) for t in dft_tables())
    offsets = offsets[0, 0]
    r, c, half = (lax.axis_index(axes).astype(jnp.int32) for axes in (ROW, COL, ("zl",)))
    whole = 2 * SIZE
    place_in_group = jnp.stack([r, half])
    edges = jnp.stack([
        jnp.where(r == 0, HALF, 0),
        jnp.where(r == size_of(ROW) - 1, whole - HALF, whole),
        jnp.where(c == 0, HALF, 0),
        jnp.where(c == size_of(COL) - 1, whole - HALF, whole),
    ]).astype(jnp.int32)

    strip = shape(2, HALF + TILES, SIZE)
    side = shape(2, SIZE + TILES, SIZE)
    to_below, to_above = call(send_kernel, [offsets, obj], [strip, strip])
    above = shift(to_below, 1, 0)
    below = shift(to_above, -1, 0)
    to_left, to_right, codes = call(
        pack_kernel, [above, obj, below, to_below], [side, side, shape(TILES, SIZE)])
    from_left = shift(to_right, 0, 1)
    from_right = shift(to_left, 0, -1)
    others = jnp.concatenate([from_left[0, SIZE:], codes, from_right[0, SIZE:]], axis=0).astype(jnp.int32)

    field = shape(2, 2, whole, SIZE)
    edge = shape(3, 2, HALF, SIZE)
    quads = shape(2, 2, SIZE, SIZE)
    planes = shape(2, MODES, SIZE, SIZE)
    sums_shape = shape(5, SIZE, SIZE)
    packed_shape = shape(SIZE // TILES, 2, 4, TILES, SIZE)

    top, bottom, sums, padded = call(
        first_kernel,
        [offsets, above, obj, below, from_left, from_right, probe, measured, right3, left3],
        [quads, quads, sums_shape, field],
        [pltpu.VMEM((2, 2, whole, SIZE), F32)],
    )
    from_above = shift(bottom, 1, 0)
    from_below = shift(top, -1, 0)
    cover, near = call(
        cover_kernel, [others, probe],
        [shape(2, whole, SIZE), jax.ShapeDtypeStruct((LIST_SIZE, 2), jnp.int32)],
        [pltpu.VMEM((3 * SIZE, SIZE), F32)])
    left, right = call(wide_fold_kernel, [top, bottom, from_above, from_below], [quads, quads])
    from_left = shift(right, 0, 1)
    from_right = shift(left, 0, -1)
    packed, direction = call(
        wide_merge_kernel,
        [edges, offsets, left, right, from_left, from_right, cover, padded, sums],
        [packed_shape, field],
        [pltpu.VMEM((2, 2, whole, SIZE), F32)],
    )
    totals = reduce_all(packed, probe, place_in_group)

    top, middle, bottom, sums, padded, probe = call(
        next_kernel,
        [offsets, totals, padded, direction, probe, measured, right3, left3],
        [edge, shape(3, 2, SIZE, SIZE), edge, sums_shape, field, planes],
        [pltpu.VMEM((3, 2, whole, SIZE), F32)],
    )
    from_above = shift(bottom, 1, 0)
    from_below = shift(top, -1, 0)
    side = shape(3, HALF, SIZE)
    tile, left, right = call(
        fold_kernel, [middle, from_above, from_below], [shape(3, SIZE, SIZE), side, side])
    from_left = shift(right, 0, 1)
    from_right = shift(left, 0, -1)
    packed, direction = call(
        merge_kernel,
        [near, tile, from_left, from_right, padded, sums],
        [packed_shape, shape(2, SIZE, SIZE)],
        [pltpu.VMEM((2, 3 * SIZE, SIZE), F32), pltpu.VMEM((2, SIZE, SIZE), F32)],
    )
    totals = reduce_all(packed, probe, place_in_group)
    return tuple(call(
        last_kernel, [totals, padded, direction, probe], [shape(2, SIZE, SIZE), planes, planes]
    ))


def solution(mesh):
    parts = Mesh(mesh.devices.reshape(2, 4, 2, 4, 4, 2), ALL)
    in_specs = (P(None, ROW, COL), P(), P(ROW, COL), P(ROW, COL))
    out_specs = (P(None, ROW, COL), P(), P())
    return jax.shard_map(
        per_device, mesh=parts, in_specs=in_specs, out_specs=out_specs, check_vma=False
    )
```

```python
import math
from functools import partial

import jax
import jax.numpy as jnp
import numpy as np
from jax import lax
from jax.experimental import pallas as pl
from jax.experimental.pallas import tpu as pltpu
from jax.sharding import Mesh, PartitionSpec as P

SIZE = 128
HALF = 64
MODES = 2
COUNT = 8
ROW = ("yl", "x", "c")
COL = ("yh", "zh", "zl")
ALL = ROW + COL
SCATTER = ROW + ("zl",)
REST = ("zh", "yh")
MARK = 1024
LIST_STEP = 4
LIST_SIZE = 9 * COUNT + 8
TILES = 8
VMEM_LIMIT = 16 * 1024 * 1024
F32 = jnp.float32
BF16 = jnp.bfloat16


def dft_tables():
    index = np.arange(SIZE)
    angle = 2.0 * math.pi / SIZE * (np.outer(index, index) % SIZE)
    real = np.cos(angle) / math.sqrt(SIZE)
    imag = -np.sin(angle) / math.sqrt(SIZE)
    right = np.block([[real, imag], [-imag, real]]).astype(np.float32)
    high = right.astype(jnp.bfloat16)
    low = (right - high.astype(np.float32)).astype(jnp.bfloat16)
    right3 = np.concatenate([high, high, low], axis=0)
    left3 = np.ascontiguousarray(right3.T)
    return right3, left3


def halves(x):
    high = x.astype(BF16)
    return high, (x - high.astype(F32)).astype(BF16)


def right_transform(fields, table):
    rows = []
    for real, imag in fields:
        rh, rl = halves(real)
        ih, il = halves(imag)
        rows.append(jnp.concatenate([rh, ih, rl, il, rh, ih], axis=1))
    out = jnp.dot(jnp.concatenate(rows, axis=0), table, preferred_element_type=F32)
    return [
        (out[SIZE * n : SIZE * (n + 1), :SIZE], out[SIZE * n : SIZE * (n + 1), SIZE:])
        for n in range(len(fields))
    ]


def left_transform(fields, table):
    cols = []
    for real, imag in fields:
        rh, rl = halves(real)
        ih, il = halves(imag)
        cols.append(jnp.concatenate([rh, ih, rl, il, rh, ih], axis=0))
    out = jnp.dot(table, jnp.concatenate(cols, axis=1), preferred_element_type=F32)
    return [
        (out[:SIZE, SIZE * n : SIZE * (n + 1)], out[SIZE:, SIZE * n : SIZE * (n + 1)])
        for n in range(len(fields))
    ]


def lanes():
    return lax.broadcasted_iota(jnp.int32, (SIZE, SIZE), 1)


def window(ref, lead, row, col):
    shift = lax.rem(SIZE - col, SIZE)
    rows = pl.ds(row, SIZE)
    mixed = jnp.where(lanes() >= col, ref[lead + (0, rows)], ref[lead + (1, rows)])
    return pltpu.roll(mixed, shift, 1)


def place(ref, plane, row, col, block):
    moved = pltpu.roll(block, lax.rem(col, SIZE), 1)
    first = lanes() >= col
    rows = pl.ds(row, SIZE)
    ref[plane, 0, rows] += jnp.where(first, moved, 0.0)
    ref[plane, 1, rows] += jnp.where(first, 0.0, moved)


def join(low, first, second):
    return jnp.where(low, pltpu.roll(first, HALF, 1), pltpu.roll(second, HALF, 1))


def pack_low(low, upper, lower):
    return jnp.where(low, upper, pltpu.roll(lower, HALF, 1))


def pack_high(low, upper, lower):
    return jnp.where(low, pltpu.roll(upper, HALF, 1), lower)


def low_lanes(rows):
    return lax.broadcasted_iota(jnp.int32, (rows, SIZE), 1) < HALF


def bounds(edges):
    return tuple(edges[k] for k in range(4))


def inside(limits, down, across, rows=SIZE):
    row_low, row_high, col_low, col_high = limits
    line = lax.broadcasted_iota(jnp.int32, (rows, SIZE), 0) + down
    lane = lax.broadcasted_iota(jnp.int32, (rows, SIZE), 1) + across
    return (line >= row_low) & (line < row_high) & (lane >= col_low) & (lane < col_high)


def pad_field(above, own, below, from_left, from_right, store):
    low = low_lanes(HALF)
    for c in range(2):
        strips = (above[c, :HALF], own[c, :HALF], own[c, HALF:], below[c, :HALF])
        for k in range(4):
            half = slice(HALF * (k % 2), HALF * (k % 2 + 1))
            left, right = from_left[c, half], from_right[c, half]
            if k < 2:
                right = pltpu.roll(right, HALF, 1)
            else:
                left = pltpu.roll(left, HALF, 1)
            mine = pltpu.roll(strips[k], HALF, 1)
            rows = slice(HALF * k, HALF * (k + 1))
            store(c, 0, rows, jnp.where(low, left, mine))
            store(c, 1, rows, jnp.where(low, mine, right))


def send_kernel(offsets, own, tile, to_below, to_above, sems):
    strip = pl.ds(0, HALF)
    copies = [
        pltpu.make_async_copy(source, target, sems.at[k])
        for k, (source, target) in enumerate((
            (own.at[:, pl.ds(HALF, HALF)], to_below.at[:, strip]),
            (own.at[:, strip], to_above.at[:, strip]),
            (own, tile),
        ))
    ]
    for copy in copies:
        copy.start()
    line = lax.broadcasted_iota(jnp.int32, (TILES, SIZE), 0)
    lane = lax.broadcasted_iota(jnp.int32, (TILES, SIZE), 1)
    code = jnp.zeros((TILES, SIZE), jnp.int32)
    batches, _, count = offsets.shape
    for b in range(batches):
        for k in range(count):
            for d in range(2):
                code = jnp.where(lane == (b * 2 + d) * count + k, offsets[b, d, k] + MARK, code)
    code = jnp.where(line == 0, code, 0).astype(F32)
    for c in range(2):
        to_below[c, HALF:] = code
        to_above[c, HALF:] = code
    for copy in copies:
        copy.wait()


def pack_kernel(above, own, below, mine, to_left, to_right, codes):
    low = low_lanes(HALF)
    for c in range(2):
        strips = (above[c, :HALF], own[c, :HALF], own[c, HALF:], below[c, :HALF])
        for k in range(2):
            rows = slice(HALF * k, HALF * (k + 1))
            to_left[c, rows] = pack_low(low, strips[k], strips[k + 2])
            to_right[c, rows] = pack_high(low, strips[k], strips[k + 2])
    code = mine[0, HALF:] + pltpu.roll(above[0, HALF:], 1, 0) + pltpu.roll(below[0, HALF:], 2, 0)
    for c in range(2):
        to_left[c, SIZE:] = code
        to_right[c, SIZE:] = code
    codes[...] = code


def power_of(probe):
    return sum(probe[c, m] * probe[c, m] for c in range(2) for m in range(MODES))


class Staged:
    def __init__(self, batch, measured, right3, left3, places, sems):
        sources = (right3, left3, measured.at[0, 0, batch])
        self.places = places
        self.copies = [pltpu.make_async_copy(a, b, sems.at[k]) for k, (a, b) in enumerate(zip(sources, places))]
        for copy in self.copies:
            copy.start()

    def take(self, k):
        self.copies[k].wait()
        return self.places[k]


def staging():
    return [
        pltpu.VMEM((6 * SIZE, 2 * SIZE), BF16),
        pltpu.VMEM((2 * SIZE, 6 * SIZE), BF16),
        pltpu.VMEM((COUNT, SIZE, SIZE), F32),
        pltpu.SemaphoreType.DMA((3,)),
    ]


def sweep(batch, offsets, padded, probe, staged, sums, accum):
    accum[...] = jnp.zeros_like(accum)
    wins = []
    fields = []
    for j in range(COUNT):
        row, col = offsets[batch, 0, j] + HALF, offsets[batch, 1, j] + HALF
        wr = window(padded, (0,), row, col)
        wi = window(padded, (1,), row, col)
        wins.append((row, col, wr, wi))
        for m in range(MODES):
            pr, pi = probe[0, m], probe[1, m]
            fields.append((pr * wr - pi * wi, pr * wi + pi * wr))
    tr = staged.take(0)[...]
    waves = right_transform(fields, tr)
    tl = staged.take(1)[...]
    waves = left_transform(waves, tl)
    measured = staged.take(2)
    back = []
    for j in range(COUNT):
        own = waves[j * MODES : (j + 1) * MODES]
        intensity = sum(r * r + i * i for r, i in own)
        ratio = jnp.sqrt(measured[j]) / jnp.maximum(jnp.sqrt(intensity), 0.5) - 1.0
        back += [(r * ratio, -(i * ratio)) for r, i in own]
    chis = right_transform(left_transform(back, tl), tr)
    light = power_of(probe) if accum.shape[0] == 3 else None
    totals = [0.0] * 5
    for j in range(COUNT):
        row, col, wr, wi = wins[j]
        cr = jnp.zeros((SIZE, SIZE), F32)
        ci = jnp.zeros((SIZE, SIZE), F32)
        for m in range(MODES):
            xr, xn = chis[j * MODES + m]
            pr, pi = probe[0, m], probe[1, m]
            cr += pr * xr - pi * xn
            ci -= pr * xn + pi * xr
            totals[m] = totals[m] + (wr * xr - wi * xn)
            totals[MODES + m] = totals[MODES + m] - (wr * xn + wi * xr)
        totals[2 * MODES] = totals[2 * MODES] + (wr * wr + wi * wi)
        place(accum, 0, row, col, cr)
        place(accum, 1, row, col, ci)
        if light is not None:
            place(accum, 2, row, col, light)
    for k in range(5):
        sums[k] = totals[k]


def first_kernel(offsets, above, own, below, from_left, from_right, probe, measured, right3, left3,
                 top, bottom, sums, padded, accum, *stage):
    staged = Staged(0, measured, right3, left3, stage[:3], stage[3])

    def store(c, h, rows, value):
        padded[c, h, rows] = value

    pad_field(above, own, below, from_left, from_right, store)
    sweep(0, offsets, padded, probe, staged, sums, accum)
    top[...] = accum[:, :, :SIZE]
    bottom[...] = accum[:, :, SIZE:]


def offset_of(others, batch, across, down, j, d):
    return others[TILES * across + (1, 0, 2)[down], (batch * 2 + d) * COUNT + j] - MARK


def cover_kernel(others, probe, cover, near, light):
    none = jnp.zeros((SIZE, SIZE), F32)
    light[:SIZE] = none
    light[SIZE : 2 * SIZE] = power_of(probe)
    light[2 * SIZE :] = none
    lane = lanes()
    for v in range(2):
        total = [none, none]
        for down in (v, v + 1):
            for across in range(3):
                for j in range(COUNT):
                    row, col = (offset_of(others, 0, across, down, j, d) + HALF for d in range(2))
                    row = jnp.clip(row + SIZE * (down - 1 - v), -SIZE, SIZE)
                    col = jnp.clip(col, 0, SIZE)
                    moved = pltpu.roll(light[pl.ds(SIZE - row, SIZE)], lax.rem(col, SIZE), 1)
                    first = lane >= col
                    if across >= 1:
                        total[across - 1] = total[across - 1] + jnp.where(first, moved, 0.0)
                    if across <= 1:
                        total[across] = total[across] + jnp.where(first, 0.0, moved)
        for h in range(2):
            cover[h, v * SIZE : (v + 1) * SIZE] = total[h]

    count = jnp.int32(0)
    for down in range(3):
        for across in range(3):
            for j in range(COUNT):
                row = offset_of(others, 1, across, down, j, 0) + SIZE * (down - 1)
                col = offset_of(others, 1, across, down, j, 1) + SIZE * (across - 1)
                near[count, 0] = row
                near[count, 1] = col
                reaches = (jnp.abs(row) < SIZE) & (jnp.abs(col) < SIZE)
                count += reaches.astype(jnp.int32)
    for k in range(LIST_STEP):
        near[count + k, 0] = SIZE
        near[count + k, 1] = 0
    near[LIST_SIZE - 1, 0] = count


def wide_fold_kernel(top, bottom, from_above, from_below, left, right):
    for v, own, other in ((0, top, from_above), (1, bottom, from_below)):
        left[v] = own[:, 0] + other[:, 0]
        right[v] = own[:, 1] + other[:, 1]


def pack_planes(packed, planes):
    strips = (SIZE // TILES, TILES, SIZE)
    upper = lax.rem(lax.broadcasted_iota(jnp.int32, (SIZE, SIZE), 0), TILES) < TILES // 2
    for q in range(len(planes) // 2):
        one, two = planes[2 * q], planes[2 * q + 1]
        packed[:, 0, q] = jnp.where(upper, one, pltpu.roll(two, TILES // 2, 0)).reshape(strips)
        packed[:, 1, q] = jnp.where(upper, pltpu.roll(one, SIZE - TILES // 2, 0), two).reshape(strips)


def unpack_planes(packed, q):
    upper = lax.rem(lax.broadcasted_iota(jnp.int32, (SIZE, SIZE), 0), TILES) < TILES // 2
    one, two = (packed[:, h, q].reshape(SIZE, SIZE) for h in range(2))
    return (jnp.where(upper, one, pltpu.roll(two, TILES // 2, 0)),
            jnp.where(upper, pltpu.roll(one, SIZE - TILES // 2, 0), two))


def pack_sums(packed, sums, overlap, a11, b1):
    turn = lax.rem(lax.broadcasted_iota(jnp.int32, (SIZE, SIZE), 0), TILES // 2)
    numbers = jnp.where(turn == 0, a11, jnp.where(turn == 1, b1, 0.0))
    pack_planes(packed, [sums[k] for k in range(5)] + [numbers] + list(overlap))


def wide_merge_kernel(edges, offsets, left, right, from_left, from_right, cover, padded, sums,
                      packed, direction, product):
    limits = bounds(edges)
    a11 = jnp.zeros((1, SIZE), F32)
    b1 = jnp.zeros((1, SIZE), F32)
    for v in range(2):
        rows = slice(v * SIZE, (v + 1) * SIZE)
        mine_rows = lax.broadcasted_iota(jnp.int32, (SIZE, SIZE), 0) + v * SIZE
        for h in range(2):
            own, other = ((left, from_left), (right, from_right))[h]
            light = cover[h, rows]
            inverse = jnp.where(inside(limits, v * SIZE, h * SIZE), 1.0 / (light + 1.0), 0.0)
            dr, di = ((own[v, c] + other[v, c]) * inverse for c in range(2))
            direction[0, h, rows] = dr
            direction[1, h, rows] = di
            pr, pi = padded[0, h, rows], padded[1, h, rows]
            product[0, h, rows] = dr * pr + di * pi
            product[1, h, rows] = dr * pi - di * pr
            across = lanes() + h * SIZE
            mine = (mine_rows >= HALF) & (mine_rows < HALF + SIZE) & (across >= HALF) & (across < HALF + SIZE)
            power = jnp.where(mine, dr * dr + di * di, 0.0)
            a11 += jnp.sum(power * light, axis=0, keepdims=True)
            b1 += jnp.sum(power * (light + 1.0), axis=0, keepdims=True)
    overlap = [jnp.zeros((SIZE, SIZE), F32)] * 2
    for j in range(COUNT):
        row, col = offsets[0, 0, j] + HALF, offsets[0, 1, j] + HALF
        overlap = [overlap[c] + window(product, (c,), row, col) for c in range(2)]
    pack_sums(packed, sums, overlap, a11, b1)


def fold_kernel(middle, from_above, from_below, tile, left, right):
    low = low_lanes(HALF)
    for k in range(3):
        upper = [middle[k, h, :HALF] + from_above[k, h] for h in range(2)]
        lower = [middle[k, h, HALF:] + from_below[k, h] for h in range(2)]
        tile[k, :HALF] = join(low, *upper)
        tile[k, HALF:] = join(low, *lower)
        left[k] = pack_low(low, upper[0], lower[0])
        right[k] = pack_high(low, upper[1], lower[1])


def merge_kernel(near, tile, from_left, from_right, padded, sums,
                 packed, direction, product, overlap):
    low = low_lanes(HALF)
    lane = lanes()
    a11 = jnp.zeros((1, SIZE), F32)
    b1 = jnp.zeros((1, SIZE), F32)
    product[...] = jnp.zeros_like(product)
    for v in range(2):
        rows = slice(HALF * v, HALF * (v + 1))
        full = []
        for k in range(3):
            left, right = from_left[k], from_right[k]
            if v == 0:
                right = pltpu.roll(right, HALF, 1)
            else:
                left = pltpu.roll(left, HALF, 1)
            full.append(tile[k, rows] + jnp.where(low, left, right))
        gr, gi, cover = full
        inverse = 1.0 / (cover + 1.0)
        dr = gr * inverse
        di = gi * inverse
        direction[0, rows] = dr
        direction[1, rows] = di
        span = slice(HALF * (v + 1), HALF * (v + 2))
        pr = join(low, padded[0, 0, span], padded[0, 1, span])
        pi = join(low, padded[1, 0, span], padded[1, 1, span])
        inner = slice(SIZE + HALF * v, SIZE + HALF * (v + 1))
        product[0, inner] = dr * pr + di * pi
        product[1, inner] = dr * pi - di * pr
        power = dr * dr + di * di
        a11 += jnp.sum(power * cover, axis=0, keepdims=True)
        b1 += jnp.sum(power * (cover + 1.0), axis=0, keepdims=True)
    overlap[...] = jnp.zeros_like(overlap)

    def body(step, carry):
        total = [0.0, 0.0]
        for g in range(LIST_STEP):
            down, across = near[step * LIST_STEP + g, 0], near[step * LIST_STEP + g, 1]
            turn = lax.rem(2 * SIZE - across, SIZE)
            source = lane + across
            valid = (source >= 0) & (source < SIZE)
            for c in range(2):
                moved = pltpu.roll(product[c, pl.ds(SIZE + down, SIZE)], turn, 1)
                total[c] = total[c] + jnp.where(valid, moved, 0.0)
        for c in range(2):
            overlap[c] += total[c]
        return carry

    lax.fori_loop(0, lax.div(near[LIST_SIZE - 1, 0] + LIST_STEP - 1, LIST_STEP), body, 0)

    pack_sums(packed, sums, (overlap[0], overlap[1]), a11, b1)


def add_all(parts):
    total = parts[0]
    for k in range(1, parts.shape[0]):
        total = total + parts[k]
    return total


def reduce_kernel(parts, out):
    total = add_all(parts)
    for k in range(out.shape[0]):
        out[k] = total


def strip_kernel(place_ref, parts, probe, out):
    total = add_all(parts)
    line = lax.broadcasted_iota(jnp.int32, (TILES, SIZE), 0)
    half = TILES // 2
    upper = line < half
    first = place_ref[1] == 0
    rows = pl.ds(pl.multiple_of(place_ref[0] * TILES, TILES), TILES)

    def turned(x):
        return pltpu.roll(x, half, 0)

    def both(x, of_upper):
        return jnp.where(upper == of_upper, x, turned(x))

    def modes(c):
        one, two = probe[c, 0, rows], probe[c, 1, rows]
        return jnp.where(upper, jnp.where(first, one, turned(one)), jnp.where(first, turned(two), two))

    pr, pi = modes(0), modes(1)
    cover = both(total[2], True)
    inverse = 1.0 / (cover + 1.0)
    dr, di = total[0] * inverse, total[1] * inverse
    cross = (pr * dr + pi * di) * both(total[3], True) - (pr * di - pi * dr) * both(total[3], False)
    power = dr * dr + di * di
    a22, b2, a12 = (
        jnp.sum(x, axis=0, keepdims=True) for x in (power * cover, power * (cover + 1.0), cross))
    a11, b1 = total[2, half : half + 1], total[2, half + 1 : half + 2]
    low = low_lanes(1)
    known = jnp.where(low, a11 + pltpu.roll(a11, HALF, 1), b1 + pltpu.roll(b1, HALF, 1))
    numbers = total[2]
    for k, term in enumerate((known, a22, b2, a12)):
        numbers = jnp.where(line == half + k, term, numbers)
    for k in range(out.shape[0]):
        out[k, 0] = total[0]
        out[k, 1] = total[1]
        out[k, 2] = numbers


def step_sizes(totals, probe, new_probe, gradient=None):
    numbers = jnp.zeros((TILES, SIZE), F32)
    for k in range(totals.shape[0]):
        numbers += totals[k, 0, 2] + totals[k, 1, 2]
    half = TILES // 2
    low = low_lanes(1)
    known, *rest = (numbers[half + k : half + k + 1] for k in range(4))
    a22, b2, a12 = (jnp.sum(x, axis=1, keepdims=True) for x in rest)
    share = 1.0 / (2 * totals.shape[0])
    a11 = jnp.sum(jnp.where(low, known, 0.0), axis=1, keepdims=True) * share
    b1 = jnp.sum(jnp.where(low, 0.0, known), axis=1, keepdims=True) * share
    a11 = 1.1 * a11
    a22 = 1.1 * a22
    det = a11 * a22 - a12 * a12
    step_obj = (b1 * a22 - a12 * b2) / det
    step_probe = (a11 * b2 - a12 * b1) / det
    cover, _ = unpack_planes(totals, 2)
    cover = cover + 1.0
    scale = step_probe / cover
    for c in range(2):
        for m, numer in enumerate(unpack_planes(totals, c)):
            new_probe[c, m] = probe[c, m] + scale * numer
            if gradient is not None:
                gradient[c, m] = numer * lax.rsqrt(cover)
    return step_obj


def next_kernel(offsets, totals, padded, direction, probe, measured, right3, left3,
                top, middle, bottom, sums, new_padded, new_probe, accum, *stage):
    staged = Staged(1, measured, right3, left3, stage[:3], stage[3])
    step = step_sizes(totals, probe, new_probe)
    new_padded[...] = padded[...] + step * direction[...]
    sweep(1, offsets, new_padded, new_probe, staged, sums, accum)
    top[...] = accum[:, :, :HALF]
    middle[...] = accum[:, :, HALF : HALF + SIZE]
    bottom[...] = accum[:, :, HALF + SIZE :]


def last_kernel(totals, padded, direction, probe, new_obj, new_probe, gradient):
    step = step_sizes(totals, probe, new_probe, gradient)
    low = lanes() < HALF
    rows = slice(HALF, HALF + SIZE)
    for c in range(2):
        old = join(low, padded[c, 0, rows], padded[c, 1, rows])
        new_obj[c] = old + step * direction[c]


def shape(*dims):
    return jax.ShapeDtypeStruct(dims, F32)


def call(kernel, ins, outs, scratch=(), in_hbm=()):
    vmem = pl.BlockSpec(memory_space=pltpu.VMEM)
    smem = pl.BlockSpec(memory_space=pltpu.SMEM)
    hbm = pl.BlockSpec(memory_space=pltpu.HBM)
    ins = [pltpu.with_memory_space_constraint(x, pltpu.HBM) if k in in_hbm else x for k, x in enumerate(ins)]
    specs = [hbm if k in in_hbm else smem if x.dtype == jnp.int32 else vmem for k, x in enumerate(ins)]
    return pl.pallas_call(
        kernel,
        in_specs=specs,
        out_specs=[smem if x.dtype == jnp.int32 else vmem for x in outs],
        out_shape=list(outs),
        scratch_shapes=list(scratch),
        compiler_params=pltpu.CompilerParams(vmem_limit_bytes=VMEM_LIMIT),
        name=getattr(kernel, "func", kernel).__name__,
    )(*ins)


def shift(block, rows, cols):
    n_row = math.prod(lax.axis_size(a) for a in ROW)
    n_col = math.prod(lax.axis_size(a) for a in COL)
    route = [
        (r * n_col + c, (r + rows) * n_col + c + cols)
        for r in range(n_row)
        for c in range(n_col)
        if 0 <= r + rows < n_row and 0 <= c + cols < n_col
    ]
    return lax.ppermute(block, ALL, route)


def exchange(block, axes):
    return lax.all_to_all(block, axes, 0, 0, tiled=True)


def size_of(axes):
    return math.prod(lax.axis_size(a) for a in axes)


def reduce_all(packed, probe, place_in_group):
    group, rest = size_of(SCATTER), size_of(REST)
    part = exchange(packed.reshape(group, 4, TILES, SIZE), SCATTER)
    (part,) = call(reduce_kernel, [part], [shape(rest, 4, TILES, SIZE)])
    part = exchange(part, REST)
    (part,) = call(strip_kernel, [place_in_group, part, probe], [shape(group, 3, TILES, SIZE)])
    return exchange(part, SCATTER).reshape(SIZE // TILES, 2, 3, TILES, SIZE)


def per_device(obj, probe, measured, offsets):
    right3, left3 = (jnp.asarray(t) for t in dft_tables())
    offsets = jnp.swapaxes(offsets[0, 0], 1, 2)
    r, c, half = (lax.axis_index(axes).astype(jnp.int32) for axes in (ROW, COL, ("zl",)))
    whole = 2 * SIZE
    place_in_group = jnp.stack([r, half])
    edges = jnp.stack([
        jnp.where(r == 0, HALF, 0),
        jnp.where(r == size_of(ROW) - 1, whole - HALF, whole),
        jnp.where(c == 0, HALF, 0),
        jnp.where(c == size_of(COL) - 1, whole - HALF, whole),
    ]).astype(jnp.int32)

    strip = shape(2, HALF + TILES, SIZE)
    side = shape(2, SIZE + TILES, SIZE)
    tile, to_below, to_above = call(
        send_kernel, [offsets, obj], [shape(2, SIZE, SIZE), strip, strip],
        [pltpu.SemaphoreType.DMA((3,))], in_hbm=(1,))
    above = shift(to_below, 1, 0)
    below = shift(to_above, -1, 0)
    to_left, to_right, codes = call(
        pack_kernel, [above, tile, below, to_below], [side, side, shape(TILES, SIZE)])
    from_left = shift(to_right, 0, 1)
    from_right = shift(to_left, 0, -1)
    others = jnp.concatenate([from_left[0, SIZE:], codes, from_right[0, SIZE:]], axis=0).astype(jnp.int32)

    field = shape(2, 2, whole, SIZE)
    edge = shape(3, 2, HALF, SIZE)
    quads = shape(2, 2, SIZE, SIZE)
    planes = shape(2, MODES, SIZE, SIZE)
    sums_shape = shape(5, SIZE, SIZE)
    packed_shape = shape(SIZE // TILES, 2, 4, TILES, SIZE)

    top, bottom, sums, padded = call(
        first_kernel,
        [offsets, above, tile, below, from_left, from_right, probe, measured, right3, left3],
        [quads, quads, sums_shape, field],
        [pltpu.VMEM((2, 2, whole, SIZE), F32)] + staging(),
        in_hbm=(7, 8, 9),
    )
    from_above = shift(bottom, 1, 0)
    from_below = shift(top, -1, 0)
    cover, near = call(
        cover_kernel, [others, probe],
        [shape(2, whole, SIZE), jax.ShapeDtypeStruct((LIST_SIZE, 2), jnp.int32)],
        [pltpu.VMEM((3 * SIZE, SIZE), F32)])
    left, right = call(wide_fold_kernel, [top, bottom, from_above, from_below], [quads, quads])
    from_left = shift(right, 0, 1)
    from_right = shift(left, 0, -1)
    packed, direction = call(
        wide_merge_kernel,
        [edges, offsets, left, right, from_left, from_right, cover, padded, sums],
        [packed_shape, field],
        [pltpu.VMEM((2, 2, whole, SIZE), F32)],
    )
    totals = reduce_all(packed, probe, place_in_group)

    top, middle, bottom, sums, padded, probe = call(
        next_kernel,
        [offsets, totals, padded, direction, probe, measured, right3, left3],
        [edge, shape(3, 2, SIZE, SIZE), edge, sums_shape, field, planes],
        [pltpu.VMEM((3, 2, whole, SIZE), F32)] + staging(),
        in_hbm=(5, 6, 7),
    )
    from_above = shift(bottom, 1, 0)
    from_below = shift(top, -1, 0)
    side = shape(3, HALF, SIZE)
    middle, left, right = call(
        fold_kernel, [middle, from_above, from_below], [shape(3, SIZE, SIZE), side, side])
    from_left = shift(right, 0, 1)
    from_right = shift(left, 0, -1)
    packed, direction = call(
        merge_kernel,
        [near, middle, from_left, from_right, padded, sums],
        [packed_shape, shape(2, SIZE, SIZE)],
        [pltpu.VMEM((2, 3 * SIZE, SIZE), F32), pltpu.VMEM((2, SIZE, SIZE), F32)],
    )
    totals = reduce_all(packed, probe, place_in_group)
    return tuple(call(
        last_kernel, [totals, padded, direction, probe], [shape(2, SIZE, SIZE), planes, planes]
    ))


def solution(mesh):
    parts = Mesh(mesh.devices.reshape(2, 4, 2, 4, 4, 2), ALL)
    in_specs = (P(None, ROW, COL), P(), P(ROW, COL), P(ROW, COL))
    out_specs = (P(None, ROW, COL), P(), P())
    return jax.shard_map(
        per_device, mesh=parts, in_specs=in_specs, out_specs=out_specs, check_vma=False
    )
```

```python
import math
from functools import partial

import jax
import jax.numpy as jnp
import numpy as np
from jax import lax
from jax.experimental import pallas as pl
from jax.experimental.pallas import tpu as pltpu
from jax.sharding import Mesh, PartitionSpec as P

SIZE = 128
HALF = 64
MODES = 2
COUNT = 8
ROW = ("yl", "x", "c")
COL = ("yh", "zh", "zl")
ALL = ROW + COL
SCATTER = ROW + ("zl",)
REST = ("zh", "yh")
MARK = 1024
LIST_STEP = 4
LIST_SIZE = 9 * COUNT + 8
TILES = 8
VMEM_LIMIT = 16 * 1024 * 1024
F32 = jnp.float32
BF16 = jnp.bfloat16


def dft_tables():
    index = np.arange(SIZE)
    angle = 2.0 * math.pi / SIZE * (np.outer(index, index) % SIZE)
    real = np.cos(angle) / math.sqrt(SIZE)
    imag = -np.sin(angle) / math.sqrt(SIZE)
    right = np.block([[real, imag], [-imag, real]]).astype(np.float32)
    high = right.astype(jnp.bfloat16)
    low = (right - high.astype(np.float32)).astype(jnp.bfloat16)
    right3 = np.concatenate([high, high, low], axis=0)
    left3 = np.ascontiguousarray(right3.T)
    return right3, left3


def halves(x):
    high = x.astype(BF16)
    return high, (x - high.astype(F32)).astype(BF16)


def right_transform(fields, table):
    rows = []
    for real, imag in fields:
        rh, rl = halves(real)
        ih, il = halves(imag)
        rows.append(jnp.concatenate([rh, ih, rl, il, rh, ih], axis=1))
    out = jnp.dot(jnp.concatenate(rows, axis=0), table, preferred_element_type=F32)
    return [
        (out[SIZE * n : SIZE * (n + 1), :SIZE], out[SIZE * n : SIZE * (n + 1), SIZE:])
        for n in range(len(fields))
    ]


def left_transform(fields, table):
    cols = []
    for real, imag in fields:
        rh, rl = halves(real)
        ih, il = halves(imag)
        cols.append(jnp.concatenate([rh, ih, rl, il, rh, ih], axis=0))
    out = jnp.dot(table, jnp.concatenate(cols, axis=1), preferred_element_type=F32)
    return [
        (out[:SIZE, SIZE * n : SIZE * (n + 1)], out[SIZE:, SIZE * n : SIZE * (n + 1)])
        for n in range(len(fields))
    ]


def lanes():
    return lax.broadcasted_iota(jnp.int32, (SIZE, SIZE), 1)


def window(ref, lead, row, col):
    shift = lax.rem(SIZE - col, SIZE)
    rows = pl.ds(row, SIZE)
    mixed = jnp.where(lanes() >= col, ref[lead + (0, rows)], ref[lead + (1, rows)])
    return pltpu.roll(mixed, shift, 1)


def place(ref, plane, row, col, block):
    moved = pltpu.roll(block, lax.rem(col, SIZE), 1)
    first = lanes() >= col
    rows = pl.ds(row, SIZE)
    ref[plane, 0, rows] += jnp.where(first, moved, 0.0)
    ref[plane, 1, rows] += jnp.where(first, 0.0, moved)


def join(low, first, second):
    return jnp.where(low, pltpu.roll(first, HALF, 1), pltpu.roll(second, HALF, 1))


def pack_low(low, upper, lower):
    return jnp.where(low, upper, pltpu.roll(lower, HALF, 1))


def pack_high(low, upper, lower):
    return jnp.where(low, pltpu.roll(upper, HALF, 1), lower)


def low_lanes(rows):
    return lax.broadcasted_iota(jnp.int32, (rows, SIZE), 1) < HALF


def bounds(edges):
    return tuple(edges[k] for k in range(4))


def inside(limits, down, across, rows=SIZE):
    row_low, row_high, col_low, col_high = limits
    line = lax.broadcasted_iota(jnp.int32, (rows, SIZE), 0) + down
    lane = lax.broadcasted_iota(jnp.int32, (rows, SIZE), 1) + across
    return (line >= row_low) & (line < row_high) & (lane >= col_low) & (lane < col_high)


def pad_field(above, own, below, from_left, from_right, store):
    low = low_lanes(HALF)
    for c in range(2):
        strips = (above[c, :HALF], own[c, :HALF], own[c, HALF:], below[c, :HALF])
        for k in range(4):
            half = slice(HALF * (k % 2), HALF * (k % 2 + 1))
            left, right = from_left[c, half], from_right[c, half]
            if k < 2:
                right = pltpu.roll(right, HALF, 1)
            else:
                left = pltpu.roll(left, HALF, 1)
            mine = pltpu.roll(strips[k], HALF, 1)
            rows = slice(HALF * k, HALF * (k + 1))
            store(c, 0, rows, jnp.where(low, left, mine))
            store(c, 1, rows, jnp.where(low, mine, right))


def send_kernel(offsets, own, tile, to_below, to_above, sems):
    strip = pl.ds(0, HALF)
    copies = [
        pltpu.make_async_copy(source, target, sems.at[k])
        for k, (source, target) in enumerate((
            (own.at[:, pl.ds(HALF, HALF)], to_below.at[:, strip]),
            (own.at[:, strip], to_above.at[:, strip]),
            (own, tile),
        ))
    ]
    for copy in copies:
        copy.start()
    line = lax.broadcasted_iota(jnp.int32, (TILES, SIZE), 0)
    lane = lax.broadcasted_iota(jnp.int32, (TILES, SIZE), 1)
    code = jnp.zeros((TILES, SIZE), jnp.int32)
    batches, _, count = offsets.shape
    for b in range(batches):
        for k in range(count):
            for d in range(2):
                code = jnp.where(lane == (b * 2 + d) * count + k, offsets[b, d, k] + MARK, code)
    code = jnp.where(line == 0, code, 0).astype(F32)
    for c in range(2):
        to_below[c, HALF:] = code
        to_above[c, HALF:] = code
    for copy in copies:
        copy.wait()


def pack_kernel(above, own, below, mine, to_left, to_right, codes):
    low = low_lanes(HALF)
    for c in range(2):
        strips = (above[c, :HALF], own[c, :HALF], own[c, HALF:], below[c, :HALF])
        for k in range(2):
            rows = slice(HALF * k, HALF * (k + 1))
            to_left[c, rows] = pack_low(low, strips[k], strips[k + 2])
            to_right[c, rows] = pack_high(low, strips[k], strips[k + 2])
    code = mine[0, HALF:] + pltpu.roll(above[0, HALF:], 1, 0) + pltpu.roll(below[0, HALF:], 2, 0)
    for c in range(2):
        to_left[c, SIZE:] = code
        to_right[c, SIZE:] = code
    codes[...] = code


def power_of(probe):
    return sum(probe[c, m] * probe[c, m] for c in range(2) for m in range(MODES))


def stage_kernel(codes, *refs):
    count = (len(refs) - 1) // 2
    sems = refs[-1]
    copies = [pltpu.make_async_copy(refs[k], refs[count + k], sems.at[k]) for k in range(count)]
    for copy in copies:
        copy.start()
    for copy in copies:
        copy.wait()


def sweep(batch, offsets, padded, probe, measured, right3, left3, sums, accum):
    accum[...] = jnp.zeros_like(accum)
    tr = right3[...]
    tl = left3[...]
    wins = []
    waves = []
    for j in range(COUNT):
        row, col = offsets[batch, 0, j] + HALF, offsets[batch, 1, j] + HALF
        wr = window(padded, (0,), row, col)
        wi = window(padded, (1,), row, col)
        wins.append((row, col, wr, wi))
        fields = []
        for m in range(MODES):
            pr, pi = probe[0, m], probe[1, m]
            fields.append((pr * wr - pi * wi, pr * wi + pi * wr))
        waves.append(right_transform(fields, tr))
    waves = [left_transform(fields, tl) for fields in waves]
    chis = []
    for j in range(COUNT):
        intensity = sum(r * r + i * i for r, i in waves[j])
        ratio = jnp.sqrt(measured[0, 0, batch, j]) / jnp.maximum(jnp.sqrt(intensity), 0.5) - 1.0
        chis.append(left_transform([(r * ratio, -(i * ratio)) for r, i in waves[j]], tl))
    chis = [right_transform(fields, tr) for fields in chis]
    light = power_of(probe) if accum.shape[0] == 3 else None
    totals = [0.0] * 5
    for j in range(COUNT):
        row, col, wr, wi = wins[j]
        cr = jnp.zeros((SIZE, SIZE), F32)
        ci = jnp.zeros((SIZE, SIZE), F32)
        for m in range(MODES):
            xr, xn = chis[j][m]
            pr, pi = probe[0, m], probe[1, m]
            cr += pr * xr - pi * xn
            ci -= pr * xn + pi * xr
            totals[m] = totals[m] + (wr * xr - wi * xn)
            totals[MODES + m] = totals[MODES + m] - (wr * xn + wi * xr)
        totals[2 * MODES] = totals[2 * MODES] + (wr * wr + wi * wi)
        place(accum, 0, row, col, cr)
        place(accum, 1, row, col, ci)
        if light is not None:
            place(accum, 2, row, col, light)
    for k in range(5):
        sums[k] = totals[k]


def first_kernel(offsets, above, own, below, from_left, from_right, probe, measured, right3, left3,
                 top, bottom, sums, padded, accum):
    def store(c, h, rows, value):
        padded[c, h, rows] = value

    pad_field(above, own, below, from_left, from_right, store)
    sweep(0, offsets, padded, probe, measured, right3, left3, sums, accum)
    top[...] = accum[:, :, :SIZE]
    bottom[...] = accum[:, :, SIZE:]


def offset_of(others, batch, across, down, j, d):
    return others[TILES * across + (1, 0, 2)[down], (batch * 2 + d) * COUNT + j] - MARK


def cover_kernel(others, probe, cover, near, light):
    none = jnp.zeros((SIZE, SIZE), F32)
    light[:SIZE] = none
    light[SIZE : 2 * SIZE] = power_of(probe)
    light[2 * SIZE :] = none
    lane = lanes()
    for v in range(2):
        total = [none, none]
        for down in (v, v + 1):
            for across in range(3):
                for j in range(COUNT):
                    row, col = (offset_of(others, 0, across, down, j, d) + HALF for d in range(2))
                    row = jnp.clip(row + SIZE * (down - 1 - v), -SIZE, SIZE)
                    col = jnp.clip(col, 0, SIZE)
                    moved = pltpu.roll(light[pl.ds(SIZE - row, SIZE)], lax.rem(col, SIZE), 1)
                    first = lane >= col
                    if across >= 1:
                        total[across - 1] = total[across - 1] + jnp.where(first, moved, 0.0)
                    if across <= 1:
                        total[across] = total[across] + jnp.where(first, 0.0, moved)
        for h in range(2):
            cover[h, v * SIZE : (v + 1) * SIZE] = total[h]

    count = jnp.int32(0)
    for down in range(3):
        for across in range(3):
            for j in range(COUNT):
                row = offset_of(others, 1, across, down, j, 0) + SIZE * (down - 1)
                col = offset_of(others, 1, across, down, j, 1) + SIZE * (across - 1)
                near[count, 0] = row
                near[count, 1] = col
                reaches = (jnp.abs(row) < SIZE) & (jnp.abs(col) < SIZE)
                count += reaches.astype(jnp.int32)
    for k in range(LIST_STEP):
        near[count + k, 0] = SIZE
        near[count + k, 1] = 0
    near[LIST_SIZE - 1, 0] = count


def wide_fold_kernel(top, bottom, from_above, from_below, left, right):
    for v, own, other in ((0, top, from_above), (1, bottom, from_below)):
        left[v] = own[:, 0] + other[:, 0]
        right[v] = own[:, 1] + other[:, 1]


def pack_planes(packed, planes):
    strips = (SIZE // TILES, TILES, SIZE)
    upper = lax.rem(lax.broadcasted_iota(jnp.int32, (SIZE, SIZE), 0), TILES) < TILES // 2
    for q in range(len(planes) // 2):
        one, two = planes[2 * q], planes[2 * q + 1]
        packed[:, 0, q] = jnp.where(upper, one, pltpu.roll(two, TILES // 2, 0)).reshape(strips)
        packed[:, 1, q] = jnp.where(upper, pltpu.roll(one, SIZE - TILES // 2, 0), two).reshape(strips)


def unpack_planes(packed, q):
    upper = lax.rem(lax.broadcasted_iota(jnp.int32, (SIZE, SIZE), 0), TILES) < TILES // 2
    one, two = (packed[:, h, q].reshape(SIZE, SIZE) for h in range(2))
    return (jnp.where(upper, one, pltpu.roll(two, TILES // 2, 0)),
            jnp.where(upper, pltpu.roll(one, SIZE - TILES // 2, 0), two))


def pack_sums(packed, sums, overlap, a11, b1):
    turn = lax.rem(lax.broadcasted_iota(jnp.int32, (SIZE, SIZE), 0), TILES // 2)
    numbers = jnp.where(turn == 0, a11, jnp.where(turn == 1, b1, 0.0))
    pack_planes(packed, [sums[k] for k in range(5)] + [numbers] + list(overlap))


def wide_merge_kernel(edges, offsets, left, right, from_left, from_right, cover, padded, sums,
                      packed, direction, product):
    limits = bounds(edges)
    a11 = jnp.zeros((1, SIZE), F32)
    b1 = jnp.zeros((1, SIZE), F32)
    for v in range(2):
        rows = slice(v * SIZE, (v + 1) * SIZE)
        mine_rows = lax.broadcasted_iota(jnp.int32, (SIZE, SIZE), 0) + v * SIZE
        for h in range(2):
            own, other = ((left, from_left), (right, from_right))[h]
            light = cover[h, rows]
            inverse = jnp.where(inside(limits, v * SIZE, h * SIZE), 1.0 / (light + 1.0), 0.0)
            dr, di = ((own[v, c] + other[v, c]) * inverse for c in range(2))
            direction[0, h, rows] = dr
            direction[1, h, rows] = di
            pr, pi = padded[0, h, rows], padded[1, h, rows]
            product[0, h, rows] = dr * pr + di * pi
            product[1, h, rows] = dr * pi - di * pr
            across = lanes() + h * SIZE
            mine = (mine_rows >= HALF) & (mine_rows < HALF + SIZE) & (across >= HALF) & (across < HALF + SIZE)
            power = jnp.where(mine, dr * dr + di * di, 0.0)
            a11 += jnp.sum(power * light, axis=0, keepdims=True)
            b1 += jnp.sum(power * (light + 1.0), axis=0, keepdims=True)
    overlap = [jnp.zeros((SIZE, SIZE), F32)] * 2
    for j in range(COUNT):
        row, col = offsets[0, 0, j] + HALF, offsets[0, 1, j] + HALF
        overlap = [overlap[c] + window(product, (c,), row, col) for c in range(2)]
    pack_sums(packed, sums, overlap, a11, b1)


def fold_kernel(middle, from_above, from_below, tile, left, right):
    low = low_lanes(HALF)
    for k in range(3):
        upper = [middle[k, h, :HALF] + from_above[k, h] for h in range(2)]
        lower = [middle[k, h, HALF:] + from_below[k, h] for h in range(2)]
        tile[k, :HALF] = join(low, *upper)
        tile[k, HALF:] = join(low, *lower)
        left[k] = pack_low(low, upper[0], lower[0])
        right[k] = pack_high(low, upper[1], lower[1])


def merge_kernel(near, tile, from_left, from_right, padded, sums,
                 packed, direction, product, overlap):
    low = low_lanes(HALF)
    lane = lanes()
    a11 = jnp.zeros((1, SIZE), F32)
    b1 = jnp.zeros((1, SIZE), F32)
    product[...] = jnp.zeros_like(product)
    for v in range(2):
        rows = slice(HALF * v, HALF * (v + 1))
        full = []
        for k in range(3):
            left, right = from_left[k], from_right[k]
            if v == 0:
                right = pltpu.roll(right, HALF, 1)
            else:
                left = pltpu.roll(left, HALF, 1)
            full.append(tile[k, rows] + jnp.where(low, left, right))
        gr, gi, cover = full
        inverse = 1.0 / (cover + 1.0)
        dr = gr * inverse
        di = gi * inverse
        direction[0, rows] = dr
        direction[1, rows] = di
        span = slice(HALF * (v + 1), HALF * (v + 2))
        pr = join(low, padded[0, 0, span], padded[0, 1, span])
        pi = join(low, padded[1, 0, span], padded[1, 1, span])
        inner = slice(SIZE + HALF * v, SIZE + HALF * (v + 1))
        product[0, inner] = dr * pr + di * pi
        product[1, inner] = dr * pi - di * pr
        power = dr * dr + di * di
        a11 += jnp.sum(power * cover, axis=0, keepdims=True)
        b1 += jnp.sum(power * (cover + 1.0), axis=0, keepdims=True)
    overlap[...] = jnp.zeros_like(overlap)

    def body(step, carry):
        total = [0.0, 0.0]
        for g in range(LIST_STEP):
            down, across = near[step * LIST_STEP + g, 0], near[step * LIST_STEP + g, 1]
            turn = lax.rem(2 * SIZE - across, SIZE)
            source = lane + across
            valid = (source >= 0) & (source < SIZE)
            for c in range(2):
                moved = pltpu.roll(product[c, pl.ds(SIZE + down, SIZE)], turn, 1)
                total[c] = total[c] + jnp.where(valid, moved, 0.0)
        for c in range(2):
            overlap[c] += total[c]
        return carry

    lax.fori_loop(0, lax.div(near[LIST_SIZE - 1, 0] + LIST_STEP - 1, LIST_STEP), body, 0)

    pack_sums(packed, sums, (overlap[0], overlap[1]), a11, b1)


def add_all(parts):
    total = parts[0]
    for k in range(1, parts.shape[0]):
        total = total + parts[k]
    return total


def reduce_kernel(parts, out):
    total = add_all(parts)
    for k in range(out.shape[0]):
        out[k] = total


def strip_kernel(place_ref, parts, probe, out):
    total = add_all(parts)
    line = lax.broadcasted_iota(jnp.int32, (TILES, SIZE), 0)
    half = TILES // 2
    upper = line < half
    first = place_ref[1] == 0
    rows = pl.ds(pl.multiple_of(place_ref[0] * TILES, TILES), TILES)

    def turned(x):
        return pltpu.roll(x, half, 0)

    def both(x, of_upper):
        return jnp.where(upper == of_upper, x, turned(x))

    def modes(c):
        one, two = probe[c, 0, rows], probe[c, 1, rows]
        return jnp.where(upper, jnp.where(first, one, turned(one)), jnp.where(first, turned(two), two))

    pr, pi = modes(0), modes(1)
    cover = both(total[2], True)
    inverse = 1.0 / (cover + 1.0)
    dr, di = total[0] * inverse, total[1] * inverse
    cross = (pr * dr + pi * di) * both(total[3], True) - (pr * di - pi * dr) * both(total[3], False)
    power = dr * dr + di * di
    a22, b2, a12 = (
        jnp.sum(x, axis=0, keepdims=True) for x in (power * cover, power * (cover + 1.0), cross))
    a11, b1 = total[2, half : half + 1], total[2, half + 1 : half + 2]
    low = low_lanes(1)
    known = jnp.where(low, a11 + pltpu.roll(a11, HALF, 1), b1 + pltpu.roll(b1, HALF, 1))
    numbers = total[2]
    for k, term in enumerate((known, a22, b2, a12)):
        numbers = jnp.where(line == half + k, term, numbers)
    for k in range(out.shape[0]):
        out[k, 0] = total[0]
        out[k, 1] = total[1]
        out[k, 2] = numbers


def step_sizes(totals, probe, new_probe, gradient=None):
    numbers = jnp.zeros((TILES, SIZE), F32)
    for k in range(totals.shape[0]):
        numbers += totals[k, 0, 2] + totals[k, 1, 2]
    half = TILES // 2
    low = low_lanes(1)
    known, *rest = (numbers[half + k : half + k + 1] for k in range(4))
    a22, b2, a12 = (jnp.sum(x, axis=1, keepdims=True) for x in rest)
    share = 1.0 / (2 * totals.shape[0])
    a11 = jnp.sum(jnp.where(low, known, 0.0), axis=1, keepdims=True) * share
    b1 = jnp.sum(jnp.where(low, 0.0, known), axis=1, keepdims=True) * share
    a11 = 1.1 * a11
    a22 = 1.1 * a22
    det = a11 * a22 - a12 * a12
    step_obj = (b1 * a22 - a12 * b2) / det
    step_probe = (a11 * b2 - a12 * b1) / det
    cover, _ = unpack_planes(totals, 2)
    cover = cover + 1.0
    scale = step_probe / cover
    for c in range(2):
        for m, numer in enumerate(unpack_planes(totals, c)):
            new_probe[c, m] = probe[c, m] + scale * numer
            if gradient is not None:
                gradient[c, m] = numer * lax.rsqrt(cover)
    return step_obj


def next_kernel(offsets, totals, padded, direction, probe, measured, right3, left3,
                top, middle, bottom, sums, new_padded, new_probe, accum):
    step = step_sizes(totals, probe, new_probe)
    new_padded[...] = padded[...] + step * direction[...]
    sweep(1, offsets, new_padded, new_probe, measured, right3, left3, sums, accum)
    top[...] = accum[:, :, :HALF]
    middle[...] = accum[:, :, HALF : HALF + SIZE]
    bottom[...] = accum[:, :, HALF + SIZE :]


def last_kernel(totals, padded, direction, probe, new_obj, new_probe, gradient):
    step = step_sizes(totals, probe, new_probe, gradient)
    low = lanes() < HALF
    rows = slice(HALF, HALF + SIZE)
    for c in range(2):
        old = join(low, padded[c, 0, rows], padded[c, 1, rows])
        new_obj[c] = old + step * direction[c]


def shape(*dims):
    return jax.ShapeDtypeStruct(dims, F32)


def call(kernel, ins, outs, scratch=(), in_hbm=()):
    vmem = pl.BlockSpec(memory_space=pltpu.VMEM)
    smem = pl.BlockSpec(memory_space=pltpu.SMEM)
    hbm = pl.BlockSpec(memory_space=pltpu.HBM)
    ins = [pltpu.with_memory_space_constraint(x, pltpu.HBM) if k in in_hbm else x for k, x in enumerate(ins)]
    specs = [hbm if k in in_hbm else smem if x.dtype == jnp.int32 else vmem for k, x in enumerate(ins)]
    return pl.pallas_call(
        kernel,
        in_specs=specs,
        out_specs=[smem if x.dtype == jnp.int32 else vmem for x in outs],
        out_shape=list(outs),
        scratch_shapes=list(scratch),
        compiler_params=pltpu.CompilerParams(vmem_limit_bytes=VMEM_LIMIT),
        name=getattr(kernel, "func", kernel).__name__,
    )(*ins)


def shift(block, rows, cols):
    n_row = math.prod(lax.axis_size(a) for a in ROW)
    n_col = math.prod(lax.axis_size(a) for a in COL)
    route = [
        (r * n_col + c, (r + rows) * n_col + c + cols)
        for r in range(n_row)
        for c in range(n_col)
        if 0 <= r + rows < n_row and 0 <= c + cols < n_col
    ]
    return lax.ppermute(block, ALL, route)


def exchange(block, axes):
    return lax.all_to_all(block, axes, 0, 0, tiled=True)


def size_of(axes):
    return math.prod(lax.axis_size(a) for a in axes)


def reduce_all(packed, probe, place_in_group):
    group, rest = size_of(SCATTER), size_of(REST)
    part = exchange(packed.reshape(group, 4, TILES, SIZE), SCATTER)
    (part,) = call(reduce_kernel, [part], [shape(rest, 4, TILES, SIZE)])
    part = exchange(part, REST)
    (part,) = call(strip_kernel, [place_in_group, part, probe], [shape(group, 3, TILES, SIZE)])
    return exchange(part, SCATTER).reshape(SIZE // TILES, 2, 3, TILES, SIZE)


def per_device(obj, probe, measured, offsets):
    right3, left3 = (jnp.asarray(t) for t in dft_tables())
    offsets = jnp.swapaxes(offsets[0, 0], 1, 2)
    r, c, half = (lax.axis_index(axes).astype(jnp.int32) for axes in (ROW, COL, ("zl",)))
    whole = 2 * SIZE
    place_in_group = jnp.stack([r, half])
    edges = jnp.stack([
        jnp.where(r == 0, HALF, 0),
        jnp.where(r == size_of(ROW) - 1, whole - HALF, whole),
        jnp.where(c == 0, HALF, 0),
        jnp.where(c == size_of(COL) - 1, whole - HALF, whole),
    ]).astype(jnp.int32)

    strip = shape(2, HALF + TILES, SIZE)
    side = shape(2, SIZE + TILES, SIZE)
    tile, to_below, to_above = call(
        send_kernel, [offsets, obj], [shape(2, SIZE, SIZE), strip, strip],
        [pltpu.SemaphoreType.DMA((3,))], in_hbm=(1,))
    above = shift(to_below, 1, 0)
    below = shift(to_above, -1, 0)
    to_left, to_right, codes = call(
        pack_kernel, [above, tile, below, to_below], [side, side, shape(TILES, SIZE)])
    from_left = shift(to_right, 0, 1)
    from_right = shift(to_left, 0, -1)
    staged = [measured, right3, left3]
    measured, right3, left3 = call(
        stage_kernel, [codes, *staged], [jax.ShapeDtypeStruct(x.shape, x.dtype) for x in staged],
        [pltpu.SemaphoreType.DMA((len(staged),))], in_hbm=(1, 2, 3))
    others = jnp.concatenate([from_left[0, SIZE:], codes, from_right[0, SIZE:]], axis=0).astype(jnp.int32)

    field = shape(2, 2, whole, SIZE)
    edge = shape(3, 2, HALF, SIZE)
    quads = shape(2, 2, SIZE, SIZE)
    planes = shape(2, MODES, SIZE, SIZE)
    sums_shape = shape(5, SIZE, SIZE)
    packed_shape = shape(SIZE // TILES, 2, 4, TILES, SIZE)

    top, bottom, sums, padded = call(
        first_kernel,
        [offsets, above, tile, below, from_left, from_right, probe, measured, right3, left3],
        [quads, quads, sums_shape, field],
        [pltpu.VMEM((2, 2, whole, SIZE), F32)],
    )
    from_above = shift(bottom, 1, 0)
    from_below = shift(top, -1, 0)
    cover, near = call(
        cover_kernel, [others, probe],
        [shape(2, whole, SIZE), jax.ShapeDtypeStruct((LIST_SIZE, 2), jnp.int32)],
        [pltpu.VMEM((3 * SIZE, SIZE), F32)])
    left, right = call(wide_fold_kernel, [top, bottom, from_above, from_below], [quads, quads])
    from_left = shift(right, 0, 1)
    from_right = shift(left, 0, -1)
    packed, direction = call(
        wide_merge_kernel,
        [edges, offsets, left, right, from_left, from_right, cover, padded, sums],
        [packed_shape, field],
        [pltpu.VMEM((2, 2, whole, SIZE), F32)],
    )
    totals = reduce_all(packed, probe, place_in_group)

    top, middle, bottom, sums, padded, probe = call(
        next_kernel,
        [offsets, totals, padded, direction, probe, measured, right3, left3],
        [edge, shape(3, 2, SIZE, SIZE), edge, sums_shape, field, planes],
        [pltpu.VMEM((3, 2, whole, SIZE), F32)],
    )
    from_above = shift(bottom, 1, 0)
    from_below = shift(top, -1, 0)
    side = shape(3, HALF, SIZE)
    middle, left, right = call(
        fold_kernel, [middle, from_above, from_below], [shape(3, SIZE, SIZE), side, side])
    from_left = shift(right, 0, 1)
    from_right = shift(left, 0, -1)
    packed, direction = call(
        merge_kernel,
        [near, middle, from_left, from_right, padded, sums],
        [packed_shape, shape(2, SIZE, SIZE)],
        [pltpu.VMEM((2, 3 * SIZE, SIZE), F32), pltpu.VMEM((2, SIZE, SIZE), F32)],
    )
    totals = reduce_all(packed, probe, place_in_group)
    return tuple(call(
        last_kernel, [totals, padded, direction, probe], [shape(2, SIZE, SIZE), planes, planes]
    ))


def solution(mesh):
    parts = Mesh(mesh.devices.reshape(2, 4, 2, 4, 4, 2), ALL)
    in_specs = (P(None, ROW, COL), P(), P(ROW, COL), P(ROW, COL))
    out_specs = (P(None, ROW, COL), P(), P())
    return jax.shard_map(
        per_device, mesh=parts, in_specs=in_specs, out_specs=out_specs, check_vma=False
    )
```

```python
import math
from functools import partial

import jax
import jax.numpy as jnp
import numpy as np
from jax import lax
from jax.experimental import pallas as pl
from jax.experimental.pallas import tpu as pltpu
from jax.sharding import Mesh, PartitionSpec as P

SIZE = 128
HALF = 64
MODES = 2
COUNT = 8
ROW = ("yl", "x", "c")
COL = ("yh", "zh", "zl")
ALL = ROW + COL
SCATTER = ROW + ("zl",)
REST = ("zh", "yh")
MARK = 1024
LIST_STEP = 4
LIST_SIZE = 9 * COUNT + 8
TILES = 8
VMEM_LIMIT = 16 * 1024 * 1024
F32 = jnp.float32
BF16 = jnp.bfloat16


def dft_tables():
    index = np.arange(SIZE)
    angle = 2.0 * math.pi / SIZE * (np.outer(index, index) % SIZE)
    real = np.cos(angle) / math.sqrt(SIZE)
    imag = -np.sin(angle) / math.sqrt(SIZE)
    right = np.block([[real, imag], [-imag, real]]).astype(np.float32)
    high = right.astype(jnp.bfloat16)
    low = (right - high.astype(np.float32)).astype(jnp.bfloat16)
    right3 = np.concatenate([high, high, low], axis=0)
    left3 = np.ascontiguousarray(right3.T)
    return right3, left3


def halves(x):
    high = x.astype(BF16)
    return high, (x - high.astype(F32)).astype(BF16)


def right_transform(fields, table):
    rows = []
    for real, imag in fields:
        rh, rl = halves(real)
        ih, il = halves(imag)
        rows.append(jnp.concatenate([rh, ih, rl, il, rh, ih], axis=1))
    out = jnp.dot(jnp.concatenate(rows, axis=0), table, preferred_element_type=F32)
    return [
        (out[SIZE * n : SIZE * (n + 1), :SIZE], out[SIZE * n : SIZE * (n + 1), SIZE:])
        for n in range(len(fields))
    ]


def left_transform(fields, table):
    cols = []
    for real, imag in fields:
        rh, rl = halves(real)
        ih, il = halves(imag)
        cols.append(jnp.concatenate([rh, ih, rl, il, rh, ih], axis=0))
    out = jnp.dot(table, jnp.concatenate(cols, axis=1), preferred_element_type=F32)
    return [
        (out[:SIZE, SIZE * n : SIZE * (n + 1)], out[SIZE:, SIZE * n : SIZE * (n + 1)])
        for n in range(len(fields))
    ]


def lanes():
    return lax.broadcasted_iota(jnp.int32, (SIZE, SIZE), 1)


def window(ref, lead, row, col):
    shift = lax.rem(SIZE - col, SIZE)
    rows = pl.ds(row, SIZE)
    mixed = jnp.where(lanes() >= col, ref[lead + (0, rows)], ref[lead + (1, rows)])
    return pltpu.roll(mixed, shift, 1)


def place(ref, plane, row, col, block):
    moved = pltpu.roll(block, lax.rem(col, SIZE), 1)
    first = lanes() >= col
    rows = pl.ds(row, SIZE)
    ref[plane, 0, rows] += jnp.where(first, moved, 0.0)
    ref[plane, 1, rows] += jnp.where(first, 0.0, moved)


def join(low, first, second):
    return jnp.where(low, pltpu.roll(first, HALF, 1), pltpu.roll(second, HALF, 1))


def pack_low(low, upper, lower):
    return jnp.where(low, upper, pltpu.roll(lower, HALF, 1))


def pack_high(low, upper, lower):
    return jnp.where(low, pltpu.roll(upper, HALF, 1), lower)


def low_lanes(rows):
    return lax.broadcasted_iota(jnp.int32, (rows, SIZE), 1) < HALF


def bounds(edges):
    return tuple(edges[k] for k in range(4))


def inside(limits, down, across, rows=SIZE):
    row_low, row_high, col_low, col_high = limits
    line = lax.broadcasted_iota(jnp.int32, (rows, SIZE), 0) + down
    lane = lax.broadcasted_iota(jnp.int32, (rows, SIZE), 1) + across
    return (line >= row_low) & (line < row_high) & (lane >= col_low) & (lane < col_high)


def pad_field(above, own, below, from_left, from_right, store):
    low = low_lanes(HALF)
    for c in range(2):
        strips = (above[c, :HALF], own[c, :HALF], own[c, HALF:], below[c, :HALF])
        for k in range(4):
            half = slice(HALF * (k % 2), HALF * (k % 2 + 1))
            left, right = from_left[c, half], from_right[c, half]
            if k < 2:
                right = pltpu.roll(right, HALF, 1)
            else:
                left = pltpu.roll(left, HALF, 1)
            mine = pltpu.roll(strips[k], HALF, 1)
            rows = slice(HALF * k, HALF * (k + 1))
            store(c, 0, rows, jnp.where(low, left, mine))
            store(c, 1, rows, jnp.where(low, mine, right))


def send_kernel(raw, own, tile, to_below, to_above, offsets, sems):
    strip = pl.ds(0, HALF)
    first = pltpu.make_async_copy(raw, offsets, sems.at[3])
    first.start()
    copies = [
        pltpu.make_async_copy(source, target, sems.at[k])
        for k, (source, target) in enumerate((
            (own.at[:, pl.ds(HALF, HALF)], to_below.at[:, strip]),
            (own.at[:, strip], to_above.at[:, strip]),
            (own, tile),
        ))
    ]
    for copy in copies:
        copy.start()
    line = lax.broadcasted_iota(jnp.int32, (TILES, SIZE), 0)
    lane = lax.broadcasted_iota(jnp.int32, (TILES, SIZE), 1)
    code = jnp.zeros((TILES, SIZE), jnp.int32)
    first.wait()
    batches, _, count = offsets.shape
    for b in range(batches):
        for k in range(count):
            for d in range(2):
                code = jnp.where(lane == (b * 2 + d) * count + k, offsets[b, d, k] + MARK, code)
    code = jnp.where(line == 0, code, 0).astype(F32)
    for c in range(2):
        to_below[c, HALF:] = code
        to_above[c, HALF:] = code
    for copy in copies:
        copy.wait()


def pack_kernel(above, own, below, mine, to_left, to_right, codes):
    low = low_lanes(HALF)
    for c in range(2):
        strips = (above[c, :HALF], own[c, :HALF], own[c, HALF:], below[c, :HALF])
        for k in range(2):
            rows = slice(HALF * k, HALF * (k + 1))
            to_left[c, rows] = pack_low(low, strips[k], strips[k + 2])
            to_right[c, rows] = pack_high(low, strips[k], strips[k + 2])
    code = mine[0, HALF:] + pltpu.roll(above[0, HALF:], 1, 0) + pltpu.roll(below[0, HALF:], 2, 0)
    for c in range(2):
        to_left[c, SIZE:] = code
        to_right[c, SIZE:] = code
    codes[...] = code


def power_of(probe):
    return sum(probe[c, m] * probe[c, m] for c in range(2) for m in range(MODES))


def stage_kernel(codes, *refs):
    count = (len(refs) - 1) // 2
    sems = refs[-1]
    copies = [pltpu.make_async_copy(refs[k], refs[count + k], sems.at[k]) for k in range(count)]
    for copy in copies:
        copy.start()
    for copy in copies:
        copy.wait()


def sweep(batch, offsets, padded, probe, measured, right3, left3, sums, accum):
    accum[...] = jnp.zeros_like(accum)
    tr = right3[...]
    tl = left3[...]
    wins = []
    waves = []
    for j in range(COUNT):
        row, col = offsets[batch, 0, j] + HALF, offsets[batch, 1, j] + HALF
        wr = window(padded, (0,), row, col)
        wi = window(padded, (1,), row, col)
        wins.append((row, col, wr, wi))
        fields = []
        for m in range(MODES):
            pr, pi = probe[0, m], probe[1, m]
            fields.append((pr * wr - pi * wi, pr * wi + pi * wr))
        waves.append(right_transform(fields, tr))
    waves = [left_transform(fields, tl) for fields in waves]
    chis = []
    for j in range(COUNT):
        intensity = sum(r * r + i * i for r, i in waves[j])
        ratio = jnp.sqrt(measured[0, 0, batch, j]) / jnp.maximum(jnp.sqrt(intensity), 0.5) - 1.0
        chis.append(left_transform([(r * ratio, -(i * ratio)) for r, i in waves[j]], tl))
    chis = [right_transform(fields, tr) for fields in chis]
    totals = [0.0] * 5
    for j in range(COUNT):
        row, col, wr, wi = wins[j]
        cr = jnp.zeros((SIZE, SIZE), F32)
        ci = jnp.zeros((SIZE, SIZE), F32)
        for m in range(MODES):
            xr, xn = chis[j][m]
            pr, pi = probe[0, m], probe[1, m]
            cr += pr * xr - pi * xn
            ci -= pr * xn + pi * xr
            totals[m] = totals[m] + (wr * xr - wi * xn)
            totals[MODES + m] = totals[MODES + m] - (wr * xn + wi * xr)
        totals[2 * MODES] = totals[2 * MODES] + (wr * wr + wi * wi)
        place(accum, 0, row, col, cr)
        place(accum, 1, row, col, ci)
    for k in range(5):
        sums[k] = totals[k]


def first_kernel(offsets, above, own, below, from_left, from_right, probe, measured, right3, left3,
                 top, bottom, sums, padded, accum):
    def store(c, h, rows, value):
        padded[c, h, rows] = value

    pad_field(above, own, below, from_left, from_right, store)
    sweep(0, offsets, padded, probe, measured, right3, left3, sums, accum)
    top[...] = accum[:, :, :SIZE]
    bottom[...] = accum[:, :, SIZE:]


def offset_of(others, batch, across, down, j, d):
    return others[TILES * across + (1, 0, 2)[down], (batch * 2 + d) * COUNT + j] - MARK


def cover_kernel(others, probe, cover, near, light):
    none = jnp.zeros((SIZE, SIZE), F32)
    light[:SIZE] = none
    light[SIZE : 2 * SIZE] = power_of(probe)
    light[2 * SIZE :] = none
    lane = lanes()
    for v in range(2):
        total = [none, none]
        for down in (v, v + 1):
            for across in range(3):
                for j in range(COUNT):
                    row, col = (offset_of(others, 0, across, down, j, d) + HALF for d in range(2))
                    row = jnp.clip(row + SIZE * (down - 1 - v), -SIZE, SIZE)
                    col = jnp.clip(col, 0, SIZE)
                    moved = pltpu.roll(light[pl.ds(SIZE - row, SIZE)], lax.rem(col, SIZE), 1)
                    first = lane >= col
                    if across >= 1:
                        total[across - 1] = total[across - 1] + jnp.where(first, moved, 0.0)
                    if across <= 1:
                        total[across] = total[across] + jnp.where(first, 0.0, moved)
        for h in range(2):
            cover[h, v * SIZE : (v + 1) * SIZE] = total[h]

    count = jnp.int32(0)
    for down in range(3):
        for across in range(3):
            for j in range(COUNT):
                row = offset_of(others, 1, across, down, j, 0) + SIZE * (down - 1)
                col = offset_of(others, 1, across, down, j, 1) + SIZE * (across - 1)
                near[count, 0] = row
                near[count, 1] = col
                reaches = (jnp.abs(row) < SIZE) & (jnp.abs(col) < SIZE)
                count += reaches.astype(jnp.int32)
    for k in range(LIST_STEP):
        near[count + k, 0] = SIZE
        near[count + k, 1] = 0
    near[LIST_SIZE - 1, 0] = count


def wide_fold_kernel(top, bottom, from_above, from_below, left, right):
    for v, own, other in ((0, top, from_above), (1, bottom, from_below)):
        left[v] = own[:, 0] + other[:, 0]
        right[v] = own[:, 1] + other[:, 1]


def pack_planes(packed, planes):
    strips = (SIZE // TILES, TILES, SIZE)
    upper = lax.rem(lax.broadcasted_iota(jnp.int32, (SIZE, SIZE), 0), TILES) < TILES // 2
    for q in range(len(planes) // 2):
        one, two = planes[2 * q], planes[2 * q + 1]
        packed[:, 0, q] = jnp.where(upper, one, pltpu.roll(two, TILES // 2, 0)).reshape(strips)
        packed[:, 1, q] = jnp.where(upper, pltpu.roll(one, SIZE - TILES // 2, 0), two).reshape(strips)


def unpack_planes(packed, q):
    upper = lax.rem(lax.broadcasted_iota(jnp.int32, (SIZE, SIZE), 0), TILES) < TILES // 2
    one, two = (packed[:, h, q].reshape(SIZE, SIZE) for h in range(2))
    return (jnp.where(upper, one, pltpu.roll(two, TILES // 2, 0)),
            jnp.where(upper, pltpu.roll(one, SIZE - TILES // 2, 0), two))


def pack_sums(packed, sums, overlap, a11, b1):
    turn = lax.rem(lax.broadcasted_iota(jnp.int32, (SIZE, SIZE), 0), TILES // 2)
    numbers = jnp.where(turn == 0, a11, jnp.where(turn == 1, b1, 0.0))
    pack_planes(packed, [sums[k] for k in range(5)] + [numbers] + list(overlap))


def wide_merge_kernel(edges, offsets, left, right, from_left, from_right, cover, padded, sums,
                      packed, direction, product):
    limits = bounds(edges)
    a11 = jnp.zeros((1, SIZE), F32)
    b1 = jnp.zeros((1, SIZE), F32)
    for v in range(2):
        rows = slice(v * SIZE, (v + 1) * SIZE)
        mine_rows = lax.broadcasted_iota(jnp.int32, (SIZE, SIZE), 0) + v * SIZE
        for h in range(2):
            own, other = ((left, from_left), (right, from_right))[h]
            light = cover[h, rows]
            inverse = jnp.where(inside(limits, v * SIZE, h * SIZE), 1.0 / (light + 1.0), 0.0)
            dr, di = ((own[v, c] + other[v, c]) * inverse for c in range(2))
            direction[0, h, rows] = dr
            direction[1, h, rows] = di
            pr, pi = padded[0, h, rows], padded[1, h, rows]
            product[0, h, rows] = dr * pr + di * pi
            product[1, h, rows] = dr * pi - di * pr
            across = lanes() + h * SIZE
            mine = (mine_rows >= HALF) & (mine_rows < HALF + SIZE) & (across >= HALF) & (across < HALF + SIZE)
            power = jnp.where(mine, dr * dr + di * di, 0.0)
            a11 += jnp.sum(power * light, axis=0, keepdims=True)
            b1 += jnp.sum(power * (light + 1.0), axis=0, keepdims=True)
    overlap = [jnp.zeros((SIZE, SIZE), F32)] * 2
    for j in range(COUNT):
        row, col = offsets[0, 0, j] + HALF, offsets[0, 1, j] + HALF
        overlap = [overlap[c] + window(product, (c,), row, col) for c in range(2)]
    pack_sums(packed, sums, overlap, a11, b1)


def fold_kernel(middle, from_above, from_below, tile, left, right):
    low = low_lanes(HALF)
    for k in range(2):
        upper = [middle[k, h, :HALF] + from_above[k, h] for h in range(2)]
        lower = [middle[k, h, HALF:] + from_below[k, h] for h in range(2)]
        tile[k, :HALF] = join(low, *upper)
        tile[k, HALF:] = join(low, *lower)
        left[k] = pack_low(low, upper[0], lower[0])
        right[k] = pack_high(low, upper[1], lower[1])


def tile_cover_kernel(near, probe, cover, light):
    none = jnp.zeros((SIZE, SIZE), F32)
    light[:SIZE] = none
    light[SIZE : 2 * SIZE] = power_of(probe)
    light[2 * SIZE :] = none
    cover[...] = none
    lane = lanes()

    def body(step, carry):
        total = 0.0
        for g in range(LIST_STEP):
            down, across = near[step * LIST_STEP + g, 0], near[step * LIST_STEP + g, 1]
            source = lane - across
            valid = (source >= 0) & (source < SIZE)
            moved = pltpu.roll(light[pl.ds(SIZE - down, SIZE)], lax.rem(2 * SIZE + across, SIZE), 1)
            total = total + jnp.where(valid, moved, 0.0)
        cover[...] += total
        return carry

    lax.fori_loop(0, lax.div(near[LIST_SIZE - 1, 0] + LIST_STEP - 1, LIST_STEP), body, 0)


def merge_kernel(near, tile, from_left, from_right, cover, padded, sums,
                 packed, direction, product, overlap):
    low = low_lanes(HALF)
    lane = lanes()
    a11 = jnp.zeros((1, SIZE), F32)
    b1 = jnp.zeros((1, SIZE), F32)
    for c in range(2):
        product[c, :SIZE] = jnp.zeros((SIZE, SIZE), F32)
        product[c, 2 * SIZE :] = jnp.zeros((SIZE, SIZE), F32)
        overlap[c] = jnp.zeros((SIZE, SIZE), F32)
    for v in range(2):
        rows = slice(HALF * v, HALF * (v + 1))
        full = []
        for k in range(2):
            left, right = from_left[k], from_right[k]
            if v == 0:
                right = pltpu.roll(right, HALF, 1)
            else:
                left = pltpu.roll(left, HALF, 1)
            full.append(tile[k, rows] + jnp.where(low, left, right))
        gr, gi = full
        light = cover[rows]
        inverse = 1.0 / (light + 1.0)
        dr = gr * inverse
        di = gi * inverse
        direction[0, rows] = dr
        direction[1, rows] = di
        span = slice(HALF * (v + 1), HALF * (v + 2))
        pr = join(low, padded[0, 0, span], padded[0, 1, span])
        pi = join(low, padded[1, 0, span], padded[1, 1, span])
        inner = slice(SIZE + HALF * v, SIZE + HALF * (v + 1))
        product[0, inner] = dr * pr + di * pi
        product[1, inner] = dr * pi - di * pr
        power = dr * dr + di * di
        a11 += jnp.sum(power * light, axis=0, keepdims=True)
        b1 += jnp.sum(power * (light + 1.0), axis=0, keepdims=True)

    def body(step, carry):
        total = [0.0, 0.0]
        for g in range(LIST_STEP):
            down, across = near[step * LIST_STEP + g, 0], near[step * LIST_STEP + g, 1]
            turn = lax.rem(2 * SIZE - across, SIZE)
            source = lane + across
            valid = (source >= 0) & (source < SIZE)
            for c in range(2):
                moved = pltpu.roll(product[c, pl.ds(SIZE + down, SIZE)], turn, 1)
                total[c] = total[c] + jnp.where(valid, moved, 0.0)
        for c in range(2):
            overlap[c] += total[c]
        return carry

    lax.fori_loop(0, lax.div(near[LIST_SIZE - 1, 0] + LIST_STEP - 1, LIST_STEP), body, 0)

    pack_sums(packed, sums, (overlap[0], overlap[1]), a11, b1)


def add_all(parts):
    total = parts[0]
    for k in range(1, parts.shape[0]):
        total = total + parts[k]
    return total


def reduce_kernel(parts, out):
    total = add_all(parts)
    for k in range(out.shape[0]):
        out[k] = total


def strip_kernel(place_ref, parts, probe, out):
    total = add_all(parts)
    line = lax.broadcasted_iota(jnp.int32, (TILES, SIZE), 0)
    half = TILES // 2
    upper = line < half
    first = place_ref[1] == 0
    rows = pl.ds(pl.multiple_of(place_ref[0] * TILES, TILES), TILES)

    def turned(x):
        return pltpu.roll(x, half, 0)

    def both(x, of_upper):
        return jnp.where(upper == of_upper, x, turned(x))

    def modes(c):
        one, two = probe[c, 0, rows], probe[c, 1, rows]
        return jnp.where(upper, jnp.where(first, one, turned(one)), jnp.where(first, turned(two), two))

    pr, pi = modes(0), modes(1)
    cover = both(total[2], True)
    inverse = 1.0 / (cover + 1.0)
    dr, di = total[0] * inverse, total[1] * inverse
    cross = (pr * dr + pi * di) * both(total[3], True) - (pr * di - pi * dr) * both(total[3], False)
    power = dr * dr + di * di
    a22, b2, a12 = (
        jnp.sum(x, axis=0, keepdims=True) for x in (power * cover, power * (cover + 1.0), cross))
    a11, b1 = total[2, half : half + 1], total[2, half + 1 : half + 2]
    low = low_lanes(1)
    known = jnp.where(low, a11 + pltpu.roll(a11, HALF, 1), b1 + pltpu.roll(b1, HALF, 1))
    numbers = total[2]
    for k, term in enumerate((known, a22, b2, a12)):
        numbers = jnp.where(line == half + k, term, numbers)
    for k in range(out.shape[0]):
        out[k, 0] = total[0]
        out[k, 1] = total[1]
        out[k, 2] = numbers


def step_sizes(totals, probe, new_probe, gradient=None):
    numbers = jnp.zeros((TILES, SIZE), F32)
    for k in range(totals.shape[0]):
        numbers += totals[k, 0, 2] + totals[k, 1, 2]
    half = TILES // 2
    low = low_lanes(1)
    known, *rest = (numbers[half + k : half + k + 1] for k in range(4))
    a22, b2, a12 = (jnp.sum(x, axis=1, keepdims=True) for x in rest)
    share = 1.0 / (2 * totals.shape[0])
    a11 = jnp.sum(jnp.where(low, known, 0.0), axis=1, keepdims=True) * share
    b1 = jnp.sum(jnp.where(low, 0.0, known), axis=1, keepdims=True) * share
    a11 = 1.1 * a11
    a22 = 1.1 * a22
    det = a11 * a22 - a12 * a12
    step_obj = (b1 * a22 - a12 * b2) / det
    step_probe = (a11 * b2 - a12 * b1) / det
    cover, _ = unpack_planes(totals, 2)
    cover = cover + 1.0
    scale = step_probe / cover
    for c in range(2):
        for m, numer in enumerate(unpack_planes(totals, c)):
            new_probe[c, m] = probe[c, m] + scale * numer
            if gradient is not None:
                gradient[c, m] = numer * lax.rsqrt(cover)
    return step_obj


def next_kernel(offsets, totals, padded, direction, probe, measured, right3, left3,
                top, middle, bottom, sums, new_padded, new_probe, accum):
    step = step_sizes(totals, probe, new_probe)
    new_padded[...] = padded[...] + step * direction[...]
    sweep(1, offsets, new_padded, new_probe, measured, right3, left3, sums, accum)
    top[...] = accum[:, :, :HALF]
    middle[...] = accum[:, :, HALF : HALF + SIZE]
    bottom[...] = accum[:, :, HALF + SIZE :]


def last_kernel(totals, padded, direction, probe, new_obj, new_probe, gradient):
    step = step_sizes(totals, probe, new_probe, gradient)
    low = lanes() < HALF
    rows = slice(HALF, HALF + SIZE)
    for c in range(2):
        old = join(low, padded[c, 0, rows], padded[c, 1, rows])
        new_obj[c] = old + step * direction[c]


def shape(*dims):
    return jax.ShapeDtypeStruct(dims, F32)


def call(kernel, ins, outs, scratch=(), in_hbm=()):
    vmem = pl.BlockSpec(memory_space=pltpu.VMEM)
    smem = pl.BlockSpec(memory_space=pltpu.SMEM)
    hbm = pl.BlockSpec(memory_space=pltpu.HBM)
    ins = [pltpu.with_memory_space_constraint(x, pltpu.HBM) if k in in_hbm else x for k, x in enumerate(ins)]
    specs = [hbm if k in in_hbm else smem if x.dtype == jnp.int32 else vmem for k, x in enumerate(ins)]
    return pl.pallas_call(
        kernel,
        in_specs=specs,
        out_specs=[smem if x.dtype == jnp.int32 else vmem for x in outs],
        out_shape=list(outs),
        scratch_shapes=list(scratch),
        compiler_params=pltpu.CompilerParams(vmem_limit_bytes=VMEM_LIMIT),
        name=getattr(kernel, "func", kernel).__name__,
    )(*ins)


def shift(block, rows, cols):
    n_row = math.prod(lax.axis_size(a) for a in ROW)
    n_col = math.prod(lax.axis_size(a) for a in COL)
    route = [
        (r * n_col + c, (r + rows) * n_col + c + cols)
        for r in range(n_row)
        for c in range(n_col)
        if 0 <= r + rows < n_row and 0 <= c + cols < n_col
    ]
    return lax.ppermute(block, ALL, route)


def exchange(block, axes):
    return lax.all_to_all(block, axes, 0, 0, tiled=True)


def size_of(axes):
    return math.prod(lax.axis_size(a) for a in axes)


def reduce_all(packed, probe, place_in_group):
    group, rest = size_of(SCATTER), size_of(REST)
    part = exchange(packed.reshape(group, 4, TILES, SIZE), SCATTER)
    (part,) = call(reduce_kernel, [part], [shape(rest, 4, TILES, SIZE)])
    part = exchange(part, REST)
    (part,) = call(strip_kernel, [place_in_group, part, probe], [shape(group, 3, TILES, SIZE)])
    return exchange(part, SCATTER).reshape(SIZE // TILES, 2, 3, TILES, SIZE)


def per_device(obj, probe, measured, offsets):
    right3, left3 = (jnp.asarray(t) for t in dft_tables())
    offsets = jnp.swapaxes(offsets[0, 0], 1, 2)
    r, c, half = (lax.axis_index(axes).astype(jnp.int32) for axes in (ROW, COL, ("zl",)))
    whole = 2 * SIZE
    place_in_group = jnp.stack([r, half])
    edges = jnp.stack([
        jnp.where(r == 0, HALF, 0),
        jnp.where(r == size_of(ROW) - 1, whole - HALF, whole),
        jnp.where(c == 0, HALF, 0),
        jnp.where(c == size_of(COL) - 1, whole - HALF, whole),
    ]).astype(jnp.int32)

    strip = shape(2, HALF + TILES, SIZE)
    side = shape(2, SIZE + TILES, SIZE)
    tile, to_below, to_above, offsets = call(
        send_kernel, [offsets, obj],
        [shape(2, SIZE, SIZE), strip, strip, jax.ShapeDtypeStruct(offsets.shape, jnp.int32)],
        [pltpu.SemaphoreType.DMA((4,))], in_hbm=(0, 1))
    above = shift(to_below, 1, 0)
    below = shift(to_above, -1, 0)
    to_left, to_right, codes = call(
        pack_kernel, [above, tile, below, to_below], [side, side, shape(TILES, SIZE)])
    from_left = shift(to_right, 0, 1)
    from_right = shift(to_left, 0, -1)
    staged = [measured, right3, left3]
    measured, right3, left3 = call(
        stage_kernel, [codes, *staged], [jax.ShapeDtypeStruct(x.shape, x.dtype) for x in staged],
        [pltpu.SemaphoreType.DMA((len(staged),))], in_hbm=(1, 2, 3))
    others = jnp.concatenate([from_left[0, SIZE:], codes, from_right[0, SIZE:]], axis=0).astype(jnp.int32)

    field = shape(2, 2, whole, SIZE)
    edge = shape(2, 2, HALF, SIZE)
    quads = shape(2, 2, SIZE, SIZE)
    planes = shape(2, MODES, SIZE, SIZE)
    sums_shape = shape(5, SIZE, SIZE)
    packed_shape = shape(SIZE // TILES, 2, 4, TILES, SIZE)

    top, bottom, sums, padded = call(
        first_kernel,
        [offsets, above, tile, below, from_left, from_right, probe, measured, right3, left3],
        [quads, quads, sums_shape, field],
        [pltpu.VMEM((2, 2, whole, SIZE), F32)],
    )
    from_above = shift(bottom, 1, 0)
    from_below = shift(top, -1, 0)
    cover, near = call(
        cover_kernel, [others, probe],
        [shape(2, whole, SIZE), jax.ShapeDtypeStruct((LIST_SIZE, 2), jnp.int32)],
        [pltpu.VMEM((3 * SIZE, SIZE), F32)])
    left, right = call(wide_fold_kernel, [top, bottom, from_above, from_below], [quads, quads])
    from_left = shift(right, 0, 1)
    from_right = shift(left, 0, -1)
    packed, direction = call(
        wide_merge_kernel,
        [edges, offsets, left, right, from_left, from_right, cover, padded, sums],
        [packed_shape, field],
        [pltpu.VMEM((2, 2, whole, SIZE), F32)],
    )
    totals = reduce_all(packed, probe, place_in_group)

    top, middle, bottom, sums, padded, probe = call(
        next_kernel,
        [offsets, totals, padded, direction, probe, measured, right3, left3],
        [edge, quads, edge, sums_shape, field, planes],
        [pltpu.VMEM((2, 2, whole, SIZE), F32)],
    )
    from_above = shift(bottom, 1, 0)
    from_below = shift(top, -1, 0)
    side = shape(2, HALF, SIZE)
    (cover,) = call(
        tile_cover_kernel, [near, probe], [shape(SIZE, SIZE)], [pltpu.VMEM((3 * SIZE, SIZE), F32)])
    middle, left, right = call(
        fold_kernel, [middle, from_above, from_below], [shape(2, SIZE, SIZE), side, side])
    from_left = shift(right, 0, 1)
    from_right = shift(left, 0, -1)
    packed, direction = call(
        merge_kernel,
        [near, middle, from_left, from_right, cover, padded, sums],
        [packed_shape, shape(2, SIZE, SIZE)],
        [pltpu.VMEM((2, 3 * SIZE, SIZE), F32), pltpu.VMEM((2, SIZE, SIZE), F32)],
    )
    totals = reduce_all(packed, probe, place_in_group)
    return tuple(call(
        last_kernel, [totals, padded, direction, probe], [shape(2, SIZE, SIZE), planes, planes]
    ))


def solution(mesh):
    parts = Mesh(mesh.devices.reshape(2, 4, 2, 4, 4, 2), ALL)
    in_specs = (P(None, ROW, COL), P(), P(ROW, COL), P(ROW, COL))
    out_specs = (P(None, ROW, COL), P(), P())
    return jax.shard_map(
        per_device, mesh=parts, in_specs=in_specs, out_specs=out_specs, check_vma=False
    )
```

```python
import itertools
import math
from functools import partial

import jax
import jax.numpy as jnp
import numpy as np
from jax import lax
from jax.experimental import pallas as pl
from jax.experimental.pallas import tpu as pltpu
from jax.sharding import Mesh, PartitionSpec as P

SIZE = 128
HALF = 64
MODES = 2
COUNT = 8
ROW = ("yl", "x", "c")
COL = ("yh", "zh", "zl")
ALL = ROW + COL
SCATTER = ROW + ("zl",)
REST = ("zh", "yh")
MARK = 1024
LIST_STEP = 4
LIST_SIZE = 9 * COUNT + 8
TILES = 8
VMEM_LIMIT = 16 * 1024 * 1024
F32 = jnp.float32
BF16 = jnp.bfloat16


def dft_tables():
    index = np.arange(SIZE)
    angle = 2.0 * math.pi / SIZE * (np.outer(index, index) % SIZE)
    real = np.cos(angle) / math.sqrt(SIZE)
    imag = -np.sin(angle) / math.sqrt(SIZE)
    right = np.block([[real, imag], [-imag, real]]).astype(np.float32)
    high = right.astype(jnp.bfloat16)
    low = (right - high.astype(np.float32)).astype(jnp.bfloat16)
    right3 = np.concatenate([high, high, low], axis=0)
    left3 = np.ascontiguousarray(right3.T)
    return right3, left3


def halves(x):
    high = x.astype(BF16)
    return high, (x - high.astype(F32)).astype(BF16)


def right_transform(fields, table):
    rows = []
    for real, imag in fields:
        rh, rl = halves(real)
        ih, il = halves(imag)
        rows.append(jnp.concatenate([rh, ih, rl, il, rh, ih], axis=1))
    out = jnp.dot(jnp.concatenate(rows, axis=0), table, preferred_element_type=F32)
    return [
        (out[SIZE * n : SIZE * (n + 1), :SIZE], out[SIZE * n : SIZE * (n + 1), SIZE:])
        for n in range(len(fields))
    ]


def left_transform(fields, table):
    cols = []
    for real, imag in fields:
        rh, rl = halves(real)
        ih, il = halves(imag)
        cols.append(jnp.concatenate([rh, ih, rl, il, rh, ih], axis=0))
    out = jnp.dot(table, jnp.concatenate(cols, axis=1), preferred_element_type=F32)
    return [
        (out[:SIZE, SIZE * n : SIZE * (n + 1)], out[SIZE:, SIZE * n : SIZE * (n + 1)])
        for n in range(len(fields))
    ]


def lanes():
    return lax.broadcasted_iota(jnp.int32, (SIZE, SIZE), 1)


def window(ref, lead, row, col):
    shift = lax.rem(SIZE - col, SIZE)
    rows = pl.ds(row, SIZE)
    mixed = jnp.where(lanes() >= col, ref[lead + (0, rows)], ref[lead + (1, rows)])
    return pltpu.roll(mixed, shift, 1)


def place(ref, plane, row, col, block):
    moved = pltpu.roll(block, lax.rem(col, SIZE), 1)
    first = lanes() >= col
    rows = pl.ds(row, SIZE)
    ref[plane, 0, rows] += jnp.where(first, moved, 0.0)
    ref[plane, 1, rows] += jnp.where(first, 0.0, moved)


def join(low, first, second):
    return jnp.where(low, pltpu.roll(first, HALF, 1), pltpu.roll(second, HALF, 1))


def pack_low(low, upper, lower):
    return jnp.where(low, upper, pltpu.roll(lower, HALF, 1))


def pack_high(low, upper, lower):
    return jnp.where(low, pltpu.roll(upper, HALF, 1), lower)


def low_lanes(rows):
    return lax.broadcasted_iota(jnp.int32, (rows, SIZE), 1) < HALF


def bounds(edges):
    return tuple(edges[k] for k in range(4))


def inside(limits, down, across, rows=SIZE):
    row_low, row_high, col_low, col_high = limits
    line = lax.broadcasted_iota(jnp.int32, (rows, SIZE), 0) + down
    lane = lax.broadcasted_iota(jnp.int32, (rows, SIZE), 1) + across
    return (line >= row_low) & (line < row_high) & (lane >= col_low) & (lane < col_high)


def evens():
    return tuple(lax.axis_index(axis) == 0 for axis in (ROW[-1], COL[-1]))


def sides(even, first, second):
    return jnp.where(even, second, first), jnp.where(even, first, second)


def pad_field(rows_in, own, cols_in, store):
    low = low_lanes(HALF)
    even_row, even_col = evens()
    for c in range(2):
        above, below = sides(even_row, *(x[c, :HALF] for x in rows_in))
        strips = (above, own[c, :HALF], own[c, HALF:], below)
        for k in range(4):
            half = slice(HALF * (k % 2), HALF * (k % 2 + 1))
            left, right = sides(even_col, *(x[c, half] for x in cols_in))
            if k < 2:
                right = pltpu.roll(right, HALF, 1)
            else:
                left = pltpu.roll(left, HALF, 1)
            mine = pltpu.roll(strips[k], HALF, 1)
            rows = slice(HALF * k, HALF * (k + 1))
            store(c, 0, rows, jnp.where(low, left, mine))
            store(c, 1, rows, jnp.where(low, mine, right))


def send_kernel(raw, own, tile, row_out0, row_out1, offsets, sems):
    strip = pl.ds(0, HALF)
    even_row, _ = evens()
    starts = [pl.multiple_of(jnp.where(even_row == (k == 0), HALF, 0), HALF) for k in range(2)]
    first = pltpu.make_async_copy(raw, offsets, sems.at[3])
    first.start()
    copies = [
        pltpu.make_async_copy(source, target, sems.at[k])
        for k, (source, target) in enumerate((
            (own.at[:, pl.ds(starts[0], HALF)], row_out0.at[:, strip]),
            (own.at[:, pl.ds(starts[1], HALF)], row_out1.at[:, strip]),
            (own, tile),
        ))
    ]
    for copy in copies:
        copy.start()
    line = lax.broadcasted_iota(jnp.int32, (TILES, SIZE), 0)
    lane = lax.broadcasted_iota(jnp.int32, (TILES, SIZE), 1)
    code = jnp.zeros((TILES, SIZE), jnp.int32)
    first.wait()
    batches, _, count = offsets.shape
    for b in range(batches):
        for k in range(count):
            for d in range(2):
                code = jnp.where(lane == (b * 2 + d) * count + k, offsets[b, d, k] + MARK, code)
    code = jnp.where(line == 0, code, 0).astype(F32)
    for c in range(2):
        row_out0[c, HALF:] = code
        row_out1[c, HALF:] = code
    for copy in copies:
        copy.wait()


def pack_kernel(row_in0, row_in1, own, mine, col_out0, col_out1, codes):
    low = low_lanes(HALF)
    even_row, even_col = evens()
    for c in range(2):
        above, below = sides(even_row, row_in0[c, :HALF], row_in1[c, :HALF])
        strips = (above, own[c, :HALF], own[c, HALF:], below)
        for k in range(2):
            rows = slice(HALF * k, HALF * (k + 1))
            to_left = pack_low(low, strips[k], strips[k + 2])
            to_right = pack_high(low, strips[k], strips[k + 2])
            col_out0[c, rows] = jnp.where(even_col, to_right, to_left)
            col_out1[c, rows] = jnp.where(even_col, to_left, to_right)
    above, below = sides(even_row, row_in0[0, HALF:], row_in1[0, HALF:])
    code = mine[0, HALF:] + pltpu.roll(above, 1, 0) + pltpu.roll(below, 2, 0)
    for c in range(2):
        col_out0[c, SIZE:] = code
        col_out1[c, SIZE:] = code
    codes[...] = code


def power_of(probe):
    return sum(probe[c, m] * probe[c, m] for c in range(2) for m in range(MODES))


def stage_kernel(codes, *refs):
    count = (len(refs) - 1) // 2
    sems = refs[-1]
    copies = [pltpu.make_async_copy(refs[k], refs[count + k], sems.at[k]) for k in range(count)]
    for copy in copies:
        copy.start()
    for copy in copies:
        copy.wait()


def sweep(batch, offsets, padded, probe, measured, right3, left3, sums, accum):
    accum[...] = jnp.zeros_like(accum)
    tr = right3[...]
    tl = left3[...]
    wins = []
    waves = []
    for j in range(COUNT):
        row, col = offsets[batch, 0, j] + HALF, offsets[batch, 1, j] + HALF
        wr = window(padded, (0,), row, col)
        wi = window(padded, (1,), row, col)
        wins.append((row, col, wr, wi))
        fields = []
        for m in range(MODES):
            pr, pi = probe[0, m], probe[1, m]
            fields.append((pr * wr - pi * wi, pr * wi + pi * wr))
        waves.append(right_transform(fields, tr))
    waves = [left_transform(fields, tl) for fields in waves]
    chis = []
    for j in range(COUNT):
        intensity = sum(r * r + i * i for r, i in waves[j])
        ratio = jnp.sqrt(measured[0, 0, batch, j]) / jnp.maximum(jnp.sqrt(intensity), 0.5) - 1.0
        chis.append(left_transform([(r * ratio, -(i * ratio)) for r, i in waves[j]], tl))
    chis = [right_transform(fields, tr) for fields in chis]
    totals = [0.0] * 5
    for j in range(COUNT):
        row, col, wr, wi = wins[j]
        cr = jnp.zeros((SIZE, SIZE), F32)
        ci = jnp.zeros((SIZE, SIZE), F32)
        for m in range(MODES):
            xr, xn = chis[j][m]
            pr, pi = probe[0, m], probe[1, m]
            cr += pr * xr - pi * xn
            ci -= pr * xn + pi * xr
            totals[m] = totals[m] + (wr * xr - wi * xn)
            totals[MODES + m] = totals[MODES + m] - (wr * xn + wi * xr)
        totals[2 * MODES] = totals[2 * MODES] + (wr * wr + wi * wi)
        place(accum, 0, row, col, cr)
        place(accum, 1, row, col, ci)
    for k in range(5):
        sums[k] = totals[k]


def first_kernel(offsets, row_in0, row_in1, own, col_in0, col_in1, probe, measured, right3, left3,
                 row_out0, row_out1, sums, padded, accum):
    def store(c, h, rows, value):
        padded[c, h, rows] = value

    pad_field((row_in0, row_in1), own, (col_in0, col_in1), store)
    sweep(0, offsets, padded, probe, measured, right3, left3, sums, accum)
    even_row, _ = evens()
    for c in range(2):
        for h in range(2):
            top, bottom = accum[c, h, :SIZE], accum[c, h, SIZE:]
            row_out0[c, h] = jnp.where(even_row, bottom, top)
            row_out1[c, h] = jnp.where(even_row, top, bottom)


def offset_of(others, batch, across, down, j, d):
    _, even_col = evens()
    tile = jnp.where(even_col, 2 - across, across)
    return others[TILES * tile + (1, 0, 2)[down], (batch * 2 + d) * COUNT + j] - MARK


def cover_kernel(others, probe, cover, near, light):
    none = jnp.zeros((SIZE, SIZE), F32)
    light[:SIZE] = none
    light[SIZE : 2 * SIZE] = power_of(probe)
    light[2 * SIZE :] = none
    lane = lanes()
    for v in range(2):
        total = [none, none]
        for down in (v, v + 1):
            for across in range(3):
                for j in range(COUNT):
                    row, col = (offset_of(others, 0, across, down, j, d) + HALF for d in range(2))
                    row = jnp.clip(row + SIZE * (down - 1 - v), -SIZE, SIZE)
                    col = jnp.clip(col, 0, SIZE)
                    moved = pltpu.roll(light[pl.ds(SIZE - row, SIZE)], lax.rem(col, SIZE), 1)
                    first = lane >= col
                    if across >= 1:
                        total[across - 1] = total[across - 1] + jnp.where(first, moved, 0.0)
                    if across <= 1:
                        total[across] = total[across] + jnp.where(first, 0.0, moved)
        for h in range(2):
            cover[h, v * SIZE : (v + 1) * SIZE] = total[h]

    count = jnp.int32(0)
    for down in range(3):
        for across in range(3):
            for j in range(COUNT):
                row = offset_of(others, 1, across, down, j, 0) + SIZE * (down - 1)
                col = offset_of(others, 1, across, down, j, 1) + SIZE * (across - 1)
                near[count, 0] = row
                near[count, 1] = col
                reaches = (jnp.abs(row) < SIZE) & (jnp.abs(col) < SIZE)
                count += reaches.astype(jnp.int32)
    for k in range(LIST_STEP):
        near[count + k, 0] = SIZE
        near[count + k, 1] = 0
    near[LIST_SIZE - 1, 0] = count


def wide_fold_kernel(row_out0, row_out1, row_in0, row_in1, col_out0, col_out1):
    even_row, even_col = evens()
    for c in range(2):
        top, bottom = [], []
        for h in range(2):
            upper, lower = sides(
                even_row, row_out0[c, h] + row_in0[c, h], row_out1[c, h] + row_in1[c, h])
            top.append(upper)
            bottom.append(lower)
        for v, (left, right) in enumerate((top, bottom)):
            col_out0[v, c] = jnp.where(even_col, right, left)
            col_out1[v, c] = jnp.where(even_col, left, right)


def pack_planes(packed, planes):
    strips = (SIZE // TILES, TILES, SIZE)
    upper = lax.rem(lax.broadcasted_iota(jnp.int32, (SIZE, SIZE), 0), TILES) < TILES // 2
    for q in range(len(planes) // 2):
        one, two = planes[2 * q], planes[2 * q + 1]
        packed[:, 0, q] = jnp.where(upper, one, pltpu.roll(two, TILES // 2, 0)).reshape(strips)
        packed[:, 1, q] = jnp.where(upper, pltpu.roll(one, SIZE - TILES // 2, 0), two).reshape(strips)


def unpack_planes(packed, q):
    upper = lax.rem(lax.broadcasted_iota(jnp.int32, (SIZE, SIZE), 0), TILES) < TILES // 2
    one, two = (packed[:, h, q].reshape(SIZE, SIZE) for h in range(2))
    return (jnp.where(upper, one, pltpu.roll(two, TILES // 2, 0)),
            jnp.where(upper, pltpu.roll(one, SIZE - TILES // 2, 0), two))


def pack_sums(packed, sums, overlap, a11, b1):
    turn = lax.rem(lax.broadcasted_iota(jnp.int32, (SIZE, SIZE), 0), TILES // 2)
    numbers = jnp.where(turn == 0, a11, jnp.where(turn == 1, b1, 0.0))
    pack_planes(packed, [sums[k] for k in range(5)] + [numbers] + list(overlap))


def wide_merge_kernel(edges, offsets, col_out0, col_out1, col_in0, col_in1, cover, padded, sums,
                      packed, direction, product):
    limits = bounds(edges)
    _, even_col = evens()
    a11 = jnp.zeros((1, SIZE), F32)
    b1 = jnp.zeros((1, SIZE), F32)
    for v in range(2):
        rows = slice(v * SIZE, (v + 1) * SIZE)
        mine_rows = lax.broadcasted_iota(jnp.int32, (SIZE, SIZE), 0) + v * SIZE
        totals = [sides(even_col, col_out0[v, c] + col_in0[v, c], col_out1[v, c] + col_in1[v, c]) for c in range(2)]
        for h in range(2):
            light = cover[h, rows]
            inverse = jnp.where(inside(limits, v * SIZE, h * SIZE), 1.0 / (light + 1.0), 0.0)
            dr, di = (totals[c][h] * inverse for c in range(2))
            direction[0, h, rows] = dr
            direction[1, h, rows] = di
            pr, pi = padded[0, h, rows], padded[1, h, rows]
            product[0, h, rows] = dr * pr + di * pi
            product[1, h, rows] = dr * pi - di * pr
            across = lanes() + h * SIZE
            mine = (mine_rows >= HALF) & (mine_rows < HALF + SIZE) & (across >= HALF) & (across < HALF + SIZE)
            power = jnp.where(mine, dr * dr + di * di, 0.0)
            a11 += jnp.sum(power * light, axis=0, keepdims=True)
            b1 += jnp.sum(power * (light + 1.0), axis=0, keepdims=True)
    overlap = [jnp.zeros((SIZE, SIZE), F32)] * 2
    for j in range(COUNT):
        row, col = offsets[0, 0, j] + HALF, offsets[0, 1, j] + HALF
        overlap = [overlap[c] + window(product, (c,), row, col) for c in range(2)]
    pack_sums(packed, sums, overlap, a11, b1)


def fold_kernel(middle, row_in0, row_in1, tile, col_out0, col_out1):
    low = low_lanes(HALF)
    even_row, even_col = evens()
    for k in range(2):
        upper, lower = [], []
        for h in range(2):
            above, below = sides(even_row, row_in0[k, h], row_in1[k, h])
            upper.append(middle[k, h, :HALF] + above)
            lower.append(middle[k, h, HALF:] + below)
        tile[k, :HALF] = join(low, *upper)
        tile[k, HALF:] = join(low, *lower)
        to_left = pack_low(low, upper[0], lower[0])
        to_right = pack_high(low, upper[1], lower[1])
        col_out0[k] = jnp.where(even_col, to_right, to_left)
        col_out1[k] = jnp.where(even_col, to_left, to_right)


def tile_cover_kernel(near, probe, cover, light):
    none = jnp.zeros((SIZE, SIZE), F32)
    light[:SIZE] = none
    light[SIZE : 2 * SIZE] = power_of(probe)
    light[2 * SIZE :] = none
    cover[...] = none
    lane = lanes()

    def body(step, carry):
        total = 0.0
        for g in range(LIST_STEP):
            down, across = near[step * LIST_STEP + g, 0], near[step * LIST_STEP + g, 1]
            source = lane - across
            valid = (source >= 0) & (source < SIZE)
            moved = pltpu.roll(light[pl.ds(SIZE - down, SIZE)], lax.rem(2 * SIZE + across, SIZE), 1)
            total = total + jnp.where(valid, moved, 0.0)
        cover[...] += total
        return carry

    lax.fori_loop(0, lax.div(near[LIST_SIZE - 1, 0] + LIST_STEP - 1, LIST_STEP), body, 0)


def merge_kernel(near, tile, col_in0, col_in1, cover, padded, sums,
                 packed, direction, product, overlap):
    low = low_lanes(HALF)
    lane = lanes()
    _, even_col = evens()
    a11 = jnp.zeros((1, SIZE), F32)
    b1 = jnp.zeros((1, SIZE), F32)
    for c in range(2):
        product[c, :SIZE] = jnp.zeros((SIZE, SIZE), F32)
        product[c, 2 * SIZE :] = jnp.zeros((SIZE, SIZE), F32)
        overlap[c] = jnp.zeros((SIZE, SIZE), F32)
    for v in range(2):
        rows = slice(HALF * v, HALF * (v + 1))
        full = []
        for k in range(2):
            left, right = sides(even_col, col_in0[k], col_in1[k])
            if v == 0:
                right = pltpu.roll(right, HALF, 1)
            else:
                left = pltpu.roll(left, HALF, 1)
            full.append(tile[k, rows] + jnp.where(low, left, right))
        gr, gi = full
        light = cover[rows]
        inverse = 1.0 / (light + 1.0)
        dr = gr * inverse
        di = gi * inverse
        direction[0, rows] = dr
        direction[1, rows] = di
        span = slice(HALF * (v + 1), HALF * (v + 2))
        pr = join(low, padded[0, 0, span], padded[0, 1, span])
        pi = join(low, padded[1, 0, span], padded[1, 1, span])
        inner = slice(SIZE + HALF * v, SIZE + HALF * (v + 1))
        product[0, inner] = dr * pr + di * pi
        product[1, inner] = dr * pi - di * pr
        power = dr * dr + di * di
        a11 += jnp.sum(power * light, axis=0, keepdims=True)
        b1 += jnp.sum(power * (light + 1.0), axis=0, keepdims=True)

    def body(step, carry):
        total = [0.0, 0.0]
        for g in range(LIST_STEP):
            down, across = near[step * LIST_STEP + g, 0], near[step * LIST_STEP + g, 1]
            turn = lax.rem(2 * SIZE - across, SIZE)
            source = lane + across
            valid = (source >= 0) & (source < SIZE)
            for c in range(2):
                moved = pltpu.roll(product[c, pl.ds(SIZE + down, SIZE)], turn, 1)
                total[c] = total[c] + jnp.where(valid, moved, 0.0)
        for c in range(2):
            overlap[c] += total[c]
        return carry

    lax.fori_loop(0, lax.div(near[LIST_SIZE - 1, 0] + LIST_STEP - 1, LIST_STEP), body, 0)

    pack_sums(packed, sums, (overlap[0], overlap[1]), a11, b1)


def add_all(parts):
    total = parts[0]
    for k in range(1, parts.shape[0]):
        total = total + parts[k]
    return total


def reduce_kernel(parts, out):
    total = add_all(parts)
    for k in range(out.shape[0]):
        out[k] = total


def strip_kernel(place_ref, parts, probe, out):
    total = add_all(parts)
    line = lax.broadcasted_iota(jnp.int32, (TILES, SIZE), 0)
    half = TILES // 2
    upper = line < half
    first = place_ref[1] == 0
    rows = pl.ds(pl.multiple_of(place_ref[0] * TILES, TILES), TILES)

    def turned(x):
        return pltpu.roll(x, half, 0)

    def both(x, of_upper):
        return jnp.where(upper == of_upper, x, turned(x))

    def modes(c):
        one, two = probe[c, 0, rows], probe[c, 1, rows]
        return jnp.where(upper, jnp.where(first, one, turned(one)), jnp.where(first, turned(two), two))

    pr, pi = modes(0), modes(1)
    cover = both(total[2], True)
    inverse = 1.0 / (cover + 1.0)
    dr, di = total[0] * inverse, total[1] * inverse
    cross = (pr * dr + pi * di) * both(total[3], True) - (pr * di - pi * dr) * both(total[3], False)
    power = dr * dr + di * di
    a22, b2, a12 = (
        jnp.sum(x, axis=0, keepdims=True) for x in (power * cover, power * (cover + 1.0), cross))
    a11, b1 = total[2, half : half + 1], total[2, half + 1 : half + 2]
    low = low_lanes(1)
    known = jnp.where(low, a11 + pltpu.roll(a11, HALF, 1), b1 + pltpu.roll(b1, HALF, 1))
    numbers = total[2]
    for k, term in enumerate((known, a22, b2, a12)):
        numbers = jnp.where(line == half + k, term, numbers)
    for k in range(out.shape[0]):
        out[k, 0] = total[0]
        out[k, 1] = total[1]
        out[k, 2] = numbers


def step_sizes(totals, probe, new_probe, gradient=None):
    numbers = jnp.zeros((TILES, SIZE), F32)
    for k in range(totals.shape[0]):
        numbers += totals[k, 0, 2] + totals[k, 1, 2]
    half = TILES // 2
    low = low_lanes(1)
    known, *rest = (numbers[half + k : half + k + 1] for k in range(4))
    a22, b2, a12 = (jnp.sum(x, axis=1, keepdims=True) for x in rest)
    share = 1.0 / (2 * totals.shape[0])
    a11 = jnp.sum(jnp.where(low, known, 0.0), axis=1, keepdims=True) * share
    b1 = jnp.sum(jnp.where(low, 0.0, known), axis=1, keepdims=True) * share
    a11 = 1.1 * a11
    a22 = 1.1 * a22
    det = a11 * a22 - a12 * a12
    step_obj = (b1 * a22 - a12 * b2) / det
    step_probe = (a11 * b2 - a12 * b1) / det
    cover, _ = unpack_planes(totals, 2)
    cover = cover + 1.0
    scale = step_probe / cover
    for c in range(2):
        for m, numer in enumerate(unpack_planes(totals, c)):
            new_probe[c, m] = probe[c, m] + scale * numer
            if gradient is not None:
                gradient[c, m] = numer * lax.rsqrt(cover)
    return step_obj


def next_kernel(offsets, totals, padded, direction, probe, measured, right3, left3,
                row_out0, middle, row_out1, sums, new_padded, new_probe, accum):
    step = step_sizes(totals, probe, new_probe)
    new_padded[...] = padded[...] + step * direction[...]
    sweep(1, offsets, new_padded, new_probe, measured, right3, left3, sums, accum)
    middle[...] = accum[:, :, HALF : HALF + SIZE]
    even_row, _ = evens()
    for c in range(2):
        for h in range(2):
            top, bottom = accum[c, h, :HALF], accum[c, h, HALF + SIZE :]
            row_out0[c, h] = jnp.where(even_row, bottom, top)
            row_out1[c, h] = jnp.where(even_row, top, bottom)


def last_kernel(totals, padded, direction, probe, new_obj, new_probe, gradient):
    step = step_sizes(totals, probe, new_probe, gradient)
    low = lanes() < HALF
    rows = slice(HALF, HALF + SIZE)
    for c in range(2):
        old = join(low, padded[c, 0, rows], padded[c, 1, rows])
        new_obj[c] = old + step * direction[c]


def shape(*dims):
    return jax.ShapeDtypeStruct(dims, F32)


def call(kernel, ins, outs, scratch=(), in_hbm=()):
    vmem = pl.BlockSpec(memory_space=pltpu.VMEM)
    smem = pl.BlockSpec(memory_space=pltpu.SMEM)
    hbm = pl.BlockSpec(memory_space=pltpu.HBM)
    ins = [pltpu.with_memory_space_constraint(x, pltpu.HBM) if k in in_hbm else x for k, x in enumerate(ins)]
    specs = [hbm if k in in_hbm else smem if x.dtype == jnp.int32 else vmem for k, x in enumerate(ins)]
    return pl.pallas_call(
        kernel,
        in_specs=specs,
        out_specs=[smem if x.dtype == jnp.int32 else vmem for x in outs],
        out_shape=list(outs),
        scratch_shapes=list(scratch),
        compiler_params=pltpu.CompilerParams(vmem_limit_bytes=VMEM_LIMIT),
        name=getattr(kernel, "func", kernel).__name__,
    )(*ins)


def swap(blocks, along):
    counts = size_of(ROW), size_of(COL)
    taken = []
    for k, block in enumerate(blocks):
        route = []
        for here in itertools.product(*(range(n) for n in counts)):
            there = list(here)
            there[along] += 1 if here[along] % 2 == k else -1
            if 0 <= there[along] < counts[along]:
                route.append((here[0] * counts[1] + here[1], there[0] * counts[1] + there[1]))
        taken.append(lax.ppermute(block, ALL, route))
    return taken


def exchange(block, axes):
    return lax.all_to_all(block, axes, 0, 0, tiled=True)


def size_of(axes):
    return math.prod(lax.axis_size(a) for a in axes)


def reduce_all(packed, probe, place_in_group):
    group, rest = size_of(SCATTER), size_of(REST)
    part = exchange(packed.reshape(group, 4, TILES, SIZE), SCATTER)
    (part,) = call(reduce_kernel, [part], [shape(rest, 4, TILES, SIZE)])
    part = exchange(part, REST)
    (part,) = call(strip_kernel, [place_in_group, part, probe], [shape(group, 3, TILES, SIZE)])
    return exchange(part, SCATTER).reshape(SIZE // TILES, 2, 3, TILES, SIZE)


def per_device(obj, probe, measured, offsets):
    right3, left3 = (jnp.asarray(t) for t in dft_tables())
    offsets = jnp.swapaxes(offsets[0, 0], 1, 2)
    r, c, half = (lax.axis_index(axes).astype(jnp.int32) for axes in (ROW, COL, ("zl",)))
    whole = 2 * SIZE
    place_in_group = jnp.stack([r, half])
    edges = jnp.stack([
        jnp.where(r == 0, HALF, 0),
        jnp.where(r == size_of(ROW) - 1, whole - HALF, whole),
        jnp.where(c == 0, HALF, 0),
        jnp.where(c == size_of(COL) - 1, whole - HALF, whole),
    ]).astype(jnp.int32)

    strip = shape(2, HALF + TILES, SIZE)
    side = shape(2, SIZE + TILES, SIZE)
    tile, *row_out, offsets = call(
        send_kernel, [offsets, obj],
        [shape(2, SIZE, SIZE), strip, strip, jax.ShapeDtypeStruct(offsets.shape, jnp.int32)],
        [pltpu.SemaphoreType.DMA((4,))], in_hbm=(0, 1))
    row_in = swap(row_out, 0)
    *col_out, codes = call(
        pack_kernel, [*row_in, tile, row_out[0]], [side, side, shape(TILES, SIZE)])
    col_in = swap(col_out, 1)
    staged = [measured, right3, left3]
    measured, right3, left3 = call(
        stage_kernel, [codes, *staged], [jax.ShapeDtypeStruct(x.shape, x.dtype) for x in staged],
        [pltpu.SemaphoreType.DMA((len(staged),))], in_hbm=(1, 2, 3))
    others = jnp.concatenate([col_in[0][0, SIZE:], codes, col_in[1][0, SIZE:]], axis=0).astype(jnp.int32)

    field = shape(2, 2, whole, SIZE)
    edge = shape(2, 2, HALF, SIZE)
    quads = shape(2, 2, SIZE, SIZE)
    planes = shape(2, MODES, SIZE, SIZE)
    sums_shape = shape(5, SIZE, SIZE)
    packed_shape = shape(SIZE // TILES, 2, 4, TILES, SIZE)

    *row_out, sums, padded = call(
        first_kernel,
        [offsets, *row_in, tile, *col_in, probe, measured, right3, left3],
        [quads, quads, sums_shape, field],
        [pltpu.VMEM((2, 2, whole, SIZE), F32)],
    )
    row_in = swap(row_out, 0)
    cover, near = call(
        cover_kernel, [others, probe],
        [shape(2, whole, SIZE), jax.ShapeDtypeStruct((LIST_SIZE, 2), jnp.int32)],
        [pltpu.VMEM((3 * SIZE, SIZE), F32)])
    col_out = call(wide_fold_kernel, [*row_out, *row_in], [quads, quads])
    col_in = swap(col_out, 1)
    packed, direction = call(
        wide_merge_kernel,
        [edges, offsets, *col_out, *col_in, cover, padded, sums],
        [packed_shape, field],
        [pltpu.VMEM((2, 2, whole, SIZE), F32)],
    )
    totals = reduce_all(packed, probe, place_in_group)

    row_out0, middle, row_out1, sums, padded, probe = call(
        next_kernel,
        [offsets, totals, padded, direction, probe, measured, right3, left3],
        [edge, quads, edge, sums_shape, field, planes],
        [pltpu.VMEM((2, 2, whole, SIZE), F32)],
    )
    row_in = swap((row_out0, row_out1), 0)
    side = shape(2, HALF, SIZE)
    (cover,) = call(
        tile_cover_kernel, [near, probe], [shape(SIZE, SIZE)], [pltpu.VMEM((3 * SIZE, SIZE), F32)])
    middle, *col_out = call(
        fold_kernel, [middle, *row_in], [shape(2, SIZE, SIZE), side, side])
    col_in = swap(col_out, 1)
    packed, direction = call(
        merge_kernel,
        [near, middle, *col_in, cover, padded, sums],
        [packed_shape, shape(2, SIZE, SIZE)],
        [pltpu.VMEM((2, 3 * SIZE, SIZE), F32), pltpu.VMEM((2, SIZE, SIZE), F32)],
    )
    totals = reduce_all(packed, probe, place_in_group)
    return tuple(call(
        last_kernel, [totals, padded, direction, probe], [shape(2, SIZE, SIZE), planes, planes]
    ))


def solution(mesh):
    parts = Mesh(mesh.devices.reshape(2, 4, 2, 4, 4, 2), ALL)
    in_specs = (P(None, ROW, COL), P(), P(ROW, COL), P(ROW, COL))
    out_specs = (P(None, ROW, COL), P(), P())
    return jax.shard_map(
        per_device, mesh=parts, in_specs=in_specs, out_specs=out_specs, check_vma=False
    )
```

```python
import itertools
import math
from functools import partial

import jax
import jax.numpy as jnp
import numpy as np
from jax import lax
from jax.experimental import pallas as pl
from jax.experimental.pallas import tpu as pltpu
from jax.sharding import Mesh, PartitionSpec as P

SIZE = 128
HALF = 64
MODES = 2
COUNT = 8
ROW = ("yl", "x", "c")
COL = ("yh", "zh", "zl")
ALL = ROW + COL
SCATTER = ROW + ("zl",)
REST = ("zh", "yh")
MARK = 1024
LIST_STEP = 4
LIST_SIZE = 9 * COUNT + 8
TILES = 8
VMEM_LIMIT = 16 * 1024 * 1024
F32 = jnp.float32
BF16 = jnp.bfloat16


def dft_tables():
    index = np.arange(SIZE)
    angle = 2.0 * math.pi / SIZE * (np.outer(index, index) % SIZE)
    real = np.cos(angle) / math.sqrt(SIZE)
    imag = -np.sin(angle) / math.sqrt(SIZE)
    right = np.block([[real, imag], [-imag, real]]).astype(np.float32)
    high = right.astype(jnp.bfloat16)
    low = (right - high.astype(np.float32)).astype(jnp.bfloat16)
    right3 = np.concatenate([high, high, low], axis=0)
    left3 = np.ascontiguousarray(right3.T)
    return right3, left3


def halves(x):
    high = x.astype(BF16)
    return high, (x - high.astype(F32)).astype(BF16)


def right_transform(fields, table):
    rows = []
    for real, imag in fields:
        rh, rl = halves(real)
        ih, il = halves(imag)
        rows.append(jnp.concatenate([rh, ih, rl, il, rh, ih], axis=1))
    out = jnp.dot(jnp.concatenate(rows, axis=0), table, preferred_element_type=F32)
    return [
        (out[SIZE * n : SIZE * (n + 1), :SIZE], out[SIZE * n : SIZE * (n + 1), SIZE:])
        for n in range(len(fields))
    ]


def left_transform(fields, table):
    cols = []
    for real, imag in fields:
        rh, rl = halves(real)
        ih, il = halves(imag)
        cols.append(jnp.concatenate([rh, ih, rl, il, rh, ih], axis=0))
    out = jnp.dot(table, jnp.concatenate(cols, axis=1), preferred_element_type=F32)
    return [
        (out[:SIZE, SIZE * n : SIZE * (n + 1)], out[SIZE:, SIZE * n : SIZE * (n + 1)])
        for n in range(len(fields))
    ]


def lanes():
    return lax.broadcasted_iota(jnp.int32, (SIZE, SIZE), 1)


def window(ref, lead, row, col):
    shift = lax.rem(SIZE - col, SIZE)
    rows = pl.ds(row, SIZE)
    mixed = jnp.where(lanes() >= col, ref[lead + (0, rows)], ref[lead + (1, rows)])
    return pltpu.roll(mixed, shift, 1)


def place(ref, plane, row, col, block):
    moved = pltpu.roll(block, lax.rem(col, SIZE), 1)
    first = lanes() >= col
    rows = pl.ds(row, SIZE)
    ref[plane, 0, rows] += jnp.where(first, moved, 0.0)
    ref[plane, 1, rows] += jnp.where(first, 0.0, moved)


def join(low, first, second):
    return jnp.where(low, pltpu.roll(first, HALF, 1), pltpu.roll(second, HALF, 1))


def pack_low(low, upper, lower):
    return jnp.where(low, upper, pltpu.roll(lower, HALF, 1))


def pack_high(low, upper, lower):
    return jnp.where(low, pltpu.roll(upper, HALF, 1), lower)


def low_lanes(rows):
    return lax.broadcasted_iota(jnp.int32, (rows, SIZE), 1) < HALF


def bounds(edges):
    return tuple(edges[k] for k in range(4))


def inside(limits, down, across, rows=SIZE):
    row_low, row_high, col_low, col_high = limits
    line = lax.broadcasted_iota(jnp.int32, (rows, SIZE), 0) + down
    lane = lax.broadcasted_iota(jnp.int32, (rows, SIZE), 1) + across
    return (line >= row_low) & (line < row_high) & (lane >= col_low) & (lane < col_high)


def odds():
    return tuple(lax.axis_index(axis) == 1 for axis in (ROW[-1], COL[-1]))


def sides(odd, first, second):
    return jnp.where(odd, second, first), jnp.where(odd, first, second)


def pad_field(rows_in, own, cols_in, store):
    low = low_lanes(HALF)
    odd_row, odd_col = odds()
    for c in range(2):
        above, below = sides(odd_row, *(x[c, :HALF] for x in rows_in))
        strips = (above, own[c, :HALF], own[c, HALF:], below)
        for k in range(4):
            half = slice(HALF * (k % 2), HALF * (k % 2 + 1))
            left, right = sides(odd_col, *(x[c, half] for x in cols_in))
            if k < 2:
                right = pltpu.roll(right, HALF, 1)
            else:
                left = pltpu.roll(left, HALF, 1)
            mine = pltpu.roll(strips[k], HALF, 1)
            rows = slice(HALF * k, HALF * (k + 1))
            store(c, 0, rows, jnp.where(low, left, mine))
            store(c, 1, rows, jnp.where(low, mine, right))


def send_kernel(raw, own, tile, row_out0, row_out1, offsets, sems):
    strip = pl.ds(0, HALF)
    odd_row, _ = odds()
    starts = [pl.multiple_of(jnp.where(odd_row == (k == 0), HALF, 0), HALF) for k in range(2)]
    first = pltpu.make_async_copy(raw, offsets, sems.at[3])
    first.start()
    copies = [
        pltpu.make_async_copy(source, target, sems.at[k])
        for k, (source, target) in enumerate((
            (own.at[:, pl.ds(starts[0], HALF)], row_out0.at[:, strip]),
            (own.at[:, pl.ds(starts[1], HALF)], row_out1.at[:, strip]),
            (own, tile),
        ))
    ]
    for copy in copies:
        copy.start()
    line = lax.broadcasted_iota(jnp.int32, (TILES, SIZE), 0)
    lane = lax.broadcasted_iota(jnp.int32, (TILES, SIZE), 1)
    code = jnp.zeros((TILES, SIZE), jnp.int32)
    first.wait()
    batches, _, count = offsets.shape
    for b in range(batches):
        for k in range(count):
            for d in range(2):
                code = jnp.where(lane == (b * 2 + d) * count + k, offsets[b, d, k] + MARK, code)
    code = jnp.where(line == 0, code, 0).astype(F32)
    for c in range(2):
        row_out0[c, HALF:] = code
        row_out1[c, HALF:] = code
    for copy in copies:
        copy.wait()


def pack_kernel(row_in0, row_in1, own, mine, col_out0, col_out1, codes):
    low = low_lanes(HALF)
    odd_row, odd_col = odds()
    for c in range(2):
        above, below = sides(odd_row, row_in0[c, :HALF], row_in1[c, :HALF])
        strips = (above, own[c, :HALF], own[c, HALF:], below)
        for k in range(2):
            rows = slice(HALF * k, HALF * (k + 1))
            to_left = pack_low(low, strips[k], strips[k + 2])
            to_right = pack_high(low, strips[k], strips[k + 2])
            col_out0[c, rows] = jnp.where(odd_col, to_right, to_left)
            col_out1[c, rows] = jnp.where(odd_col, to_left, to_right)
    above, below = sides(odd_row, row_in0[0, HALF:], row_in1[0, HALF:])
    code = mine[0, HALF:] + pltpu.roll(above, 1, 0) + pltpu.roll(below, 2, 0)
    for c in range(2):
        col_out0[c, SIZE:] = code
        col_out1[c, SIZE:] = code
    codes[...] = code


def power_of(probe):
    return sum(probe[c, m] * probe[c, m] for c in range(2) for m in range(MODES))


def stage_kernel(codes, *refs):
    count = (len(refs) - 1) // 2
    sems = refs[-1]
    copies = [pltpu.make_async_copy(refs[k], refs[count + k], sems.at[k]) for k in range(count)]
    for copy in copies:
        copy.start()
    for copy in copies:
        copy.wait()


def sweep(batch, offsets, padded, probe, measured, right3, left3, sums, accum):
    accum[...] = jnp.zeros_like(accum)
    tr = right3[...]
    tl = left3[...]
    wins = []
    waves = []
    for j in range(COUNT):
        row, col = offsets[batch, 0, j] + HALF, offsets[batch, 1, j] + HALF
        wr = window(padded, (0,), row, col)
        wi = window(padded, (1,), row, col)
        wins.append((row, col, wr, wi))
        fields = []
        for m in range(MODES):
            pr, pi = probe[0, m], probe[1, m]
            fields.append((pr * wr - pi * wi, pr * wi + pi * wr))
        waves.append(right_transform(fields, tr))
    waves = [left_transform(fields, tl) for fields in waves]
    chis = []
    for j in range(COUNT):
        intensity = sum(r * r + i * i for r, i in waves[j])
        ratio = jnp.sqrt(measured[0, 0, batch, j]) / jnp.maximum(jnp.sqrt(intensity), 0.5) - 1.0
        chis.append(left_transform([(r * ratio, -(i * ratio)) for r, i in waves[j]], tl))
    chis = [right_transform(fields, tr) for fields in chis]
    totals = [0.0] * 5
    for j in range(COUNT):
        row, col, wr, wi = wins[j]
        cr = jnp.zeros((SIZE, SIZE), F32)
        ci = jnp.zeros((SIZE, SIZE), F32)
        for m in range(MODES):
            xr, xn = chis[j][m]
            pr, pi = probe[0, m], probe[1, m]
            cr += pr * xr - pi * xn
            ci -= pr * xn + pi * xr
            totals[m] = totals[m] + (wr * xr - wi * xn)
            totals[MODES + m] = totals[MODES + m] - (wr * xn + wi * xr)
        totals[2 * MODES] = totals[2 * MODES] + (wr * wr + wi * wi)
        place(accum, 0, row, col, cr)
        place(accum, 1, row, col, ci)
    for k in range(5):
        sums[k] = totals[k]


def first_kernel(offsets, row_in0, row_in1, own, col_in0, col_in1, probe, measured, right3, left3,
                 row_out0, row_out1, sums, padded, accum):
    def store(c, h, rows, value):
        padded[c, h, rows] = value

    pad_field((row_in0, row_in1), own, (col_in0, col_in1), store)
    sweep(0, offsets, padded, probe, measured, right3, left3, sums, accum)
    odd_row, _ = odds()
    for c in range(2):
        for h in range(2):
            top, bottom = accum[c, h, :SIZE], accum[c, h, SIZE:]
            row_out0[c, h] = jnp.where(odd_row, bottom, top)
            row_out1[c, h] = jnp.where(odd_row, top, bottom)


def offset_of(others, batch, across, down, j, d):
    _, odd_col = odds()
    tile = jnp.where(odd_col, 2 - across, across)
    return others[TILES * tile + (1, 0, 2)[down], (batch * 2 + d) * COUNT + j] - MARK


def cover_kernel(others, probe, cover, near, light):
    none = jnp.zeros((SIZE, SIZE), F32)
    light[:SIZE] = none
    light[SIZE : 2 * SIZE] = power_of(probe)
    light[2 * SIZE :] = none
    lane = lanes()
    for v in range(2):
        total = [none, none]
        for down in (v, v + 1):
            for across in range(3):
                for j in range(COUNT):
                    row, col = (offset_of(others, 0, across, down, j, d) + HALF for d in range(2))
                    row = jnp.clip(row + SIZE * (down - 1 - v), -SIZE, SIZE)
                    col = jnp.clip(col, 0, SIZE)
                    moved = pltpu.roll(light[pl.ds(SIZE - row, SIZE)], lax.rem(col, SIZE), 1)
                    first = lane >= col
                    if across >= 1:
                        total[across - 1] = total[across - 1] + jnp.where(first, moved, 0.0)
                    if across <= 1:
                        total[across] = total[across] + jnp.where(first, 0.0, moved)
        for h in range(2):
            cover[h, v * SIZE : (v + 1) * SIZE] = total[h]

    count = jnp.int32(0)
    for down in range(3):
        for across in range(3):
            for j in range(COUNT):
                row = offset_of(others, 1, across, down, j, 0) + SIZE * (down - 1)
                col = offset_of(others, 1, across, down, j, 1) + SIZE * (across - 1)
                near[count, 0] = row
                near[count, 1] = col
                reaches = (jnp.abs(row) < SIZE) & (jnp.abs(col) < SIZE)
                count += reaches.astype(jnp.int32)
    for k in range(LIST_STEP):
        near[count + k, 0] = SIZE
        near[count + k, 1] = 0
    near[LIST_SIZE - 1, 0] = count


def wide_fold_kernel(row_out0, row_out1, row_in0, row_in1, col_out0, col_out1):
    odd_row, odd_col = odds()
    for c in range(2):
        top, bottom = [], []
        for h in range(2):
            upper, lower = sides(
                odd_row, row_out0[c, h] + row_in0[c, h], row_out1[c, h] + row_in1[c, h])
            top.append(upper)
            bottom.append(lower)
        for v, (left, right) in enumerate((top, bottom)):
            col_out0[v, c] = jnp.where(odd_col, right, left)
            col_out1[v, c] = jnp.where(odd_col, left, right)


def pack_planes(packed, planes):
    strips = (SIZE // TILES, TILES, SIZE)
    upper = lax.rem(lax.broadcasted_iota(jnp.int32, (SIZE, SIZE), 0), TILES) < TILES // 2
    for q in range(len(planes) // 2):
        one, two = planes[2 * q], planes[2 * q + 1]
        packed[:, 0, q] = jnp.where(upper, one, pltpu.roll(two, TILES // 2, 0)).reshape(strips)
        packed[:, 1, q] = jnp.where(upper, pltpu.roll(one, SIZE - TILES // 2, 0), two).reshape(strips)


def unpack_planes(packed, q):
    upper = lax.rem(lax.broadcasted_iota(jnp.int32, (SIZE, SIZE), 0), TILES) < TILES // 2
    one, two = (packed[:, h, q].reshape(SIZE, SIZE) for h in range(2))
    return (jnp.where(upper, one, pltpu.roll(two, TILES // 2, 0)),
            jnp.where(upper, pltpu.roll(one, SIZE - TILES // 2, 0), two))


def pack_sums(packed, sums, overlap, a11, b1):
    turn = lax.rem(lax.broadcasted_iota(jnp.int32, (SIZE, SIZE), 0), TILES // 2)
    numbers = jnp.where(turn == 0, a11, jnp.where(turn == 1, b1, 0.0))
    pack_planes(packed, [sums[k] for k in range(5)] + [numbers] + list(overlap))


def wide_merge_kernel(edges, offsets, col_out0, col_out1, col_in0, col_in1, cover, padded, sums,
                      packed, direction, product):
    limits = bounds(edges)
    _, odd_col = odds()
    a11 = jnp.zeros((1, SIZE), F32)
    b1 = jnp.zeros((1, SIZE), F32)
    for v in range(2):
        rows = slice(v * SIZE, (v + 1) * SIZE)
        mine_rows = lax.broadcasted_iota(jnp.int32, (SIZE, SIZE), 0) + v * SIZE
        totals = [sides(odd_col, col_out0[v, c] + col_in0[v, c], col_out1[v, c] + col_in1[v, c]) for c in range(2)]
        for h in range(2):
            light = cover[h, rows]
            inverse = jnp.where(inside(limits, v * SIZE, h * SIZE), 1.0 / (light + 1.0), 0.0)
            dr, di = (totals[c][h] * inverse for c in range(2))
            direction[0, h, rows] = dr
            direction[1, h, rows] = di
            pr, pi = padded[0, h, rows], padded[1, h, rows]
            product[0, h, rows] = dr * pr + di * pi
            product[1, h, rows] = dr * pi - di * pr
            across = lanes() + h * SIZE
            mine = (mine_rows >= HALF) & (mine_rows < HALF + SIZE) & (across >= HALF) & (across < HALF + SIZE)
            power = jnp.where(mine, dr * dr + di * di, 0.0)
            a11 += jnp.sum(power * light, axis=0, keepdims=True)
            b1 += jnp.sum(power * (light + 1.0), axis=0, keepdims=True)
    overlap = [jnp.zeros((SIZE, SIZE), F32)] * 2
    for j in range(COUNT):
        row, col = offsets[0, 0, j] + HALF, offsets[0, 1, j] + HALF
        overlap = [overlap[c] + window(product, (c,), row, col) for c in range(2)]
    pack_sums(packed, sums, overlap, a11, b1)


def fold_kernel(middle, row_in0, row_in1, tile, col_out0, col_out1):
    low = low_lanes(HALF)
    odd_row, odd_col = odds()
    for k in range(2):
        upper, lower = [], []
        for h in range(2):
            above, below = sides(odd_row, row_in0[k, h], row_in1[k, h])
            upper.append(middle[k, h, :HALF] + above)
            lower.append(middle[k, h, HALF:] + below)
        tile[k, :HALF] = join(low, *upper)
        tile[k, HALF:] = join(low, *lower)
        to_left = pack_low(low, upper[0], lower[0])
        to_right = pack_high(low, upper[1], lower[1])
        col_out0[k] = jnp.where(odd_col, to_right, to_left)
        col_out1[k] = jnp.where(odd_col, to_left, to_right)


def tile_cover_kernel(near, probe, cover, light):
    none = jnp.zeros((SIZE, SIZE), F32)
    light[:SIZE] = none
    light[SIZE : 2 * SIZE] = power_of(probe)
    light[2 * SIZE :] = none
    cover[...] = none
    lane = lanes()

    def body(step, carry):
        total = 0.0
        for g in range(LIST_STEP):
            down, across = near[step * LIST_STEP + g, 0], near[step * LIST_STEP + g, 1]
            source = lane - across
            valid = (source >= 0) & (source < SIZE)
            moved = pltpu.roll(light[pl.ds(SIZE - down, SIZE)], lax.rem(2 * SIZE + across, SIZE), 1)
            total = total + jnp.where(valid, moved, 0.0)
        cover[...] += total
        return carry

    lax.fori_loop(0, lax.div(near[LIST_SIZE - 1, 0] + LIST_STEP - 1, LIST_STEP), body, 0)


def merge_kernel(near, tile, col_in0, col_in1, cover, padded, sums,
                 packed, direction, product, overlap):
    low = low_lanes(HALF)
    lane = lanes()
    _, odd_col = odds()
    a11 = jnp.zeros((1, SIZE), F32)
    b1 = jnp.zeros((1, SIZE), F32)
    for c in range(2):
        product[c, :SIZE] = jnp.zeros((SIZE, SIZE), F32)
        product[c, 2 * SIZE :] = jnp.zeros((SIZE, SIZE), F32)
        overlap[c] = jnp.zeros((SIZE, SIZE), F32)
    for v in range(2):
        rows = slice(HALF * v, HALF * (v + 1))
        full = []
        for k in range(2):
            left, right = sides(odd_col, col_in0[k], col_in1[k])
            if v == 0:
                right = pltpu.roll(right, HALF, 1)
            else:
                left = pltpu.roll(left, HALF, 1)
            full.append(tile[k, rows] + jnp.where(low, left, right))
        gr, gi = full
        light = cover[rows]
        inverse = 1.0 / (light + 1.0)
        dr = gr * inverse
        di = gi * inverse
        direction[0, rows] = dr
        direction[1, rows] = di
        span = slice(HALF * (v + 1), HALF * (v + 2))
        pr = join(low, padded[0, 0, span], padded[0, 1, span])
        pi = join(low, padded[1, 0, span], padded[1, 1, span])
        inner = slice(SIZE + HALF * v, SIZE + HALF * (v + 1))
        product[0, inner] = dr * pr + di * pi
        product[1, inner] = dr * pi - di * pr
        power = dr * dr + di * di
        a11 += jnp.sum(power * light, axis=0, keepdims=True)
        b1 += jnp.sum(power * (light + 1.0), axis=0, keepdims=True)

    def body(step, carry):
        total = [0.0, 0.0]
        for g in range(LIST_STEP):
            down, across = near[step * LIST_STEP + g, 0], near[step * LIST_STEP + g, 1]
            turn = lax.rem(2 * SIZE - across, SIZE)
            source = lane + across
            valid = (source >= 0) & (source < SIZE)
            for c in range(2):
                moved = pltpu.roll(product[c, pl.ds(SIZE + down, SIZE)], turn, 1)
                total[c] = total[c] + jnp.where(valid, moved, 0.0)
        for c in range(2):
            overlap[c] += total[c]
        return carry

    lax.fori_loop(0, lax.div(near[LIST_SIZE - 1, 0] + LIST_STEP - 1, LIST_STEP), body, 0)

    pack_sums(packed, sums, (overlap[0], overlap[1]), a11, b1)


def add_all(parts):
    total = parts[0]
    for k in range(1, parts.shape[0]):
        total = total + parts[k]
    return total


def reduce_kernel(parts, out):
    total = add_all(parts)
    for k in range(out.shape[0]):
        out[k] = total


def strip_kernel(place_ref, parts, probe, out):
    total = add_all(parts)
    line = lax.broadcasted_iota(jnp.int32, (TILES, SIZE), 0)
    half = TILES // 2
    upper = line < half
    first = place_ref[1] == 0
    rows = pl.ds(pl.multiple_of(place_ref[0] * TILES, TILES), TILES)

    def turned(x):
        return pltpu.roll(x, half, 0)

    def both(x, of_upper):
        return jnp.where(upper == of_upper, x, turned(x))

    def modes(c):
        one, two = probe[c, 0, rows], probe[c, 1, rows]
        return jnp.where(upper, jnp.where(first, one, turned(one)), jnp.where(first, turned(two), two))

    pr, pi = modes(0), modes(1)
    cover = both(total[2], True)
    inverse = 1.0 / (cover + 1.0)
    dr, di = total[0] * inverse, total[1] * inverse
    cross = (pr * dr + pi * di) * both(total[3], True) - (pr * di - pi * dr) * both(total[3], False)
    power = dr * dr + di * di
    a22, b2, a12 = (
        jnp.sum(x, axis=0, keepdims=True) for x in (power * cover, power * (cover + 1.0), cross))
    a11, b1 = total[2, half : half + 1], total[2, half + 1 : half + 2]
    low = low_lanes(1)
    known = jnp.where(low, a11 + pltpu.roll(a11, HALF, 1), b1 + pltpu.roll(b1, HALF, 1))
    numbers = total[2]
    for k, term in enumerate((known, a22, b2, a12)):
        numbers = jnp.where(line == half + k, term, numbers)
    for k in range(out.shape[0]):
        out[k, 0] = total[0]
        out[k, 1] = total[1]
        out[k, 2] = numbers


def step_sizes(totals, probe, new_probe, gradient=None):
    numbers = jnp.zeros((TILES, SIZE), F32)
    for k in range(totals.shape[0]):
        numbers += totals[k, 0, 2] + totals[k, 1, 2]
    half = TILES // 2
    low = low_lanes(1)
    known, *rest = (numbers[half + k : half + k + 1] for k in range(4))
    a22, b2, a12 = (jnp.sum(x, axis=1, keepdims=True) for x in rest)
    share = 1.0 / (2 * totals.shape[0])
    a11 = jnp.sum(jnp.where(low, known, 0.0), axis=1, keepdims=True) * share
    b1 = jnp.sum(jnp.where(low, 0.0, known), axis=1, keepdims=True) * share
    a11 = 1.1 * a11
    a22 = 1.1 * a22
    det = a11 * a22 - a12 * a12
    step_obj = (b1 * a22 - a12 * b2) / det
    step_probe = (a11 * b2 - a12 * b1) / det
    cover, _ = unpack_planes(totals, 2)
    cover = cover + 1.0
    scale = step_probe / cover
    for c in range(2):
        for m, numer in enumerate(unpack_planes(totals, c)):
            new_probe[c, m] = probe[c, m] + scale * numer
            if gradient is not None:
                gradient[c, m] = numer * lax.rsqrt(cover)
    return step_obj


def next_kernel(offsets, totals, padded, direction, probe, measured, right3, left3,
                row_out0, middle, row_out1, sums, new_padded, new_probe, accum):
    step = step_sizes(totals, probe, new_probe)
    new_padded[...] = padded[...] + step * direction[...]
    sweep(1, offsets, new_padded, new_probe, measured, right3, left3, sums, accum)
    middle[...] = accum[:, :, HALF : HALF + SIZE]
    odd_row, _ = odds()
    for c in range(2):
        for h in range(2):
            top, bottom = accum[c, h, :HALF], accum[c, h, HALF + SIZE :]
            row_out0[c, h] = jnp.where(odd_row, bottom, top)
            row_out1[c, h] = jnp.where(odd_row, top, bottom)


def last_kernel(totals, padded, direction, probe, new_obj, new_probe, gradient):
    step = step_sizes(totals, probe, new_probe, gradient)
    low = lanes() < HALF
    rows = slice(HALF, HALF + SIZE)
    for c in range(2):
        old = join(low, padded[c, 0, rows], padded[c, 1, rows])
        new_obj[c] = old + step * direction[c]


def shape(*dims):
    return jax.ShapeDtypeStruct(dims, F32)


def call(kernel, ins, outs, scratch=(), in_hbm=()):
    vmem = pl.BlockSpec(memory_space=pltpu.VMEM)
    smem = pl.BlockSpec(memory_space=pltpu.SMEM)
    hbm = pl.BlockSpec(memory_space=pltpu.HBM)
    ins = [pltpu.with_memory_space_constraint(x, pltpu.HBM) if k in in_hbm else x for k, x in enumerate(ins)]
    specs = [hbm if k in in_hbm else smem if x.dtype == jnp.int32 else vmem for k, x in enumerate(ins)]
    return pl.pallas_call(
        kernel,
        in_specs=specs,
        out_specs=[smem if x.dtype == jnp.int32 else vmem for x in outs],
        out_shape=list(outs),
        scratch_shapes=list(scratch),
        compiler_params=pltpu.CompilerParams(vmem_limit_bytes=VMEM_LIMIT),
        name=getattr(kernel, "func", kernel).__name__,
    )(*ins)


def swap(blocks, along):
    counts = size_of(ROW), size_of(COL)
    taken = []
    for k, block in enumerate(blocks):
        route = []
        for here in itertools.product(*(range(n) for n in counts)):
            there = list(here)
            there[along] += 1 if here[along] % 2 != k else -1
            if 0 <= there[along] < counts[along]:
                route.append((here[0] * counts[1] + here[1], there[0] * counts[1] + there[1]))
        taken.append(lax.ppermute(block, ALL, route))
    return taken


def exchange(block, axes):
    return lax.all_to_all(block, axes, 0, 0, tiled=True)


def size_of(axes):
    return math.prod(lax.axis_size(a) for a in axes)


def reduce_all(packed, probe, place_in_group):
    group, rest = size_of(SCATTER), size_of(REST)
    part = exchange(packed.reshape(group, 4, TILES, SIZE), SCATTER)
    (part,) = call(reduce_kernel, [part], [shape(rest, 4, TILES, SIZE)])
    part = exchange(part, REST)
    (part,) = call(strip_kernel, [place_in_group, part, probe], [shape(group, 3, TILES, SIZE)])
    return exchange(part, SCATTER).reshape(SIZE // TILES, 2, 3, TILES, SIZE)


def per_device(obj, probe, measured, offsets):
    right3, left3 = (jnp.asarray(t) for t in dft_tables())
    offsets = jnp.swapaxes(offsets[0, 0], 1, 2)
    r, c, half = (lax.axis_index(axes).astype(jnp.int32) for axes in (ROW, COL, ("zl",)))
    whole = 2 * SIZE
    place_in_group = jnp.stack([r, half])
    edges = jnp.stack([
        jnp.where(r == 0, HALF, 0),
        jnp.where(r == size_of(ROW) - 1, whole - HALF, whole),
        jnp.where(c == 0, HALF, 0),
        jnp.where(c == size_of(COL) - 1, whole - HALF, whole),
    ]).astype(jnp.int32)

    strip = shape(2, HALF + TILES, SIZE)
    side = shape(2, SIZE + TILES, SIZE)
    tile, *row_out, offsets = call(
        send_kernel, [offsets, obj],
        [shape(2, SIZE, SIZE), strip, strip, jax.ShapeDtypeStruct(offsets.shape, jnp.int32)],
        [pltpu.SemaphoreType.DMA((4,))], in_hbm=(0, 1))
    row_in = swap(row_out, 0)
    *col_out, codes = call(
        pack_kernel, [*row_in, tile, row_out[1]], [side, side, shape(TILES, SIZE)])
    col_in = swap(col_out, 1)
    staged = [measured, right3, left3]
    measured, right3, left3 = call(
        stage_kernel, [codes, *staged], [jax.ShapeDtypeStruct(x.shape, x.dtype) for x in staged],
        [pltpu.SemaphoreType.DMA((len(staged),))], in_hbm=(1, 2, 3))
    others = jnp.concatenate([col_in[0][0, SIZE:], codes, col_in[1][0, SIZE:]], axis=0).astype(jnp.int32)

    field = shape(2, 2, whole, SIZE)
    edge = shape(2, 2, HALF, SIZE)
    quads = shape(2, 2, SIZE, SIZE)
    planes = shape(2, MODES, SIZE, SIZE)
    sums_shape = shape(5, SIZE, SIZE)
    packed_shape = shape(SIZE // TILES, 2, 4, TILES, SIZE)

    *row_out, sums, padded = call(
        first_kernel,
        [offsets, *row_in, tile, *col_in, probe, measured, right3, left3],
        [quads, quads, sums_shape, field],
        [pltpu.VMEM((2, 2, whole, SIZE), F32)],
    )
    row_in = swap(row_out, 0)
    cover, near = call(
        cover_kernel, [others, probe],
        [shape(2, whole, SIZE), jax.ShapeDtypeStruct((LIST_SIZE, 2), jnp.int32)],
        [pltpu.VMEM((3 * SIZE, SIZE), F32)])
    col_out = call(wide_fold_kernel, [*row_out, *row_in], [quads, quads])
    col_in = swap(col_out, 1)
    packed, direction = call(
        wide_merge_kernel,
        [edges, offsets, *col_out, *col_in, cover, padded, sums],
        [packed_shape, field],
        [pltpu.VMEM((2, 2, whole, SIZE), F32)],
    )
    totals = reduce_all(packed, probe, place_in_group)

    row_out0, middle, row_out1, sums, padded, probe = call(
        next_kernel,
        [offsets, totals, padded, direction, probe, measured, right3, left3],
        [edge, quads, edge, sums_shape, field, planes],
        [pltpu.VMEM((2, 2, whole, SIZE), F32)],
    )
    row_in = swap((row_out0, row_out1), 0)
    side = shape(2, HALF, SIZE)
    (cover,) = call(
        tile_cover_kernel, [near, probe], [shape(SIZE, SIZE)], [pltpu.VMEM((3 * SIZE, SIZE), F32)])
    middle, *col_out = call(
        fold_kernel, [middle, *row_in], [shape(2, SIZE, SIZE), side, side])
    col_in = swap(col_out, 1)
    packed, direction = call(
        merge_kernel,
        [near, middle, *col_in, cover, padded, sums],
        [packed_shape, shape(2, SIZE, SIZE)],
        [pltpu.VMEM((2, 3 * SIZE, SIZE), F32), pltpu.VMEM((2, SIZE, SIZE), F32)],
    )
    totals = reduce_all(packed, probe, place_in_group)
    return tuple(call(
        last_kernel, [totals, padded, direction, probe], [shape(2, SIZE, SIZE), planes, planes]
    ))


def solution(mesh):
    parts = Mesh(mesh.devices.reshape(2, 4, 2, 4, 4, 2), ALL)
    in_specs = (P(None, ROW, COL), P(), P(ROW, COL), P(ROW, COL))
    out_specs = (P(None, ROW, COL), P(), P())
    return jax.shard_map(
        per_device, mesh=parts, in_specs=in_specs, out_specs=out_specs, check_vma=False
    )
```

```python
import itertools
import math
from functools import partial

import jax
import jax.numpy as jnp
import numpy as np
from jax import lax
from jax.experimental import pallas as pl
from jax.experimental.pallas import tpu as pltpu
from jax.sharding import Mesh, PartitionSpec as P

SIZE = 128
HALF = 64
MODES = 2
COUNT = 8
ROW = ("yl", "x", "c")
COL = ("yh", "zh", "zl")
ALL = ROW + COL
SCATTER = ("x", "c", "yl", "zl")
REST = ("zh", "yh")
MARK = 1024
LIST_STEP = 4
LIST_SIZE = 9 * COUNT + 8
TILES = 8
VMEM_LIMIT = 16 * 1024 * 1024
F32 = jnp.float32
BF16 = jnp.bfloat16


def dft_tables():
    index = np.arange(SIZE)
    angle = 2.0 * math.pi / SIZE * (np.outer(index, index) % SIZE)
    real = np.cos(angle) / math.sqrt(SIZE)
    imag = -np.sin(angle) / math.sqrt(SIZE)
    right = np.block([[real, imag], [-imag, real]]).astype(np.float32)
    high = right.astype(jnp.bfloat16)
    low = (right - high.astype(np.float32)).astype(jnp.bfloat16)
    right3 = np.concatenate([high, high, low], axis=0)
    left3 = np.ascontiguousarray(right3.T)
    return right3, left3


def halves(x):
    high = x.astype(BF16)
    return high, (x - high.astype(F32)).astype(BF16)


def right_transform(fields, table):
    rows = []
    for real, imag in fields:
        rh, rl = halves(real)
        ih, il = halves(imag)
        rows.append(jnp.concatenate([rh, ih, rl, il, rh, ih], axis=1))
    out = jnp.dot(jnp.concatenate(rows, axis=0), table, preferred_element_type=F32)
    return [
        (out[SIZE * n : SIZE * (n + 1), :SIZE], out[SIZE * n : SIZE * (n + 1), SIZE:])
        for n in range(len(fields))
    ]


def left_transform(fields, table):
    cols = []
    for real, imag in fields:
        rh, rl = halves(real)
        ih, il = halves(imag)
        cols.append(jnp.concatenate([rh, ih, rl, il, rh, ih], axis=0))
    out = jnp.dot(table, jnp.concatenate(cols, axis=1), preferred_element_type=F32)
    return [
        (out[:SIZE, SIZE * n : SIZE * (n + 1)], out[SIZE:, SIZE * n : SIZE * (n + 1)])
        for n in range(len(fields))
    ]


def lanes():
    return lax.broadcasted_iota(jnp.int32, (SIZE, SIZE), 1)


def window(ref, lead, row, col):
    shift = lax.rem(SIZE - col, SIZE)
    rows = pl.ds(row, SIZE)
    mixed = jnp.where(lanes() >= col, ref[lead + (0, rows)], ref[lead + (1, rows)])
    return pltpu.roll(mixed, shift, 1)


def place(ref, plane, row, col, block):
    moved = pltpu.roll(block, lax.rem(col, SIZE), 1)
    first = lanes() >= col
    rows = pl.ds(row, SIZE)
    ref[plane, 0, rows] += jnp.where(first, moved, 0.0)
    ref[plane, 1, rows] += jnp.where(first, 0.0, moved)


def join(low, first, second):
    return jnp.where(low, pltpu.roll(first, HALF, 1), pltpu.roll(second, HALF, 1))


def pack_low(low, upper, lower):
    return jnp.where(low, upper, pltpu.roll(lower, HALF, 1))


def pack_high(low, upper, lower):
    return jnp.where(low, pltpu.roll(upper, HALF, 1), lower)


def low_lanes(rows):
    return lax.broadcasted_iota(jnp.int32, (rows, SIZE), 1) < HALF


def bounds(edges):
    return tuple(edges[k] for k in range(4))


def inside(limits, down, across, rows=SIZE):
    row_low, row_high, col_low, col_high = limits
    line = lax.broadcasted_iota(jnp.int32, (rows, SIZE), 0) + down
    lane = lax.broadcasted_iota(jnp.int32, (rows, SIZE), 1) + across
    return (line >= row_low) & (line < row_high) & (lane >= col_low) & (lane < col_high)


def odds():
    return tuple(lax.axis_index(axis) == 1 for axis in (ROW[-1], COL[-1]))


def sides(odd, first, second):
    return jnp.where(odd, second, first), jnp.where(odd, first, second)


def send_kernel(raw, own, tile, col_out0, col_out1, offsets, sems):
    copies = [
        pltpu.make_async_copy(source, target, sems.at[k])
        for k, (source, target) in enumerate(((raw, offsets), (own, tile)))
    ]
    for copy in copies:
        copy.start()
    line = lax.broadcasted_iota(jnp.int32, (TILES, SIZE), 0)
    lane = lax.broadcasted_iota(jnp.int32, (TILES, SIZE), 1)
    code = jnp.zeros((TILES, SIZE), jnp.int32)
    copies[0].wait()
    batches, _, count = offsets.shape
    for b in range(batches):
        for k in range(count):
            for d in range(2):
                code = jnp.where(lane == (b * 2 + d) * count + k, offsets[b, d, k] + MARK, code)
    code = jnp.where(line == 0, code, 0).astype(F32)
    copies[1].wait()
    low = low_lanes(HALF)
    _, odd_col = odds()
    for c in range(2):
        upper, lower = tile[c, :HALF], tile[c, HALF:]
        to_left = pack_low(low, upper, lower)
        to_right = pack_high(low, upper, lower)
        col_out0[c, :HALF] = jnp.where(odd_col, to_right, to_left)
        col_out1[c, :HALF] = jnp.where(odd_col, to_left, to_right)
        col_out0[c, HALF:] = code
        col_out1[c, HALF:] = code


def spread_kernel(col_in0, col_in1, tile, mine, staged, middle, row_out0, row_out1, codes):
    low = low_lanes(HALF)
    odd_row, odd_col = odds()
    left, right = sides(odd_col, col_in0[0, HALF:], col_in1[0, HALF:])
    code = mine[0, HALF:] + pltpu.roll(left, 1, 0) + pltpu.roll(right, 2, 0)
    codes[...] = code
    for c in range(2):
        left, right = sides(odd_col, col_in0[c, :HALF], col_in1[c, :HALF])
        ends = []
        for k in range(2):
            rows = slice(HALF * k, HALF * (k + 1))
            own = pltpu.roll(tile[c, rows], HALF, 1)
            first = jnp.where(low, left if k == 0 else pltpu.roll(left, HALF, 1), own)
            second = jnp.where(low, own, right if k == 1 else pltpu.roll(right, HALF, 1))
            middle[c, 0, rows] = first
            middle[c, 1, rows] = second
            ends.append((first, second))
        for h in range(2):
            top, bottom = ends[0][h], ends[1][h]
            row_out0[c, h, :HALF] = jnp.where(odd_row, bottom, top)
            row_out1[c, h, :HALF] = jnp.where(odd_row, top, bottom)
            row_out0[c, h, HALF:] = code
            row_out1[c, h, HALF:] = code


def power_of(probe):
    return sum(probe[c, m] * probe[c, m] for c in range(2) for m in range(MODES))


def stage_kernel(tile, *refs):
    count = (len(refs) - 1) // 2
    sems = refs[-1]
    copies = [pltpu.make_async_copy(refs[k], refs[count + k], sems.at[k]) for k in range(count)]
    for copy in copies:
        copy.start()
    for copy in copies:
        copy.wait()


def sweep(batch, offsets, padded, probe, measured, right3, left3, sums, accum):
    accum[...] = jnp.zeros_like(accum)
    tr = right3[...]
    tl = left3[...]
    wins = []
    waves = []
    for j in range(COUNT):
        row, col = offsets[batch, 0, j] + HALF, offsets[batch, 1, j] + HALF
        wr = window(padded, (0,), row, col)
        wi = window(padded, (1,), row, col)
        wins.append((row, col, wr, wi))
        fields = []
        for m in range(MODES):
            pr, pi = probe[0, m], probe[1, m]
            fields.append((pr * wr - pi * wi, pr * wi + pi * wr))
        waves.append(right_transform(fields, tr))
    waves = [left_transform(fields, tl) for fields in waves]
    chis = []
    for j in range(COUNT):
        intensity = sum(r * r + i * i for r, i in waves[j])
        ratio = jnp.sqrt(measured[0, 0, batch, j]) / jnp.maximum(jnp.sqrt(intensity), 0.5) - 1.0
        chis.append(left_transform([(r * ratio, -(i * ratio)) for r, i in waves[j]], tl))
    chis = [right_transform(fields, tr) for fields in chis]
    totals = [0.0] * 5
    for j in range(COUNT):
        row, col, wr, wi = wins[j]
        cr = jnp.zeros((SIZE, SIZE), F32)
        ci = jnp.zeros((SIZE, SIZE), F32)
        for m in range(MODES):
            xr, xn = chis[j][m]
            pr, pi = probe[0, m], probe[1, m]
            cr += pr * xr - pi * xn
            ci -= pr * xn + pi * xr
            totals[m] = totals[m] + (wr * xr - wi * xn)
            totals[MODES + m] = totals[MODES + m] - (wr * xn + wi * xr)
        totals[2 * MODES] = totals[2 * MODES] + (wr * wr + wi * wi)
        place(accum, 0, row, col, cr)
        place(accum, 1, row, col, ci)
    for k in range(5):
        sums[k] = totals[k]


def first_kernel(offsets, row_in0, row_in1, middle, probe, measured, right3, left3,
                 row_out0, row_out1, sums, padded, accum):
    odd_row, _ = odds()
    for c in range(2):
        for h in range(2):
            above, below = sides(odd_row, row_in0[c, h, :HALF], row_in1[c, h, :HALF])
            padded[c, h, :HALF] = above
            padded[c, h, HALF : HALF + SIZE] = middle[c, h]
            padded[c, h, HALF + SIZE :] = below
    sweep(0, offsets, padded, probe, measured, right3, left3, sums, accum)
    for c in range(2):
        for h in range(2):
            top, bottom = accum[c, h, :SIZE], accum[c, h, SIZE:]
            row_out0[c, h] = jnp.where(odd_row, bottom, top)
            row_out1[c, h] = jnp.where(odd_row, top, bottom)


def offset_of(others, batch, across, down, j, d):
    odd_row, _ = odds()
    tile = jnp.where(odd_row, 2 - down, down)
    return others[TILES * tile + (1, 0, 2)[across], (batch * 2 + d) * COUNT + j] - MARK


def cover_kernel(others, probe, cover, near, light):
    none = jnp.zeros((SIZE, SIZE), F32)
    light[:SIZE] = none
    light[SIZE : 2 * SIZE] = power_of(probe)
    light[2 * SIZE :] = none
    lane = lanes()
    for v in range(2):
        total = [none, none]
        for down in (v, v + 1):
            for across in range(3):
                for j in range(COUNT):
                    row, col = (offset_of(others, 0, across, down, j, d) + HALF for d in range(2))
                    row = jnp.clip(row + SIZE * (down - 1 - v), -SIZE, SIZE)
                    col = jnp.clip(col, 0, SIZE)
                    moved = pltpu.roll(light[pl.ds(SIZE - row, SIZE)], lax.rem(col, SIZE), 1)
                    first = lane >= col
                    if across >= 1:
                        total[across - 1] = total[across - 1] + jnp.where(first, moved, 0.0)
                    if across <= 1:
                        total[across] = total[across] + jnp.where(first, 0.0, moved)
        for h in range(2):
            cover[h, v * SIZE : (v + 1) * SIZE] = total[h]

    count = jnp.int32(0)
    for down in range(3):
        for across in range(3):
            for j in range(COUNT):
                row = offset_of(others, 1, across, down, j, 0) + SIZE * (down - 1)
                col = offset_of(others, 1, across, down, j, 1) + SIZE * (across - 1)
                near[count, 0] = row
                near[count, 1] = col
                reaches = (jnp.abs(row) < SIZE) & (jnp.abs(col) < SIZE)
                count += reaches.astype(jnp.int32)
    for k in range(LIST_STEP):
        near[count + k, 0] = SIZE
        near[count + k, 1] = 0
    near[LIST_SIZE - 1, 0] = count


def wide_fold_kernel(row_out0, row_out1, row_in0, row_in1, col_out0, col_out1):
    odd_row, odd_col = odds()
    for c in range(2):
        top, bottom = [], []
        for h in range(2):
            upper, lower = sides(
                odd_row, row_out0[c, h] + row_in0[c, h], row_out1[c, h] + row_in1[c, h])
            top.append(upper)
            bottom.append(lower)
        for v, (left, right) in enumerate((top, bottom)):
            col_out0[v, c] = jnp.where(odd_col, right, left)
            col_out1[v, c] = jnp.where(odd_col, left, right)


def pack_planes(packed, planes):
    strips = (SIZE // TILES, TILES, SIZE)
    upper = lax.rem(lax.broadcasted_iota(jnp.int32, (SIZE, SIZE), 0), TILES) < TILES // 2
    for q in range(len(planes) // 2):
        one, two = planes[2 * q], planes[2 * q + 1]
        packed[:, 0, q] = jnp.where(upper, one, pltpu.roll(two, TILES // 2, 0)).reshape(strips)
        packed[:, 1, q] = jnp.where(upper, pltpu.roll(one, SIZE - TILES // 2, 0), two).reshape(strips)


def unpack_planes(packed, q):
    upper = lax.rem(lax.broadcasted_iota(jnp.int32, (SIZE, SIZE), 0), TILES) < TILES // 2
    one, two = (packed[:, h, q].reshape(SIZE, SIZE) for h in range(2))
    return (jnp.where(upper, one, pltpu.roll(two, TILES // 2, 0)),
            jnp.where(upper, pltpu.roll(one, SIZE - TILES // 2, 0), two))


def pack_sums(packed, sums, overlap, a11, b1):
    turn = lax.rem(lax.broadcasted_iota(jnp.int32, (SIZE, SIZE), 0), TILES // 2)
    numbers = jnp.where(turn == 0, a11, jnp.where(turn == 1, b1, 0.0))
    pack_planes(packed, [sums[k] for k in range(5)] + [numbers] + list(overlap))


def wide_merge_kernel(edges, offsets, col_out0, col_out1, col_in0, col_in1, cover, padded, sums,
                      packed, direction, product):
    limits = bounds(edges)
    _, odd_col = odds()
    a11 = jnp.zeros((1, SIZE), F32)
    b1 = jnp.zeros((1, SIZE), F32)
    for v in range(2):
        rows = slice(v * SIZE, (v + 1) * SIZE)
        mine_rows = lax.broadcasted_iota(jnp.int32, (SIZE, SIZE), 0) + v * SIZE
        totals = [sides(odd_col, col_out0[v, c] + col_in0[v, c], col_out1[v, c] + col_in1[v, c]) for c in range(2)]
        for h in range(2):
            light = cover[h, rows]
            inverse = jnp.where(inside(limits, v * SIZE, h * SIZE), 1.0 / (light + 1.0), 0.0)
            dr, di = (totals[c][h] * inverse for c in range(2))
            direction[0, h, rows] = dr
            direction[1, h, rows] = di
            pr, pi = padded[0, h, rows], padded[1, h, rows]
            product[0, h, rows] = dr * pr + di * pi
            product[1, h, rows] = dr * pi - di * pr
            across = lanes() + h * SIZE
            mine = (mine_rows >= HALF) & (mine_rows < HALF + SIZE) & (across >= HALF) & (across < HALF + SIZE)
            power = jnp.where(mine, dr * dr + di * di, 0.0)
            a11 += jnp.sum(power * light, axis=0, keepdims=True)
            b1 += jnp.sum(power * (light + 1.0), axis=0, keepdims=True)
    overlap = [jnp.zeros((SIZE, SIZE), F32)] * 2
    for j in range(COUNT):
        row, col = offsets[0, 0, j] + HALF, offsets[0, 1, j] + HALF
        overlap = [overlap[c] + window(product, (c,), row, col) for c in range(2)]
    pack_sums(packed, sums, overlap, a11, b1)


def fold_kernel(middle, row_in0, row_in1, cover, tile, col_out0, col_out1):
    low = low_lanes(HALF)
    odd_row, odd_col = odds()
    for k in range(2):
        upper, lower = [], []
        for h in range(2):
            above, below = sides(odd_row, row_in0[k, h], row_in1[k, h])
            upper.append(middle[k, h, :HALF] + above)
            lower.append(middle[k, h, HALF:] + below)
        tile[k, :HALF] = join(low, *upper)
        tile[k, HALF:] = join(low, *lower)
        to_left = pack_low(low, upper[0], lower[0])
        to_right = pack_high(low, upper[1], lower[1])
        col_out0[k] = jnp.where(odd_col, to_right, to_left)
        col_out1[k] = jnp.where(odd_col, to_left, to_right)


def tile_cover_kernel(near, probe, cover, light):
    none = jnp.zeros((SIZE, SIZE), F32)
    light[:SIZE] = none
    light[SIZE : 2 * SIZE] = power_of(probe)
    light[2 * SIZE :] = none
    cover[...] = none
    lane = lanes()

    def body(step, carry):
        total = 0.0
        for g in range(LIST_STEP):
            down, across = near[step * LIST_STEP + g, 0], near[step * LIST_STEP + g, 1]
            source = lane - across
            valid = (source >= 0) & (source < SIZE)
            moved = pltpu.roll(light[pl.ds(SIZE - down, SIZE)], lax.rem(2 * SIZE + across, SIZE), 1)
            total = total + jnp.where(valid, moved, 0.0)
        cover[...] += total
        return carry

    lax.fori_loop(0, lax.div(near[LIST_SIZE - 1, 0] + LIST_STEP - 1, LIST_STEP), body, 0)


def merge_kernel(near, tile, col_in0, col_in1, cover, padded, sums,
                 packed, direction, product, overlap):
    low = low_lanes(HALF)
    lane = lanes()
    _, odd_col = odds()
    a11 = jnp.zeros((1, SIZE), F32)
    b1 = jnp.zeros((1, SIZE), F32)
    for c in range(2):
        product[c, :SIZE] = jnp.zeros((SIZE, SIZE), F32)
        product[c, 2 * SIZE :] = jnp.zeros((SIZE, SIZE), F32)
        overlap[c] = jnp.zeros((SIZE, SIZE), F32)
    for v in range(2):
        rows = slice(HALF * v, HALF * (v + 1))
        full = []
        for k in range(2):
            left, right = sides(odd_col, col_in0[k], col_in1[k])
            if v == 0:
                right = pltpu.roll(right, HALF, 1)
            else:
                left = pltpu.roll(left, HALF, 1)
            full.append(tile[k, rows] + jnp.where(low, left, right))
        gr, gi = full
        light = cover[rows]
        inverse = 1.0 / (light + 1.0)
        dr = gr * inverse
        di = gi * inverse
        direction[0, rows] = dr
        direction[1, rows] = di
        span = slice(HALF * (v + 1), HALF * (v + 2))
        pr = join(low, padded[0, 0, span], padded[0, 1, span])
        pi = join(low, padded[1, 0, span], padded[1, 1, span])
        inner = slice(SIZE + HALF * v, SIZE + HALF * (v + 1))
        product[0, inner] = dr * pr + di * pi
        product[1, inner] = dr * pi - di * pr
        power = dr * dr + di * di
        a11 += jnp.sum(power * light, axis=0, keepdims=True)
        b1 += jnp.sum(power * (light + 1.0), axis=0, keepdims=True)

    def body(step, carry):
        total = [0.0, 0.0]
        for g in range(LIST_STEP):
            down, across = near[step * LIST_STEP + g, 0], near[step * LIST_STEP + g, 1]
            turn = lax.rem(2 * SIZE - across, SIZE)
            source = lane + across
            valid = (source >= 0) & (source < SIZE)
            for c in range(2):
                moved = pltpu.roll(product[c, pl.ds(SIZE + down, SIZE)], turn, 1)
                total[c] = total[c] + jnp.where(valid, moved, 0.0)
        for c in range(2):
            overlap[c] += total[c]
        return carry

    lax.fori_loop(0, lax.div(near[LIST_SIZE - 1, 0] + LIST_STEP - 1, LIST_STEP), body, 0)

    pack_sums(packed, sums, (overlap[0], overlap[1]), a11, b1)


def add_all(parts):
    total = parts[0]
    for k in range(1, parts.shape[0]):
        total = total + parts[k]
    return total


def reduce_kernel(parts, out):
    total = add_all(parts)
    for k in range(out.shape[0]):
        out[k] = total


def strip_kernel(place_ref, parts, probe, out):
    total = add_all(parts)
    line = lax.broadcasted_iota(jnp.int32, (TILES, SIZE), 0)
    half = TILES // 2
    upper = line < half
    first = place_ref[1] == 0
    rows = pl.ds(pl.multiple_of(place_ref[0] * TILES, TILES), TILES)

    def turned(x):
        return pltpu.roll(x, half, 0)

    def both(x, of_upper):
        return jnp.where(upper == of_upper, x, turned(x))

    def modes(c):
        one, two = probe[c, 0, rows], probe[c, 1, rows]
        return jnp.where(upper, jnp.where(first, one, turned(one)), jnp.where(first, turned(two), two))

    pr, pi = modes(0), modes(1)
    cover = both(total[2], True)
    inverse = 1.0 / (cover + 1.0)
    dr, di = total[0] * inverse, total[1] * inverse
    cross = (pr * dr + pi * di) * both(total[3], True) - (pr * di - pi * dr) * both(total[3], False)
    power = dr * dr + di * di
    a22, b2, a12 = (
        jnp.sum(x, axis=0, keepdims=True) for x in (power * cover, power * (cover + 1.0), cross))
    a11, b1 = total[2, half : half + 1], total[2, half + 1 : half + 2]
    low = low_lanes(1)
    known = jnp.where(low, a11 + pltpu.roll(a11, HALF, 1), b1 + pltpu.roll(b1, HALF, 1))
    numbers = total[2]
    for k, term in enumerate((known, a22, b2, a12)):
        numbers = jnp.where(line == half + k, term, numbers)
    for k in range(out.shape[0]):
        out[k, 0] = total[0]
        out[k, 1] = total[1]
        out[k, 2] = numbers


def step_sizes(totals, probe, new_probe, gradient=None):
    numbers = jnp.zeros((TILES, SIZE), F32)
    for k in range(totals.shape[0]):
        numbers += totals[k, 0, 2] + totals[k, 1, 2]
    half = TILES // 2
    low = low_lanes(1)
    known, *rest = (numbers[half + k : half + k + 1] for k in range(4))
    a22, b2, a12 = (jnp.sum(x, axis=1, keepdims=True) for x in rest)
    share = 1.0 / (2 * totals.shape[0])
    a11 = jnp.sum(jnp.where(low, known, 0.0), axis=1, keepdims=True) * share
    b1 = jnp.sum(jnp.where(low, 0.0, known), axis=1, keepdims=True) * share
    a11 = 1.1 * a11
    a22 = 1.1 * a22
    det = a11 * a22 - a12 * a12
    step_obj = (b1 * a22 - a12 * b2) / det
    step_probe = (a11 * b2 - a12 * b1) / det
    cover, _ = unpack_planes(totals, 2)
    cover = cover + 1.0
    scale = step_probe / cover
    for c in range(2):
        for m, numer in enumerate(unpack_planes(totals, c)):
            new_probe[c, m] = probe[c, m] + scale * numer
            if gradient is not None:
                gradient[c, m] = numer * lax.rsqrt(cover)
    return step_obj


def next_kernel(offsets, totals, padded, direction, probe, measured, right3, left3,
                row_out0, middle, row_out1, sums, new_padded, new_probe, accum):
    step = step_sizes(totals, probe, new_probe)
    new_padded[...] = padded[...] + step * direction[...]
    sweep(1, offsets, new_padded, new_probe, measured, right3, left3, sums, accum)
    middle[...] = accum[:, :, HALF : HALF + SIZE]
    odd_row, _ = odds()
    for c in range(2):
        for h in range(2):
            top, bottom = accum[c, h, :HALF], accum[c, h, HALF + SIZE :]
            row_out0[c, h] = jnp.where(odd_row, bottom, top)
            row_out1[c, h] = jnp.where(odd_row, top, bottom)


def last_kernel(totals, padded, direction, probe, new_obj, new_probe, gradient):
    step = step_sizes(totals, probe, new_probe, gradient)
    low = lanes() < HALF
    rows = slice(HALF, HALF + SIZE)
    for c in range(2):
        old = join(low, padded[c, 0, rows], padded[c, 1, rows])
        new_obj[c] = old + step * direction[c]


def shape(*dims):
    return jax.ShapeDtypeStruct(dims, F32)


def call(kernel, ins, outs, scratch=(), in_hbm=()):
    vmem = pl.BlockSpec(memory_space=pltpu.VMEM)
    smem = pl.BlockSpec(memory_space=pltpu.SMEM)
    hbm = pl.BlockSpec(memory_space=pltpu.HBM)
    ins = [pltpu.with_memory_space_constraint(x, pltpu.HBM) if k in in_hbm else x for k, x in enumerate(ins)]
    specs = [hbm if k in in_hbm else smem if x.dtype == jnp.int32 else vmem for k, x in enumerate(ins)]
    return pl.pallas_call(
        kernel,
        in_specs=specs,
        out_specs=[smem if x.dtype == jnp.int32 else vmem for x in outs],
        out_shape=list(outs),
        scratch_shapes=list(scratch),
        compiler_params=pltpu.CompilerParams(vmem_limit_bytes=VMEM_LIMIT),
        name=getattr(kernel, "func", kernel).__name__,
    )(*ins)


def swap(blocks, along):
    counts = size_of(ROW), size_of(COL)
    taken = []
    for k, block in enumerate(blocks):
        route = []
        for here in itertools.product(*(range(n) for n in counts)):
            there = list(here)
            there[along] += 1 if here[along] % 2 != k else -1
            if 0 <= there[along] < counts[along]:
                route.append((here[0] * counts[1] + here[1], there[0] * counts[1] + there[1]))
        taken.append(lax.ppermute(block, ALL, route))
    return taken


def exchange(block, axes):
    return lax.all_to_all(block, axes, 0, 0, tiled=True)


def size_of(axes):
    return math.prod(lax.axis_size(a) for a in axes)


def reduce_all(packed, probe, place_in_group):
    group, rest = size_of(SCATTER), size_of(REST)
    part = exchange(packed.reshape(group, 4, TILES, SIZE), SCATTER)
    (part,) = call(reduce_kernel, [part], [shape(rest, 4, TILES, SIZE)])
    part = exchange(part, REST)
    (part,) = call(strip_kernel, [place_in_group, part, probe], [shape(group, 3, TILES, SIZE)])
    return exchange(part, SCATTER).reshape(SIZE // TILES, 2, 3, TILES, SIZE)


def per_device(obj, probe, measured, offsets):
    right3, left3 = (jnp.asarray(t) for t in dft_tables())
    offsets = jnp.swapaxes(offsets[0, 0], 1, 2)
    r, c, half = (lax.axis_index(axes).astype(jnp.int32) for axes in (ROW, COL, ("zl",)))
    whole = 2 * SIZE
    place_in_group = jnp.stack([lax.axis_index(SCATTER[:-1]).astype(jnp.int32), half])
    edges = jnp.stack([
        jnp.where(r == 0, HALF, 0),
        jnp.where(r == size_of(ROW) - 1, whole - HALF, whole),
        jnp.where(c == 0, HALF, 0),
        jnp.where(c == size_of(COL) - 1, whole - HALF, whole),
    ]).astype(jnp.int32)

    strip = shape(2, HALF + TILES, SIZE)
    rows_strip = shape(2, 2, HALF + TILES, SIZE)
    quads = shape(2, 2, SIZE, SIZE)
    tile, *col_out, offsets = call(
        send_kernel, [offsets, obj],
        [shape(2, SIZE, SIZE), strip, strip, jax.ShapeDtypeStruct(offsets.shape, jnp.int32)],
        [pltpu.SemaphoreType.DMA((2,))], in_hbm=(0, 1))
    col_in = swap(col_out, 1)
    staged = [measured, right3, left3]
    measured, right3, left3 = call(
        stage_kernel, [tile, *staged], [jax.ShapeDtypeStruct(x.shape, x.dtype) for x in staged],
        [pltpu.SemaphoreType.DMA((len(staged),))], in_hbm=(1, 2, 3))
    middle, *row_out, codes = call(
        spread_kernel, [*col_in, tile, col_out[1], right3], [quads, rows_strip, rows_strip, shape(TILES, SIZE)])
    row_in = swap(row_out, 0)
    others = jnp.concatenate([row_in[0][0, 0, HALF:], codes, row_in[1][0, 0, HALF:]], axis=0).astype(jnp.int32)

    field = shape(2, 2, whole, SIZE)
    edge = shape(2, 2, HALF, SIZE)
    planes = shape(2, MODES, SIZE, SIZE)
    sums_shape = shape(5, SIZE, SIZE)
    packed_shape = shape(SIZE // TILES, 2, 4, TILES, SIZE)

    *row_out, sums, padded = call(
        first_kernel,
        [offsets, *row_in, middle, probe, measured, right3, left3],
        [quads, quads, sums_shape, field],
        [pltpu.VMEM((2, 2, whole, SIZE), F32)],
    )
    row_in = swap(row_out, 0)
    cover, near = call(
        cover_kernel, [others, probe],
        [shape(2, whole, SIZE), jax.ShapeDtypeStruct((LIST_SIZE, 2), jnp.int32)],
        [pltpu.VMEM((3 * SIZE, SIZE), F32)])
    col_out = call(wide_fold_kernel, [*row_out, *row_in], [quads, quads])
    col_in = swap(col_out, 1)
    packed, direction = call(
        wide_merge_kernel,
        [edges, offsets, *col_out, *col_in, cover, padded, sums],
        [packed_shape, field],
        [pltpu.VMEM((2, 2, whole, SIZE), F32)],
    )
    totals = reduce_all(packed, probe, place_in_group)

    row_out0, middle, row_out1, sums, padded, probe = call(
        next_kernel,
        [offsets, totals, padded, direction, probe, measured, right3, left3],
        [edge, quads, edge, sums_shape, field, planes],
        [pltpu.VMEM((2, 2, whole, SIZE), F32)],
    )
    row_in = swap((row_out0, row_out1), 0)
    side = shape(2, HALF, SIZE)
    (cover,) = call(
        tile_cover_kernel, [near, probe], [shape(SIZE, SIZE)], [pltpu.VMEM((3 * SIZE, SIZE), F32)])
    middle, *col_out = call(
        fold_kernel, [middle, *row_in, cover], [shape(2, SIZE, SIZE), side, side])
    col_in = swap(col_out, 1)
    packed, direction = call(
        merge_kernel,
        [near, middle, *col_in, cover, padded, sums],
        [packed_shape, shape(2, SIZE, SIZE)],
        [pltpu.VMEM((2, 3 * SIZE, SIZE), F32), pltpu.VMEM((2, SIZE, SIZE), F32)],
    )
    totals = reduce_all(packed, probe, place_in_group)
    return tuple(call(
        last_kernel, [totals, padded, direction, probe], [shape(2, SIZE, SIZE), planes, planes]
    ))


def solution(mesh):
    parts = Mesh(mesh.devices.reshape(2, 4, 2, 4, 4, 2), ALL)
    in_specs = (P(None, ROW, COL), P(), P(ROW, COL), P(ROW, COL))
    out_specs = (P(None, ROW, COL), P(), P())
    return jax.shard_map(
        per_device, mesh=parts, in_specs=in_specs, out_specs=out_specs, check_vma=False
    )
```

```python
import itertools
import math
from functools import partial

import jax
import jax.numpy as jnp
import numpy as np
from jax import lax
from jax.experimental import pallas as pl
from jax.experimental.pallas import tpu as pltpu
from jax.sharding import Mesh, PartitionSpec as P

SIZE = 128
HALF = 64
MODES = 2
COUNT = 8
ROW = ("yl", "x", "c")
COL = ("yh", "zh", "zl")
ALL = ROW + COL
SCATTER = ("x", "c", "yl", "zl")
REST = ("zh", "yh")
MARK = 1024
LIST_STEP = 4
LIST_SIZE = 6 * COUNT + 8
TILES = 8
VMEM_LIMIT = 16 * 1024 * 1024
F32 = jnp.float32
BF16 = jnp.bfloat16


def dft_tables():
    index = np.arange(SIZE)
    angle = 2.0 * math.pi / SIZE * (np.outer(index, index) % SIZE)
    real = np.cos(angle) / math.sqrt(SIZE)
    imag = -np.sin(angle) / math.sqrt(SIZE)
    right = np.block([[real, imag], [-imag, real]]).astype(np.float32)
    high = right.astype(jnp.bfloat16)
    low = (right - high.astype(np.float32)).astype(jnp.bfloat16)
    right3 = np.concatenate([high, high, low], axis=0)
    left3 = np.ascontiguousarray(right3.T)
    return right3, left3


def halves(x):
    high = x.astype(BF16)
    return high, (x - high.astype(F32)).astype(BF16)


def right_transform(fields, table):
    rows = []
    for real, imag in fields:
        rh, rl = halves(real)
        ih, il = halves(imag)
        rows.append(jnp.concatenate([rh, ih, rl, il, rh, ih], axis=1))
    out = jnp.dot(jnp.concatenate(rows, axis=0), table, preferred_element_type=F32)
    return [
        (out[SIZE * n : SIZE * (n + 1), :SIZE], out[SIZE * n : SIZE * (n + 1), SIZE:])
        for n in range(len(fields))
    ]


def left_transform(fields, table):
    cols = []
    for real, imag in fields:
        rh, rl = halves(real)
        ih, il = halves(imag)
        cols.append(jnp.concatenate([rh, ih, rl, il, rh, ih], axis=0))
    out = jnp.dot(table, jnp.concatenate(cols, axis=1), preferred_element_type=F32)
    return [
        (out[:SIZE, SIZE * n : SIZE * (n + 1)], out[SIZE:, SIZE * n : SIZE * (n + 1)])
        for n in range(len(fields))
    ]


def lanes():
    return lax.broadcasted_iota(jnp.int32, (SIZE, SIZE), 1)


def window(ref, lead, row, col):
    shift = lax.rem(SIZE - col, SIZE)
    rows = pl.ds(row, SIZE)
    mixed = jnp.where(lanes() >= col, ref[lead + (0, rows)], ref[lead + (1, rows)])
    return pltpu.roll(mixed, shift, 1)


def place(ref, plane, row, col, block):
    moved = pltpu.roll(block, lax.rem(col, SIZE), 1)
    first = lanes() >= col
    rows = pl.ds(row, SIZE)
    ref[plane, 0, rows] += jnp.where(first, moved, 0.0)
    ref[plane, 1, rows] += jnp.where(first, 0.0, moved)


def join(low, first, second):
    return jnp.where(low, pltpu.roll(first, HALF, 1), pltpu.roll(second, HALF, 1))


def pack_low(low, upper, lower):
    return jnp.where(low, upper, pltpu.roll(lower, HALF, 1))


def pack_high(low, upper, lower):
    return jnp.where(low, pltpu.roll(upper, HALF, 1), lower)


def low_lanes(rows):
    return lax.broadcasted_iota(jnp.int32, (rows, SIZE), 1) < HALF


def bounds():
    limits = []
    for axes in (ROW, COL):
        here = lax.axis_index(axes)
        limits.append(jnp.where(here == 0, HALF, 0))
        limits.append(jnp.where(here == size_of(axes) - 1, 2 * SIZE - HALF, 2 * SIZE))
    return limits


def inside(limits, down, across, rows=SIZE):
    row_low, row_high, col_low, col_high = limits
    line = lax.broadcasted_iota(jnp.int32, (rows, SIZE), 0) + down
    lane = lax.broadcasted_iota(jnp.int32, (rows, SIZE), 1) + across
    return (line >= row_low) & (line < row_high) & (lane >= col_low) & (lane < col_high)


def odds():
    return tuple(lax.axis_index(axis) == 1 for axis in (ROW[-1], COL[-1]))


def sides(odd, first, second):
    return jnp.where(odd, second, first), jnp.where(odd, first, second)


def send_kernel(raw, own, tile, col_out0, col_out1, offsets, sems):
    copies = [
        pltpu.make_async_copy(source, target, sems.at[k])
        for k, (source, target) in enumerate(((raw, offsets), (own, tile)))
    ]
    for copy in copies:
        copy.start()
    line = lax.broadcasted_iota(jnp.int32, (TILES, SIZE), 0)
    lane = lax.broadcasted_iota(jnp.int32, (TILES, SIZE), 1)
    code = jnp.zeros((TILES, SIZE), jnp.int32)
    copies[0].wait()
    batches, _, count = offsets.shape
    for b in range(batches):
        for k in range(count):
            for d in range(2):
                code = jnp.where(lane == (b * 2 + d) * count + k, offsets[b, d, k] + MARK, code)
    code = jnp.where(line == 0, code, 0).astype(F32)
    copies[1].wait()
    low = low_lanes(HALF)
    _, odd_col = odds()
    for c in range(2):
        upper, lower = tile[c, :HALF], tile[c, HALF:]
        to_left = pack_low(low, upper, lower)
        to_right = pack_high(low, upper, lower)
        col_out0[c, :HALF] = jnp.where(odd_col, to_right, to_left)
        col_out1[c, :HALF] = jnp.where(odd_col, to_left, to_right)
        col_out0[c, HALF:] = code
        col_out1[c, HALF:] = code


def spread_kernel(col_in0, col_in1, tile, mine, staged, middle, row_out0, row_out1, codes):
    low = low_lanes(HALF)
    odd_row, odd_col = odds()
    left, right = sides(odd_col, col_in0[0, HALF:], col_in1[0, HALF:])
    code = mine[0, HALF:] + pltpu.roll(left, 1, 0) + pltpu.roll(right, 2, 0)
    codes[...] = code
    for c in range(2):
        left, right = sides(odd_col, col_in0[c, :HALF], col_in1[c, :HALF])
        ends = []
        for k in range(2):
            rows = slice(HALF * k, HALF * (k + 1))
            own = pltpu.roll(tile[c, rows], HALF, 1)
            first = jnp.where(low, left if k == 0 else pltpu.roll(left, HALF, 1), own)
            second = jnp.where(low, own, right if k == 1 else pltpu.roll(right, HALF, 1))
            middle[c, 0, rows] = first
            middle[c, 1, rows] = second
            ends.append((first, second))
        for h in range(2):
            top, bottom = ends[0][h], ends[1][h]
            row_out0[c, h, :HALF] = jnp.where(odd_row, bottom, top)
            row_out1[c, h, :HALF] = jnp.where(odd_row, top, bottom)
            row_out0[c, h, HALF:] = code
            row_out1[c, h, HALF:] = code


def power_of(probe):
    return sum(probe[c, m] * probe[c, m] for c in range(2) for m in range(MODES))


def stage_kernel(tile, *refs):
    count = (len(refs) - 1) // 2
    sems = refs[-1]
    copies = [pltpu.make_async_copy(refs[k], refs[count + k], sems.at[k]) for k in range(count)]
    for copy in copies:
        copy.start()
    for copy in copies:
        copy.wait()


def sweep(batch, offsets, padded, probe, measured, right3, left3, sums, accum):
    accum[...] = jnp.zeros_like(accum)
    tr = right3[...]
    tl = left3[...]
    wins = []
    waves = []
    for j in range(COUNT):
        row, col = offsets[batch, 0, j] + HALF, offsets[batch, 1, j] + HALF
        wr = window(padded, (0,), row, col)
        wi = window(padded, (1,), row, col)
        wins.append((row, col, wr, wi))
        fields = []
        for m in range(MODES):
            pr, pi = probe[0, m], probe[1, m]
            fields.append((pr * wr - pi * wi, pr * wi + pi * wr))
        waves.append(right_transform(fields, tr))
    waves = [left_transform(fields, tl) for fields in waves]
    chis = []
    for j in range(COUNT):
        intensity = sum(r * r + i * i for r, i in waves[j])
        ratio = jnp.sqrt(measured[0, 0, batch, j]) / jnp.maximum(jnp.sqrt(intensity), 0.5) - 1.0
        chis.append(left_transform([(r * ratio, -(i * ratio)) for r, i in waves[j]], tl))
    chis = [right_transform(fields, tr) for fields in chis]
    totals = [0.0] * 5
    for j in range(COUNT):
        row, col, wr, wi = wins[j]
        cr = jnp.zeros((SIZE, SIZE), F32)
        ci = jnp.zeros((SIZE, SIZE), F32)
        for m in range(MODES):
            xr, xn = chis[j][m]
            pr, pi = probe[0, m], probe[1, m]
            cr += pr * xr - pi * xn
            ci -= pr * xn + pi * xr
            totals[m] = totals[m] + (wr * xr - wi * xn)
            totals[MODES + m] = totals[MODES + m] - (wr * xn + wi * xr)
        totals[2 * MODES] = totals[2 * MODES] + (wr * wr + wi * wi)
        place(accum, 0, row, col, cr)
        place(accum, 1, row, col, ci)
    for k in range(5):
        sums[k] = totals[k]


def first_kernel(offsets, row_in0, row_in1, middle, probe, measured, right3, left3,
                 row_out0, row_out1, sums, padded, accum):
    odd_row, _ = odds()
    for c in range(2):
        for h in range(2):
            above, below = sides(odd_row, row_in0[c, h, :HALF], row_in1[c, h, :HALF])
            padded[c, h, :HALF] = above
            padded[c, h, HALF : HALF + SIZE] = middle[c, h]
            padded[c, h, HALF + SIZE :] = below
    sweep(0, offsets, padded, probe, measured, right3, left3, sums, accum)
    for c in range(2):
        for h in range(2):
            top, bottom = accum[c, h, :SIZE], accum[c, h, SIZE:]
            row_out0[c, h] = jnp.where(odd_row, bottom, top)
            row_out1[c, h] = jnp.where(odd_row, top, bottom)


def offset_of(others, batch, across, down, j, d):
    odd_row, _ = odds()
    tile = jnp.where(odd_row, 2 - down, down)
    return others[TILES * tile + (1, 0, 2)[across], (batch * 2 + d) * COUNT + j] - MARK


def cover_kernel(others, probe, cover, near, light):
    none = jnp.zeros((SIZE, SIZE), F32)
    light[:SIZE] = none
    light[SIZE : 2 * SIZE] = power_of(probe)
    light[2 * SIZE :] = none
    lane = lanes()
    for v in range(2):
        total = [none, none]
        for down in (v, v + 1):
            for across in range(3):
                for j in range(COUNT):
                    row, col = (offset_of(others, 0, across, down, j, d) + HALF for d in range(2))
                    row = jnp.clip(row + SIZE * (down - 1 - v), -SIZE, SIZE)
                    col = jnp.clip(col, 0, SIZE)
                    moved = pltpu.roll(light[pl.ds(SIZE - row, SIZE)], lax.rem(col, SIZE), 1)
                    first = lane >= col
                    if across >= 1:
                        total[across - 1] = total[across - 1] + jnp.where(first, moved, 0.0)
                    if across <= 1:
                        total[across] = total[across] + jnp.where(first, 0.0, moved)
        for h in range(2):
            cover[h, v * SIZE : (v + 1) * SIZE] = total[h]

    for v in range(2):
        count = jnp.int32(0)
        for down in (1, 2 - 2 * v):
            for across in range(3):
                for j in range(COUNT):
                    row = offset_of(others, 1, across, down, j, 0) + SIZE * (down - 1)
                    col = offset_of(others, 1, across, down, j, 1) + SIZE * (across - 1)
                    near[v, 0, count] = row
                    near[v, 1, count] = col
                    reaches = (jnp.abs(row) < SIZE) & (jnp.abs(col) < SIZE)
                    count += reaches.astype(jnp.int32)
        for k in range(LIST_STEP):
            near[v, 0, count + k] = 0
            near[v, 1, count + k] = SIZE
        near[v, 0, LIST_SIZE - 1] = count


def listed_sum(near, which, half, planes, sign):
    lane = lax.broadcasted_iota(jnp.int32, (HALF, SIZE), 1)

    def body(step, totals):
        totals = list(totals)
        for g in range(LIST_STEP):
            down = sign * near[which, 0, step * LIST_STEP + g]
            across = sign * near[which, 1, step * LIST_STEP + g]
            turn = lax.rem(2 * SIZE - across, SIZE)
            source = lane + across
            valid = (source >= 0) & (source < SIZE)
            for c, plane in enumerate(planes):
                moved = pltpu.roll(plane[pl.ds(SIZE + HALF * half + down, HALF)], turn, 1)
                totals[c] = totals[c] + jnp.where(valid, moved, 0.0)
        return tuple(totals)

    steps = lax.div(near[which, 0, LIST_SIZE - 1] + LIST_STEP - 1, LIST_STEP)
    return lax.fori_loop(0, steps, body, (jnp.zeros((HALF, SIZE), F32),) * len(planes))


def wide_fold_kernel(row_out0, row_out1, row_in0, row_in1, col_out0, col_out1):
    odd_row, odd_col = odds()
    for c in range(2):
        top, bottom = [], []
        for h in range(2):
            upper, lower = sides(
                odd_row, row_out0[c, h] + row_in0[c, h], row_out1[c, h] + row_in1[c, h])
            top.append(upper)
            bottom.append(lower)
        for v, (left, right) in enumerate((top, bottom)):
            col_out0[v, c] = jnp.where(odd_col, right, left)
            col_out1[v, c] = jnp.where(odd_col, left, right)


def pack_planes(packed, planes):
    strips = (SIZE // TILES, TILES, SIZE)
    upper = lax.rem(lax.broadcasted_iota(jnp.int32, (SIZE, SIZE), 0), TILES) < TILES // 2
    for q in range(len(planes) // 2):
        one, two = planes[2 * q], planes[2 * q + 1]
        packed[:, 0, q] = jnp.where(upper, one, pltpu.roll(two, TILES // 2, 0)).reshape(strips)
        packed[:, 1, q] = jnp.where(upper, pltpu.roll(one, SIZE - TILES // 2, 0), two).reshape(strips)


def unpack_planes(packed, q):
    upper = lax.rem(lax.broadcasted_iota(jnp.int32, (SIZE, SIZE), 0), TILES) < TILES // 2
    one, two = (packed[:, h, q].reshape(SIZE, SIZE) for h in range(2))
    return (jnp.where(upper, one, pltpu.roll(two, TILES // 2, 0)),
            jnp.where(upper, pltpu.roll(one, SIZE - TILES // 2, 0), two))


def pack_sums(packed, sums, overlap, a11, b1):
    turn = lax.rem(lax.broadcasted_iota(jnp.int32, (SIZE, SIZE), 0), TILES // 2)
    numbers = jnp.where(turn == 0, a11, jnp.where(turn == 1, b1, 0.0))
    pack_planes(packed, [sums[k] for k in range(5)] + [numbers] + list(overlap))


def wide_merge_kernel(offsets, col_out0, col_out1, col_in0, col_in1, cover, padded, sums,
                      packed, direction, product):
    limits = bounds()
    _, odd_col = odds()
    a11 = jnp.zeros((1, SIZE), F32)
    b1 = jnp.zeros((1, SIZE), F32)
    for v in range(2):
        rows = slice(v * SIZE, (v + 1) * SIZE)
        mine_rows = lax.broadcasted_iota(jnp.int32, (SIZE, SIZE), 0) + v * SIZE
        totals = [sides(odd_col, col_out0[v, c] + col_in0[v, c], col_out1[v, c] + col_in1[v, c]) for c in range(2)]
        for h in range(2):
            light = cover[h, rows]
            inverse = jnp.where(inside(limits, v * SIZE, h * SIZE), 1.0 / (light + 1.0), 0.0)
            dr, di = (totals[c][h] * inverse for c in range(2))
            direction[0, h, rows] = dr
            direction[1, h, rows] = di
            pr, pi = padded[0, h, rows], padded[1, h, rows]
            product[0, h, rows] = dr * pr + di * pi
            product[1, h, rows] = dr * pi - di * pr
            across = lanes() + h * SIZE
            mine = (mine_rows >= HALF) & (mine_rows < HALF + SIZE) & (across >= HALF) & (across < HALF + SIZE)
            power = jnp.where(mine, dr * dr + di * di, 0.0)
            a11 += jnp.sum(power * light, axis=0, keepdims=True)
            b1 += jnp.sum(power * (light + 1.0), axis=0, keepdims=True)
    overlap = [jnp.zeros((SIZE, SIZE), F32)] * 2
    for j in range(COUNT):
        row, col = offsets[0, 0, j] + HALF, offsets[0, 1, j] + HALF
        overlap = [overlap[c] + window(product, (c,), row, col) for c in range(2)]
    pack_sums(packed, sums, overlap, a11, b1)


def fold_kernel(middle, row_in0, row_in1, cover, tile, col_out0, col_out1):
    low = low_lanes(HALF)
    odd_row, odd_col = odds()
    for k in range(2):
        upper, lower = [], []
        for h in range(2):
            above, below = sides(odd_row, row_in0[k, h], row_in1[k, h])
            upper.append(middle[k, h, :HALF] + above)
            lower.append(middle[k, h, HALF:] + below)
        tile[k, :HALF] = join(low, *upper)
        tile[k, HALF:] = join(low, *lower)
        to_left = pack_low(low, upper[0], lower[0])
        to_right = pack_high(low, upper[1], lower[1])
        col_out0[k] = jnp.where(odd_col, to_right, to_left)
        col_out1[k] = jnp.where(odd_col, to_left, to_right)


def tile_cover_kernel(near, probe, cover, light):
    light[:SIZE] = jnp.zeros((SIZE, SIZE), F32)
    light[SIZE : 2 * SIZE] = power_of(probe)
    light[2 * SIZE :] = jnp.zeros((SIZE, SIZE), F32)
    for half in range(2):
        (cover[HALF * half : HALF * (half + 1)],) = listed_sum(near, 1 - half, half, [light], -1)


def merge_kernel(near, tile, col_in0, col_in1, cover, padded, sums,
                 packed, direction, product):
    low = low_lanes(HALF)
    lane = lanes()
    _, odd_col = odds()
    a11 = jnp.zeros((1, SIZE), F32)
    b1 = jnp.zeros((1, SIZE), F32)
    for c in range(2):
        product[c, :SIZE] = jnp.zeros((SIZE, SIZE), F32)
        product[c, 2 * SIZE :] = jnp.zeros((SIZE, SIZE), F32)
    for v in range(2):
        rows = slice(HALF * v, HALF * (v + 1))
        full = []
        for k in range(2):
            left, right = sides(odd_col, col_in0[k], col_in1[k])
            if v == 0:
                right = pltpu.roll(right, HALF, 1)
            else:
                left = pltpu.roll(left, HALF, 1)
            full.append(tile[k, rows] + jnp.where(low, left, right))
        gr, gi = full
        light = cover[rows]
        inverse = 1.0 / (light + 1.0)
        dr = gr * inverse
        di = gi * inverse
        direction[0, rows] = dr
        direction[1, rows] = di
        span = slice(HALF * (v + 1), HALF * (v + 2))
        pr = join(low, padded[0, 0, span], padded[0, 1, span])
        pi = join(low, padded[1, 0, span], padded[1, 1, span])
        inner = slice(SIZE + HALF * v, SIZE + HALF * (v + 1))
        product[0, inner] = dr * pr + di * pi
        product[1, inner] = dr * pi - di * pr
        power = dr * dr + di * di
        a11 += jnp.sum(power * light, axis=0, keepdims=True)
        b1 += jnp.sum(power * (light + 1.0), axis=0, keepdims=True)

    parts = [listed_sum(near, half, half, [product.at[0], product.at[1]], 1) for half in range(2)]
    overlap = [jnp.concatenate([parts[0][c], parts[1][c]], axis=0) for c in range(2)]
    pack_sums(packed, sums, overlap, a11, b1)


def add_all(parts):
    total = parts[0]
    for k in range(1, parts.shape[0]):
        total = total + parts[k]
    return total


def reduce_kernel(parts, out):
    total = add_all(parts)
    for k in range(out.shape[0]):
        out[k] = total


def strip_kernel(parts, probe, out):
    total = add_all(parts)
    line = lax.broadcasted_iota(jnp.int32, (TILES, SIZE), 0)
    half = TILES // 2
    upper = line < half
    first = lax.axis_index(SCATTER[-1]) == 0
    rows = pl.ds(pl.multiple_of(lax.axis_index(SCATTER[:-1]) * TILES, TILES), TILES)

    def turned(x):
        return pltpu.roll(x, half, 0)

    def both(x, of_upper):
        return jnp.where(upper == of_upper, x, turned(x))

    def modes(c):
        one, two = probe[c, 0, rows], probe[c, 1, rows]
        return jnp.where(upper, jnp.where(first, one, turned(one)), jnp.where(first, turned(two), two))

    pr, pi = modes(0), modes(1)
    cover = both(total[2], True)
    inverse = 1.0 / (cover + 1.0)
    dr, di = total[0] * inverse, total[1] * inverse
    cross = (pr * dr + pi * di) * both(total[3], True) - (pr * di - pi * dr) * both(total[3], False)
    power = dr * dr + di * di
    a22, b2, a12 = (
        jnp.sum(x, axis=0, keepdims=True) for x in (power * cover, power * (cover + 1.0), cross))
    a11, b1 = total[2, half : half + 1], total[2, half + 1 : half + 2]
    low = low_lanes(1)
    known = jnp.where(low, a11 + pltpu.roll(a11, HALF, 1), b1 + pltpu.roll(b1, HALF, 1))
    numbers = total[2]
    for k, term in enumerate((known, a22, b2, a12)):
        numbers = jnp.where(line == half + k, term, numbers)
    for k in range(out.shape[0]):
        out[k, 0] = total[0]
        out[k, 1] = total[1]
        out[k, 2] = numbers


def step_sizes(totals, probe, new_probe, gradient=None):
    numbers = jnp.zeros((TILES, SIZE), F32)
    for k in range(totals.shape[0]):
        numbers += totals[k, 0, 2] + totals[k, 1, 2]
    half = TILES // 2
    low = low_lanes(1)
    known, *rest = (numbers[half + k : half + k + 1] for k in range(4))
    a22, b2, a12 = (jnp.sum(x, axis=1, keepdims=True) for x in rest)
    share = 1.0 / (2 * totals.shape[0])
    a11 = jnp.sum(jnp.where(low, known, 0.0), axis=1, keepdims=True) * share
    b1 = jnp.sum(jnp.where(low, 0.0, known), axis=1, keepdims=True) * share
    a11 = 1.1 * a11
    a22 = 1.1 * a22
    det = a11 * a22 - a12 * a12
    step_obj = (b1 * a22 - a12 * b2) / det
    step_probe = (a11 * b2 - a12 * b1) / det
    cover, _ = unpack_planes(totals, 2)
    cover = cover + 1.0
    scale = step_probe / cover
    for c in range(2):
        for m, numer in enumerate(unpack_planes(totals, c)):
            new_probe[c, m] = probe[c, m] + scale * numer
            if gradient is not None:
                gradient[c, m] = numer * lax.rsqrt(cover)
    return step_obj


def next_kernel(offsets, totals, padded, direction, probe, measured, right3, left3,
                row_out0, middle, row_out1, sums, new_padded, new_probe, accum):
    step = step_sizes(totals, probe, new_probe)
    new_padded[...] = padded[...] + step * direction[...]
    sweep(1, offsets, new_padded, new_probe, measured, right3, left3, sums, accum)
    middle[...] = accum[:, :, HALF : HALF + SIZE]
    odd_row, _ = odds()
    for c in range(2):
        for h in range(2):
            top, bottom = accum[c, h, :HALF], accum[c, h, HALF + SIZE :]
            row_out0[c, h] = jnp.where(odd_row, bottom, top)
            row_out1[c, h] = jnp.where(odd_row, top, bottom)


def last_kernel(totals, padded, direction, probe, new_obj, new_probe, gradient):
    step = step_sizes(totals, probe, new_probe, gradient)
    low = lanes() < HALF
    rows = slice(HALF, HALF + SIZE)
    for c in range(2):
        old = join(low, padded[c, 0, rows], padded[c, 1, rows])
        new_obj[c] = old + step * direction[c]


def shape(*dims):
    return jax.ShapeDtypeStruct(dims, F32)


def call(kernel, ins, outs, scratch=(), in_hbm=()):
    vmem = pl.BlockSpec(memory_space=pltpu.VMEM)
    smem = pl.BlockSpec(memory_space=pltpu.SMEM)
    hbm = pl.BlockSpec(memory_space=pltpu.HBM)
    ins = [pltpu.with_memory_space_constraint(x, pltpu.HBM) if k in in_hbm else x for k, x in enumerate(ins)]
    specs = [hbm if k in in_hbm else smem if x.dtype == jnp.int32 else vmem for k, x in enumerate(ins)]
    return pl.pallas_call(
        kernel,
        in_specs=specs,
        out_specs=[smem if x.dtype == jnp.int32 else vmem for x in outs],
        out_shape=list(outs),
        scratch_shapes=list(scratch),
        compiler_params=pltpu.CompilerParams(vmem_limit_bytes=VMEM_LIMIT),
        name=getattr(kernel, "func", kernel).__name__,
    )(*ins)


def swap(blocks, along):
    counts = size_of(ROW), size_of(COL)
    taken = []
    for k, block in enumerate(blocks):
        route = []
        for here in itertools.product(*(range(n) for n in counts)):
            there = list(here)
            there[along] += 1 if here[along] % 2 != k else -1
            if 0 <= there[along] < counts[along]:
                route.append((here[0] * counts[1] + here[1], there[0] * counts[1] + there[1]))
        taken.append(lax.ppermute(block, ALL, route))
    return taken


def exchange(block, axes):
    return lax.all_to_all(block, axes, 0, 0, tiled=True)


def size_of(axes):
    return math.prod(lax.axis_size(a) for a in axes)


def reduce_all(packed, probe):
    group, rest = size_of(SCATTER), size_of(REST)
    part = exchange(packed.reshape(group, 4, TILES, SIZE), SCATTER)
    (part,) = call(reduce_kernel, [part], [shape(rest, 4, TILES, SIZE)])
    part = exchange(part, REST)
    (part,) = call(strip_kernel, [part, probe], [shape(group, 3, TILES, SIZE)])
    return exchange(part, SCATTER).reshape(SIZE // TILES, 2, 3, TILES, SIZE)


def per_device(obj, probe, measured, offsets):
    right3, left3 = (jnp.asarray(t) for t in dft_tables())
    offsets = jnp.swapaxes(offsets[0, 0], 1, 2)
    whole = 2 * SIZE

    strip = shape(2, HALF + TILES, SIZE)
    rows_strip = shape(2, 2, HALF + TILES, SIZE)
    quads = shape(2, 2, SIZE, SIZE)
    tile, *col_out, offsets = call(
        send_kernel, [offsets, obj],
        [shape(2, SIZE, SIZE), strip, strip, jax.ShapeDtypeStruct(offsets.shape, jnp.int32)],
        [pltpu.SemaphoreType.DMA((2,))], in_hbm=(0, 1))
    col_in = swap(col_out, 1)
    staged = [measured, right3, left3]
    measured, right3, left3 = call(
        stage_kernel, [tile, *staged], [jax.ShapeDtypeStruct(x.shape, x.dtype) for x in staged],
        [pltpu.SemaphoreType.DMA((len(staged),))], in_hbm=(1, 2, 3))
    middle, *row_out, codes = call(
        spread_kernel, [*col_in, tile, col_out[1], right3], [quads, rows_strip, rows_strip, shape(TILES, SIZE)])
    row_in = swap(row_out, 0)
    others = jnp.concatenate([row_in[0][0, 0, HALF:], codes, row_in[1][0, 0, HALF:]], axis=0).astype(jnp.int32)

    field = shape(2, 2, whole, SIZE)
    edge = shape(2, 2, HALF, SIZE)
    planes = shape(2, MODES, SIZE, SIZE)
    sums_shape = shape(5, SIZE, SIZE)
    packed_shape = shape(SIZE // TILES, 2, 4, TILES, SIZE)

    *row_out, sums, padded = call(
        first_kernel,
        [offsets, *row_in, middle, probe, measured, right3, left3],
        [quads, quads, sums_shape, field],
        [pltpu.VMEM((2, 2, whole, SIZE), F32)],
    )
    row_in = swap(row_out, 0)
    cover, near = call(
        cover_kernel, [others, probe],
        [shape(2, whole, SIZE), jax.ShapeDtypeStruct((2, 2, LIST_SIZE), jnp.int32)],
        [pltpu.VMEM((3 * SIZE, SIZE), F32)])
    col_out = call(wide_fold_kernel, [*row_out, *row_in], [quads, quads])
    col_in = swap(col_out, 1)
    packed, direction = call(
        wide_merge_kernel,
        [offsets, *col_out, *col_in, cover, padded, sums],
        [packed_shape, field],
        [pltpu.VMEM((2, 2, whole, SIZE), F32)],
    )
    totals = reduce_all(packed, probe)

    row_out0, middle, row_out1, sums, padded, probe = call(
        next_kernel,
        [offsets, totals, padded, direction, probe, measured, right3, left3],
        [edge, quads, edge, sums_shape, field, planes],
        [pltpu.VMEM((2, 2, whole, SIZE), F32)],
    )
    row_in = swap((row_out0, row_out1), 0)
    side = shape(2, HALF, SIZE)
    (cover,) = call(
        tile_cover_kernel, [near, probe], [shape(SIZE, SIZE)], [pltpu.VMEM((3 * SIZE, SIZE), F32)])
    middle, *col_out = call(
        fold_kernel, [middle, *row_in, cover], [shape(2, SIZE, SIZE), side, side])
    col_in = swap(col_out, 1)
    packed, direction = call(
        merge_kernel,
        [near, middle, *col_in, cover, padded, sums],
        [packed_shape, shape(2, SIZE, SIZE)],
        [pltpu.VMEM((2, 3 * SIZE, SIZE), F32)],
    )
    totals = reduce_all(packed, probe)
    return tuple(call(
        last_kernel, [totals, padded, direction, probe], [shape(2, SIZE, SIZE), planes, planes]
    ))


def solution(mesh):
    parts = Mesh(mesh.devices.reshape(2, 4, 2, 4, 4, 2), ALL)
    in_specs = (P(None, ROW, COL), P(), P(ROW, COL), P(ROW, COL))
    out_specs = (P(None, ROW, COL), P(), P())
    return jax.shard_map(
        per_device, mesh=parts, in_specs=in_specs, out_specs=out_specs, check_vma=False
    )
```

```python
import itertools
import math
from functools import partial

import jax
import jax.numpy as jnp
import numpy as np
from jax import lax
from jax.experimental import pallas as pl
from jax.experimental.pallas import tpu as pltpu
from jax.sharding import Mesh, PartitionSpec as P

SIZE = 128
HALF = 64
MODES = 2
COUNT = 8
ROW = ("yl", "x", "c")
COL = ("yh", "zh", "zl")
ALL = ROW + COL
SCATTER = ("c", "x", "yl", "zl")
REST = ("zh", "yh")
MARK = 1024
LIST_STEP = 4
LIST_SIZE = 6 * COUNT + 8
TILES = 8
VMEM_LIMIT = 16 * 1024 * 1024
F32 = jnp.float32
BF16 = jnp.bfloat16


def dft_tables():
    index = np.arange(SIZE)
    angle = 2.0 * math.pi / SIZE * (np.outer(index, index) % SIZE)
    real = np.cos(angle) / math.sqrt(SIZE)
    imag = -np.sin(angle) / math.sqrt(SIZE)
    right = np.block([[real, imag], [-imag, real]]).astype(np.float32)
    high = right.astype(jnp.bfloat16)
    low = (right - high.astype(np.float32)).astype(jnp.bfloat16)
    right3 = np.concatenate([high, high, low], axis=0)
    left3 = np.ascontiguousarray(right3.T)
    return right3, left3


def halves(x):
    high = x.astype(BF16)
    return high, (x - high.astype(F32)).astype(BF16)


def right_transform(fields, table):
    rows = []
    for real, imag in fields:
        rh, rl = halves(real)
        ih, il = halves(imag)
        rows.append(jnp.concatenate([rh, ih, rl, il, rh, ih], axis=1))
    out = jnp.dot(jnp.concatenate(rows, axis=0), table, preferred_element_type=F32)
    return [
        (out[SIZE * n : SIZE * (n + 1), :SIZE], out[SIZE * n : SIZE * (n + 1), SIZE:])
        for n in range(len(fields))
    ]


def left_transform(fields, table):
    cols = []
    for real, imag in fields:
        rh, rl = halves(real)
        ih, il = halves(imag)
        cols.append(jnp.concatenate([rh, ih, rl, il, rh, ih], axis=0))
    out = jnp.dot(table, jnp.concatenate(cols, axis=1), preferred_element_type=F32)
    return [
        (out[:SIZE, SIZE * n : SIZE * (n + 1)], out[SIZE:, SIZE * n : SIZE * (n + 1)])
        for n in range(len(fields))
    ]


def lanes():
    return lax.broadcasted_iota(jnp.int32, (SIZE, SIZE), 1)


def window(ref, lead, row, col):
    shift = lax.rem(SIZE - col, SIZE)
    rows = pl.ds(row, SIZE)
    mixed = jnp.where(lanes() >= col, ref[lead + (0, rows)], ref[lead + (1, rows)])
    return pltpu.roll(mixed, shift, 1)


def place(ref, plane, row, col, block):
    moved = pltpu.roll(block, lax.rem(col, SIZE), 1)
    first = lanes() >= col
    rows = pl.ds(row, SIZE)
    ref[plane, 0, rows] += jnp.where(first, moved, 0.0)
    ref[plane, 1, rows] += jnp.where(first, 0.0, moved)


def join(low, first, second):
    return jnp.where(low, pltpu.roll(first, HALF, 1), pltpu.roll(second, HALF, 1))


def pack_low(low, upper, lower):
    return jnp.where(low, upper, pltpu.roll(lower, HALF, 1))


def pack_high(low, upper, lower):
    return jnp.where(low, pltpu.roll(upper, HALF, 1), lower)


def low_lanes(rows):
    return lax.broadcasted_iota(jnp.int32, (rows, SIZE), 1) < HALF


def bounds():
    limits = []
    for axes in (ROW, COL):
        here = lax.axis_index(axes)
        limits.append(jnp.where(here == 0, HALF, 0))
        limits.append(jnp.where(here == size_of(axes) - 1, 2 * SIZE - HALF, 2 * SIZE))
    return limits


def inside(limits, down, across, rows=SIZE):
    row_low, row_high, col_low, col_high = limits
    line = lax.broadcasted_iota(jnp.int32, (rows, SIZE), 0) + down
    lane = lax.broadcasted_iota(jnp.int32, (rows, SIZE), 1) + across
    return (line >= row_low) & (line < row_high) & (lane >= col_low) & (lane < col_high)


def odds():
    return tuple(lax.axis_index(axis) == 1 for axis in (ROW[-1], COL[-1]))


def sides(odd, first, second):
    return jnp.where(odd, second, first), jnp.where(odd, first, second)


def send_kernel(raw, own, tile, col_out0, col_out1, offsets, sems):
    copies = [
        pltpu.make_async_copy(source, target, sems.at[k])
        for k, (source, target) in enumerate(((raw, offsets), (own, tile)))
    ]
    for copy in copies:
        copy.start()
    line = lax.broadcasted_iota(jnp.int32, (TILES, SIZE), 0)
    lane = lax.broadcasted_iota(jnp.int32, (TILES, SIZE), 1)
    code = jnp.zeros((TILES, SIZE), jnp.int32)
    copies[0].wait()
    batches, _, count = offsets.shape
    for b in range(batches):
        for k in range(count):
            for d in range(2):
                code = jnp.where(lane == (b * 2 + d) * count + k, offsets[b, d, k] + MARK, code)
    code = jnp.where(line == 0, code, 0).astype(F32)
    copies[1].wait()
    low = low_lanes(HALF)
    _, odd_col = odds()
    for c in range(2):
        upper, lower = tile[c, :HALF], tile[c, HALF:]
        to_left = pack_low(low, upper, lower)
        to_right = pack_high(low, upper, lower)
        col_out0[c, :HALF] = jnp.where(odd_col, to_right, to_left)
        col_out1[c, :HALF] = jnp.where(odd_col, to_left, to_right)
        col_out0[c, HALF:] = code
        col_out1[c, HALF:] = code


def spread_kernel(col_in0, col_in1, tile, mine, staged, middle, row_out0, row_out1, codes):
    low = low_lanes(HALF)
    odd_row, odd_col = odds()
    left, right = sides(odd_col, col_in0[0, HALF:], col_in1[0, HALF:])
    code = mine[0, HALF:] + pltpu.roll(left, 1, 0) + pltpu.roll(right, 2, 0)
    codes[...] = code
    for c in range(2):
        left, right = sides(odd_col, col_in0[c, :HALF], col_in1[c, :HALF])
        ends = []
        for k in range(2):
            rows = slice(HALF * k, HALF * (k + 1))
            own = pltpu.roll(tile[c, rows], HALF, 1)
            first = jnp.where(low, left if k == 0 else pltpu.roll(left, HALF, 1), own)
            second = jnp.where(low, own, right if k == 1 else pltpu.roll(right, HALF, 1))
            middle[c, 0, rows] = first
            middle[c, 1, rows] = second
            ends.append((first, second))
        for h in range(2):
            top, bottom = ends[0][h], ends[1][h]
            row_out0[c, h, :HALF] = jnp.where(odd_row, bottom, top)
            row_out1[c, h, :HALF] = jnp.where(odd_row, top, bottom)
            row_out0[c, h, HALF:] = code
            row_out1[c, h, HALF:] = code


def power_of(probe):
    return sum(probe[c, m] * probe[c, m] for c in range(2) for m in range(MODES))


def stage_kernel(tile, *refs):
    count = (len(refs) - 1) // 2
    sems = refs[-1]
    copies = [pltpu.make_async_copy(refs[k], refs[count + k], sems.at[k]) for k in range(count)]
    for copy in copies:
        copy.start()
    for copy in copies:
        copy.wait()


def sweep(batch, offsets, padded, probe, measured, right3, left3, sums, accum):
    accum[...] = jnp.zeros_like(accum)
    tr = right3[...]
    tl = left3[...]
    wins = []
    waves = []
    for j in range(COUNT):
        row, col = offsets[batch, 0, j] + HALF, offsets[batch, 1, j] + HALF
        wr = window(padded, (0,), row, col)
        wi = window(padded, (1,), row, col)
        wins.append((row, col, wr, wi))
        fields = []
        for m in range(MODES):
            pr, pi = probe[0, m], probe[1, m]
            fields.append((pr * wr - pi * wi, pr * wi + pi * wr))
        waves.append(right_transform(fields, tr))
    waves = [left_transform(fields, tl) for fields in waves]
    chis = []
    for j in range(COUNT):
        intensity = sum(r * r + i * i for r, i in waves[j])
        ratio = jnp.sqrt(measured[0, 0, batch, j]) / jnp.maximum(jnp.sqrt(intensity), 0.5) - 1.0
        chis.append(left_transform([(r * ratio, -(i * ratio)) for r, i in waves[j]], tl))
    chis = [right_transform(fields, tr) for fields in chis]
    totals = [0.0] * 5
    for j in range(COUNT):
        row, col, wr, wi = wins[j]
        cr = jnp.zeros((SIZE, SIZE), F32)
        ci = jnp.zeros((SIZE, SIZE), F32)
        for m in range(MODES):
            xr, xn = chis[j][m]
            pr, pi = probe[0, m], probe[1, m]
            cr += pr * xr - pi * xn
            ci -= pr * xn + pi * xr
            totals[m] = totals[m] + (wr * xr - wi * xn)
            totals[MODES + m] = totals[MODES + m] - (wr * xn + wi * xr)
        totals[2 * MODES] = totals[2 * MODES] + (wr * wr + wi * wi)
        place(accum, 0, row, col, cr)
        place(accum, 1, row, col, ci)
    for k in range(5):
        sums[k] = totals[k]


def first_kernel(offsets, row_in0, row_in1, middle, probe, measured, right3, left3,
                 row_out0, row_out1, sums, padded, accum):
    odd_row, _ = odds()
    for c in range(2):
        for h in range(2):
            above, below = sides(odd_row, row_in0[c, h, :HALF], row_in1[c, h, :HALF])
            padded[c, h, :HALF] = above
            padded[c, h, HALF : HALF + SIZE] = middle[c, h]
            padded[c, h, HALF + SIZE :] = below
    sweep(0, offsets, padded, probe, measured, right3, left3, sums, accum)
    for c in range(2):
        for h in range(2):
            top, bottom = accum[c, h, :SIZE], accum[c, h, SIZE:]
            row_out0[c, h] = jnp.where(odd_row, bottom, top)
            row_out1[c, h] = jnp.where(odd_row, top, bottom)


def offset_of(others, batch, across, down, j, d):
    odd_row, _ = odds()
    tile = jnp.where(odd_row, 2 - down, down)
    return others[TILES * tile + (1, 0, 2)[across], (batch * 2 + d) * COUNT + j] - MARK


def cover_kernel(others, probe, cover, near, light):
    none = jnp.zeros((SIZE, SIZE), F32)
    light[:SIZE] = none
    light[SIZE : 2 * SIZE] = power_of(probe)
    light[2 * SIZE :] = none
    lane = lanes()
    for v in range(2):
        total = [none, none]
        for down in (v, v + 1):
            for across in range(3):
                for j in range(COUNT):
                    row, col = (offset_of(others, 0, across, down, j, d) + HALF for d in range(2))
                    row = jnp.clip(row + SIZE * (down - 1 - v), -SIZE, SIZE)
                    col = jnp.clip(col, 0, SIZE)
                    moved = pltpu.roll(light[pl.ds(SIZE - row, SIZE)], lax.rem(col, SIZE), 1)
                    first = lane >= col
                    if across >= 1:
                        total[across - 1] = total[across - 1] + jnp.where(first, moved, 0.0)
                    if across <= 1:
                        total[across] = total[across] + jnp.where(first, 0.0, moved)
        for h in range(2):
            cover[h, v * SIZE : (v + 1) * SIZE] = total[h]

    for v in range(2):
        count = jnp.int32(0)
        for down in (1, 2 - 2 * v):
            for across in range(3):
                for j in range(COUNT):
                    row = offset_of(others, 1, across, down, j, 0) + SIZE * (down - 1)
                    col = offset_of(others, 1, across, down, j, 1) + SIZE * (across - 1)
                    near[v, 0, count] = row
                    near[v, 1, count] = col
                    reaches = (jnp.abs(row) < SIZE) & (jnp.abs(col) < SIZE)
                    count += reaches.astype(jnp.int32)
        for k in range(LIST_STEP):
            near[v, 0, count + k] = 0
            near[v, 1, count + k] = SIZE
        near[v, 0, LIST_SIZE - 1] = count


def listed_sum(near, which, half, planes, sign):
    lane = lax.broadcasted_iota(jnp.int32, (HALF, SIZE), 1)

    def body(step, totals):
        totals = list(totals)
        for g in range(LIST_STEP):
            down = sign * near[which, 0, step * LIST_STEP + g]
            across = sign * near[which, 1, step * LIST_STEP + g]
            turn = lax.rem(2 * SIZE - across, SIZE)
            source = lane + across
            valid = (source >= 0) & (source < SIZE)
            for c, plane in enumerate(planes):
                moved = pltpu.roll(plane[pl.ds(SIZE + HALF * half + down, HALF)], turn, 1)
                totals[c] = totals[c] + jnp.where(valid, moved, 0.0)
        return tuple(totals)

    steps = lax.div(near[which, 0, LIST_SIZE - 1] + LIST_STEP - 1, LIST_STEP)
    return lax.fori_loop(0, steps, body, (jnp.zeros((HALF, SIZE), F32),) * len(planes))


def wide_fold_kernel(row_out0, row_out1, row_in0, row_in1, col_out0, col_out1):
    odd_row, odd_col = odds()
    for c in range(2):
        top, bottom = [], []
        for h in range(2):
            upper, lower = sides(
                odd_row, row_out0[c, h] + row_in0[c, h], row_out1[c, h] + row_in1[c, h])
            top.append(upper)
            bottom.append(lower)
        for v, (left, right) in enumerate((top, bottom)):
            col_out0[v, c] = jnp.where(odd_col, right, left)
            col_out1[v, c] = jnp.where(odd_col, left, right)


def pack_planes(keep, give, planes):
    half = SIZE // TILES // 2
    strips = (2 * half, TILES, SIZE)
    upper = lax.rem(lax.broadcasted_iota(jnp.int32, (SIZE, SIZE), 0), TILES) < TILES // 2
    odd, _ = odds()
    for q in range(len(planes) // 2):
        one, two = planes[2 * q], planes[2 * q + 1]
        pieces = (
            jnp.where(upper, one, pltpu.roll(two, TILES // 2, 0)),
            jnp.where(upper, pltpu.roll(one, SIZE - TILES // 2, 0), two),
        )
        for h, piece in enumerate(pieces):
            piece = piece.reshape(strips)
            keep[:, h, q] = jnp.where(odd, piece[half:], piece[:half])
            give[:, h, q] = jnp.where(odd, piece[:half], piece[half:])


def unpack_planes(packed, q):
    upper = lax.rem(lax.broadcasted_iota(jnp.int32, (SIZE, SIZE), 0), TILES) < TILES // 2
    one, two = (packed[:, h, q].reshape(SIZE, SIZE) for h in range(2))
    return (jnp.where(upper, one, pltpu.roll(two, TILES // 2, 0)),
            jnp.where(upper, pltpu.roll(one, SIZE - TILES // 2, 0), two))


def pack_sums(keep, give, sums, overlap, a11, b1):
    turn = lax.rem(lax.broadcasted_iota(jnp.int32, (SIZE, SIZE), 0), TILES // 2)
    numbers = jnp.where(turn == 0, a11, jnp.where(turn == 1, b1, 0.0))
    pack_planes(keep, give, [sums[k] for k in range(5)] + [numbers] + list(overlap))


def wide_merge_kernel(offsets, col_out0, col_out1, col_in0, col_in1, cover, padded, sums,
                      keep, give, direction, product):
    limits = bounds()
    _, odd_col = odds()
    a11 = jnp.zeros((1, SIZE), F32)
    b1 = jnp.zeros((1, SIZE), F32)
    for v in range(2):
        rows = slice(v * SIZE, (v + 1) * SIZE)
        mine_rows = lax.broadcasted_iota(jnp.int32, (SIZE, SIZE), 0) + v * SIZE
        totals = [sides(odd_col, col_out0[v, c] + col_in0[v, c], col_out1[v, c] + col_in1[v, c]) for c in range(2)]
        for h in range(2):
            light = cover[h, rows]
            inverse = jnp.where(inside(limits, v * SIZE, h * SIZE), 1.0 / (light + 1.0), 0.0)
            dr, di = (totals[c][h] * inverse for c in range(2))
            direction[0, h, rows] = dr
            direction[1, h, rows] = di
            pr, pi = padded[0, h, rows], padded[1, h, rows]
            product[0, h, rows] = dr * pr + di * pi
            product[1, h, rows] = dr * pi - di * pr
            across = lanes() + h * SIZE
            mine = (mine_rows >= HALF) & (mine_rows < HALF + SIZE) & (across >= HALF) & (across < HALF + SIZE)
            power = jnp.where(mine, dr * dr + di * di, 0.0)
            a11 += jnp.sum(power * light, axis=0, keepdims=True)
            b1 += jnp.sum(power * (light + 1.0), axis=0, keepdims=True)
    overlap = [jnp.zeros((SIZE, SIZE), F32)] * 2
    for j in range(COUNT):
        row, col = offsets[0, 0, j] + HALF, offsets[0, 1, j] + HALF
        overlap = [overlap[c] + window(product, (c,), row, col) for c in range(2)]
    pack_sums(keep, give, sums, overlap, a11, b1)


def fold_kernel(middle, row_in0, row_in1, cover, tile, col_out0, col_out1):
    low = low_lanes(HALF)
    odd_row, odd_col = odds()
    for k in range(2):
        upper, lower = [], []
        for h in range(2):
            above, below = sides(odd_row, row_in0[k, h], row_in1[k, h])
            upper.append(middle[k, h, :HALF] + above)
            lower.append(middle[k, h, HALF:] + below)
        tile[k, :HALF] = join(low, *upper)
        tile[k, HALF:] = join(low, *lower)
        to_left = pack_low(low, upper[0], lower[0])
        to_right = pack_high(low, upper[1], lower[1])
        col_out0[k] = jnp.where(odd_col, to_right, to_left)
        col_out1[k] = jnp.where(odd_col, to_left, to_right)


def tile_cover_kernel(near, probe, cover, light):
    light[:SIZE] = jnp.zeros((SIZE, SIZE), F32)
    light[SIZE : 2 * SIZE] = power_of(probe)
    light[2 * SIZE :] = jnp.zeros((SIZE, SIZE), F32)
    for half in range(2):
        (cover[HALF * half : HALF * (half + 1)],) = listed_sum(near, 1 - half, half, [light], -1)


def merge_kernel(near, tile, col_in0, col_in1, cover, padded, sums,
                 keep, give, direction, product):
    low = low_lanes(HALF)
    lane = lanes()
    _, odd_col = odds()
    a11 = jnp.zeros((1, SIZE), F32)
    b1 = jnp.zeros((1, SIZE), F32)
    for c in range(2):
        product[c, :SIZE] = jnp.zeros((SIZE, SIZE), F32)
        product[c, 2 * SIZE :] = jnp.zeros((SIZE, SIZE), F32)
    for v in range(2):
        rows = slice(HALF * v, HALF * (v + 1))
        full = []
        for k in range(2):
            left, right = sides(odd_col, col_in0[k], col_in1[k])
            if v == 0:
                right = pltpu.roll(right, HALF, 1)
            else:
                left = pltpu.roll(left, HALF, 1)
            full.append(tile[k, rows] + jnp.where(low, left, right))
        gr, gi = full
        light = cover[rows]
        inverse = 1.0 / (light + 1.0)
        dr = gr * inverse
        di = gi * inverse
        direction[0, rows] = dr
        direction[1, rows] = di
        span = slice(HALF * (v + 1), HALF * (v + 2))
        pr = join(low, padded[0, 0, span], padded[0, 1, span])
        pi = join(low, padded[1, 0, span], padded[1, 1, span])
        inner = slice(SIZE + HALF * v, SIZE + HALF * (v + 1))
        product[0, inner] = dr * pr + di * pi
        product[1, inner] = dr * pi - di * pr
        power = dr * dr + di * di
        a11 += jnp.sum(power * light, axis=0, keepdims=True)
        b1 += jnp.sum(power * (light + 1.0), axis=0, keepdims=True)

    parts = [listed_sum(near, half, half, [product.at[0], product.at[1]], 1) for half in range(2)]
    overlap = [jnp.concatenate([parts[0][c], parts[1][c]], axis=0) for c in range(2)]
    pack_sums(keep, give, sums, overlap, a11, b1)


def add_all(parts):
    total = parts[0]
    for k in range(1, parts.shape[0]):
        total = total + parts[k]
    return total


def pair_kernel(keep, taken, out):
    out[...] = keep[...] + taken[...]


def reduce_kernel(parts, out):
    total = add_all(parts)
    for k in range(out.shape[0]):
        out[k] = total


def strip_kernel(parts, probe, out):
    total = add_all(parts)
    line = lax.broadcasted_iota(jnp.int32, (TILES, SIZE), 0)
    half = TILES // 2
    upper = line < half
    first = lax.axis_index(SCATTER[-1]) == 0
    rows = pl.ds(pl.multiple_of(lax.axis_index(SCATTER[:-1]) * TILES, TILES), TILES)

    def turned(x):
        return pltpu.roll(x, half, 0)

    def both(x, of_upper):
        return jnp.where(upper == of_upper, x, turned(x))

    def modes(c):
        one, two = probe[c, 0, rows], probe[c, 1, rows]
        return jnp.where(upper, jnp.where(first, one, turned(one)), jnp.where(first, turned(two), two))

    pr, pi = modes(0), modes(1)
    cover = both(total[2], True)
    inverse = 1.0 / (cover + 1.0)
    dr, di = total[0] * inverse, total[1] * inverse
    cross = (pr * dr + pi * di) * both(total[3], True) - (pr * di - pi * dr) * both(total[3], False)
    power = dr * dr + di * di
    a22, b2, a12 = (
        jnp.sum(x, axis=0, keepdims=True) for x in (power * cover, power * (cover + 1.0), cross))
    a11, b1 = total[2, half : half + 1], total[2, half + 1 : half + 2]
    low = low_lanes(1)
    known = jnp.where(low, a11 + pltpu.roll(a11, HALF, 1), b1 + pltpu.roll(b1, HALF, 1))
    numbers = total[2]
    for k, term in enumerate((known, a22, b2, a12)):
        numbers = jnp.where(line == half + k, term, numbers)
    for k in range(out.shape[0]):
        out[k, 0] = total[0]
        out[k, 1] = total[1]
        out[k, 2] = numbers


def step_sizes(totals, probe, new_probe, gradient=None):
    numbers = jnp.zeros((TILES, SIZE), F32)
    for k in range(totals.shape[0]):
        numbers += totals[k, 0, 2] + totals[k, 1, 2]
    half = TILES // 2
    low = low_lanes(1)
    known, *rest = (numbers[half + k : half + k + 1] for k in range(4))
    a22, b2, a12 = (jnp.sum(x, axis=1, keepdims=True) for x in rest)
    share = 1.0 / (2 * totals.shape[0])
    a11 = jnp.sum(jnp.where(low, known, 0.0), axis=1, keepdims=True) * share
    b1 = jnp.sum(jnp.where(low, 0.0, known), axis=1, keepdims=True) * share
    a11 = 1.1 * a11
    a22 = 1.1 * a22
    det = a11 * a22 - a12 * a12
    step_obj = (b1 * a22 - a12 * b2) / det
    step_probe = (a11 * b2 - a12 * b1) / det
    cover, _ = unpack_planes(totals, 2)
    cover = cover + 1.0
    scale = step_probe / cover
    for c in range(2):
        for m, numer in enumerate(unpack_planes(totals, c)):
            new_probe[c, m] = probe[c, m] + scale * numer
            if gradient is not None:
                gradient[c, m] = numer * lax.rsqrt(cover)
    return step_obj


def next_kernel(offsets, totals, padded, direction, probe, measured, right3, left3,
                row_out0, middle, row_out1, sums, new_padded, new_probe, accum):
    step = step_sizes(totals, probe, new_probe)
    new_padded[...] = padded[...] + step * direction[...]
    sweep(1, offsets, new_padded, new_probe, measured, right3, left3, sums, accum)
    middle[...] = accum[:, :, HALF : HALF + SIZE]
    odd_row, _ = odds()
    for c in range(2):
        for h in range(2):
            top, bottom = accum[c, h, :HALF], accum[c, h, HALF + SIZE :]
            row_out0[c, h] = jnp.where(odd_row, bottom, top)
            row_out1[c, h] = jnp.where(odd_row, top, bottom)


def last_kernel(totals, padded, direction, probe, new_obj, new_probe, gradient):
    step = step_sizes(totals, probe, new_probe, gradient)
    low = lanes() < HALF
    rows = slice(HALF, HALF + SIZE)
    for c in range(2):
        old = join(low, padded[c, 0, rows], padded[c, 1, rows])
        new_obj[c] = old + step * direction[c]


def shape(*dims):
    return jax.ShapeDtypeStruct(dims, F32)


def call(kernel, ins, outs, scratch=(), in_hbm=()):
    vmem = pl.BlockSpec(memory_space=pltpu.VMEM)
    smem = pl.BlockSpec(memory_space=pltpu.SMEM)
    hbm = pl.BlockSpec(memory_space=pltpu.HBM)
    ins = [pltpu.with_memory_space_constraint(x, pltpu.HBM) if k in in_hbm else x for k, x in enumerate(ins)]
    specs = [hbm if k in in_hbm else smem if x.dtype == jnp.int32 else vmem for k, x in enumerate(ins)]
    return pl.pallas_call(
        kernel,
        in_specs=specs,
        out_specs=[smem if x.dtype == jnp.int32 else vmem for x in outs],
        out_shape=list(outs),
        scratch_shapes=list(scratch),
        compiler_params=pltpu.CompilerParams(vmem_limit_bytes=VMEM_LIMIT),
        name=getattr(kernel, "func", kernel).__name__,
    )(*ins)


def swap(blocks, along):
    counts = size_of(ROW), size_of(COL)
    taken = []
    for k, block in enumerate(blocks):
        route = []
        for here in itertools.product(*(range(n) for n in counts)):
            there = list(here)
            there[along] += 1 if here[along] % 2 != k else -1
            if 0 <= there[along] < counts[along]:
                route.append((here[0] * counts[1] + here[1], there[0] * counts[1] + there[1]))
        taken.append(lax.ppermute(block, ALL, route))
    return taken


def exchange(block, axes):
    return lax.all_to_all(block, axes, 0, 0, tiled=True)


def size_of(axes):
    return math.prod(lax.axis_size(a) for a in axes)


def reduce_all(keep, give, probe):
    group, rest = size_of(SCATTER), size_of(REST)
    pairs = [(0, 1), (1, 0)]
    taken = lax.ppermute(give, SCATTER[0], pairs)
    (part,) = call(pair_kernel, [keep, taken], [shape(*keep.shape)])
    part = exchange(part.reshape(group // 2, 4, TILES, SIZE), SCATTER[1:])
    (part,) = call(reduce_kernel, [part], [shape(rest, 4, TILES, SIZE)])
    part = exchange(part, REST)
    (part,) = call(strip_kernel, [part, probe], [shape(group, 3, TILES, SIZE)])
    return exchange(part, SCATTER).reshape(SIZE // TILES, 2, 3, TILES, SIZE)


def per_device(obj, probe, measured, offsets):
    right3, left3 = (jnp.asarray(t) for t in dft_tables())
    offsets = jnp.swapaxes(offsets[0, 0], 1, 2)
    whole = 2 * SIZE

    strip = shape(2, HALF + TILES, SIZE)
    rows_strip = shape(2, 2, HALF + TILES, SIZE)
    quads = shape(2, 2, SIZE, SIZE)
    tile, *col_out, offsets = call(
        send_kernel, [offsets, obj],
        [shape(2, SIZE, SIZE), strip, strip, jax.ShapeDtypeStruct(offsets.shape, jnp.int32)],
        [pltpu.SemaphoreType.DMA((2,))], in_hbm=(0, 1))
    col_in = swap(col_out, 1)
    staged = [measured, right3, left3]
    measured, right3, left3 = call(
        stage_kernel, [tile, *staged], [jax.ShapeDtypeStruct(x.shape, x.dtype) for x in staged],
        [pltpu.SemaphoreType.DMA((len(staged),))], in_hbm=(1, 2, 3))
    middle, *row_out, codes = call(
        spread_kernel, [*col_in, tile, col_out[1], right3], [quads, rows_strip, rows_strip, shape(TILES, SIZE)])
    row_in = swap(row_out, 0)
    others = jnp.concatenate([row_in[0][0, 0, HALF:], codes, row_in[1][0, 0, HALF:]], axis=0).astype(jnp.int32)

    field = shape(2, 2, whole, SIZE)
    edge = shape(2, 2, HALF, SIZE)
    planes = shape(2, MODES, SIZE, SIZE)
    sums_shape = shape(5, SIZE, SIZE)
    strips = [shape(SIZE // TILES // 2, 2, 4, TILES, SIZE)] * 2

    *row_out, sums, padded = call(
        first_kernel,
        [offsets, *row_in, middle, probe, measured, right3, left3],
        [quads, quads, sums_shape, field],
        [pltpu.VMEM((2, 2, whole, SIZE), F32)],
    )
    row_in = swap(row_out, 0)
    cover, near = call(
        cover_kernel, [others, probe],
        [shape(2, whole, SIZE), jax.ShapeDtypeStruct((2, 2, LIST_SIZE), jnp.int32)],
        [pltpu.VMEM((3 * SIZE, SIZE), F32)])
    col_out = call(wide_fold_kernel, [*row_out, *row_in], [quads, quads])
    col_in = swap(col_out, 1)
    keep, give, direction = call(
        wide_merge_kernel,
        [offsets, *col_out, *col_in, cover, padded, sums],
        [*strips, field],
        [pltpu.VMEM((2, 2, whole, SIZE), F32)],
    )
    totals = reduce_all(keep, give, probe)

    row_out0, middle, row_out1, sums, padded, probe = call(
        next_kernel,
        [offsets, totals, padded, direction, probe, measured, right3, left3],
        [edge, quads, edge, sums_shape, field, planes],
        [pltpu.VMEM((2, 2, whole, SIZE), F32)],
    )
    row_in = swap((row_out0, row_out1), 0)
    side = shape(2, HALF, SIZE)
    (cover,) = call(
        tile_cover_kernel, [near, probe], [shape(SIZE, SIZE)], [pltpu.VMEM((3 * SIZE, SIZE), F32)])
    middle, *col_out = call(
        fold_kernel, [middle, *row_in, cover], [shape(2, SIZE, SIZE), side, side])
    col_in = swap(col_out, 1)
    keep, give, direction = call(
        merge_kernel,
        [near, middle, *col_in, cover, padded, sums],
        [*strips, shape(2, SIZE, SIZE)],
        [pltpu.VMEM((2, 3 * SIZE, SIZE), F32)],
    )
    totals = reduce_all(keep, give, probe)
    return tuple(call(
        last_kernel, [totals, padded, direction, probe], [shape(2, SIZE, SIZE), planes, planes]
    ))


def solution(mesh):
    parts = Mesh(mesh.devices.reshape(2, 4, 2, 4, 4, 2), ALL)
    in_specs = (P(None, ROW, COL), P(), P(ROW, COL), P(ROW, COL))
    out_specs = (P(None, ROW, COL), P(), P())
    return jax.shard_map(
        per_device, mesh=parts, in_specs=in_specs, out_specs=out_specs, check_vma=False
    )
```
